256 devices in a mesh: dom: 16 (over z, x_hi), orb: 16 (over x_lo, y, core).
Axes of the slice: x: 4 (x_hi: 2, x_lo: 2; x = x_hi * 2 + x_lo), y: 4, z: 8, core: 2. Of those that a mesh axis runs over, the one named last changes fastest.
Arguments:
- rhs: float32 [128, 32, 32, 128], P('orb', 'dom'), may hold values from -6 to 6
- potential: float32 [32, 32, 128], P('dom'), may hold values from 0.5 to 2
- eigen_table: float32 [4096], replicated, may hold values from -1 to -0.1
- win_index: int32 [128], P('orb'), may hold values from 0 to 4095
- occupied: bfloat16 [32, 128, 32, 32, 128], P('orb', None, 'dom'), may hold values from -6 to 6
- block_ids: int32 [4], replicated, may hold values from 0 to 31, as said below
- psi_win: bfloat16 [128, 32, 32, 128], P('orb', 'dom'), may hold values from -6 to 6
- smoother: float32 [32, 32], replicated, may hold values from -1 to 1
Outputs:
- solution: float32 [128, 32, 32, 128], P('orb', 'dom')
- correlations: float32 [4, 128, 128], P(None, None, 'orb')
- gradient: float32 [32, 32, 128], P(None, 'dom', 'orb')
The draws below stay inside these ranges and needn't reach their ends.
Inputs may be any that keep to these rules, and one draw needn't show every extreme that they name: `block_ids`: distinct block numbers; block 0 and block 31 are always among them.
All inputs are finite; a program needn't handle non-finite values.
Results may differ from the reference program's by a relative error of at most 0.0047.
Values may be sent and summed in bfloat16 or wider, within the bound.
No kernel may reach another device: no remote copies, remote signals or barrier semaphores. Data moves between devices by JAX's collectives and lax.ppermute only.
A program may use at most 64 MiB of HBM per device.

```python
import math
import jax
import jax.numpy as jnp
from jax import lax

W = 128
BLK = 128
NPROJ = 4
ITERS = 3
NY = 32
NZ = 128
NX = 32
NBLK = 32
NOCC = 4096


def draw_block_ids(key, part):
    key = jax.random.fold_in(key, 5)
    key_mid = jax.random.fold_in(key, 11)
    key_order = jax.random.fold_in(key, 12)
    middle = jax.random.permutation(key_mid, NBLK - 2)[:NPROJ - 2].astype(jnp.int32) + 1
    ends = jnp.array([0, NBLK - 1], dtype=jnp.int32)
    chosen = jnp.concatenate([ends, middle])
    return jax.random.permutation(key_order, chosen).astype(jnp.int32)


def set_ends(result, rng, smallest, high):
    longest = result.shape.index(max(result.shape))
    spots = []
    for shift in (0, 1):
        where = [jax.random.randint(jax.random.fold_in(rng, axis), (), 0, length) for axis, length in enumerate(result.shape)]
        where[longest] = (where[longest] + shift) % result.shape[longest]
        spots.append(tuple(where))
    return result.at[spots[0]].set(smallest).at[spots[1]].set(high)


def levels(stream_key, shape, split, smallest, high):
    def one(dim, parts):
        draws = jax.random.uniform(jax.random.fold_in(jax.random.fold_in(stream_key, 6), dim), (parts,), jnp.float32, smallest / len(split), high / len(split))
        return jnp.repeat(jnp.exp(draws), shape[dim] // parts).reshape((-1,) + (1,) * (len(shape) - dim - 1))

    loudness = one(*split[0])
    for cut in split[1:]:
        loudness = loudness * one(*cut)
    return loudness


def gaussian(rng, dims, spread, reach, cuts=(), kind=jnp.bfloat16):
    loudness = levels(rng, dims, cuts, -0.22, 0.18) if cuts else 1.0
    entries = jax.random.normal(rng, dims, jnp.float32) * spread * loudness
    return jnp.minimum(jnp.maximum(entries, -reach), reach).astype(kind)


def setup_inputs(seed: int = 0) -> dict:
    seeds = jax.random.split(jax.random.key(seed), 9)
    rhs = gaussian(seeds[0], (W, NX, NY, NZ), 1.0, 6.0, ((0, 16), (1, 16)), jnp.float32)
    potential = jnp.clip(jnp.exp(math.log(2.0) - 1.3862944 * jax.random.uniform(seeds[1], (NX, NY, NZ), jnp.float32) ** levels(seeds[1], (NX, NY, NZ), ((0, 16),), -0.2, 0.2)), 0.5, 2.0)
    eigen_table = jnp.clip(jax.random.uniform(seeds[2], (NOCC,), jnp.float32, -1.0, -0.1), -1.0, -0.1)
    win_index = set_ends(jax.random.randint(seeds[3], (W,), 0, NOCC), jax.random.fold_in(seeds[3], 1), 0, NOCC - 1).astype(jnp.int32)
    occupied = gaussian(seeds[4], (NBLK, BLK, NX, NY, NZ), 1.0, 6.0, ((0, 16), (2, 16)))
    block_ids = draw_block_ids(jax.random.fold_in(seeds[8], 71), 0)
    psi_win = gaussian(seeds[6], (W, NX, NY, NZ), 1.0, 6.0, ((0, 16), (1, 16)))
    smoother = gaussian(seeds[7], (NX, NX), NX ** -0.5, 1.0, (), jnp.float32)
    return {"rhs": rhs, "potential": potential, "eigen_table": eigen_table, "win_index": win_index, "occupied": occupied, "block_ids": block_ids, "psi_win": psi_win, "smoother": smoother}


def apply_operator(field, diag):
    padded = jnp.pad(field, ((0, 0), (1, 1), (1, 1), (1, 1)))
    beside = padded[:, 2:, 1:-1, 1:-1] + padded[:, :-2, 1:-1, 1:-1]
    beside = beside + padded[:, 1:-1, 2:, 1:-1] + padded[:, 1:-1, :-2, 1:-1]
    beside = beside + padded[:, 1:-1, 1:-1, 2:] + padded[:, 1:-1, 1:-1, :-2]
    return diag * field - 0.5 * beside

def reference(rhs, potential, eigen_table, win_index, occupied, block_ids, psi_win, smoother):
    width = rhs.shape[0]
    eps = eigen_table[win_index]
    diag = 3.0 + potential[None] - eps[:, None, None, None]
    blocks = occupied[block_ids].reshape(NPROJ * BLK, -1)
    scale = 1.0 / math.sqrt(NX * NY * NZ)
    solution = jnp.zeros(rhs.shape, jnp.float32)
    coeff = jnp.zeros((NPROJ * BLK, width), jnp.float32)
    for step in range(ITERS):
        resid = rhs - apply_operator(solution, diag)
        resid_b = resid.astype(jnp.bfloat16).reshape(width, -1)
        coeff = jnp.dot(blocks, resid_b.T, preferred_element_type=jnp.float32) * scale
        coeff_b = coeff.astype(jnp.bfloat16)
        corr = jnp.dot(coeff_b.T, blocks, preferred_element_type=jnp.float32) * scale
        solution = solution + (resid - corr.reshape(resid.shape)) / diag
    correlations = coeff.reshape(NPROJ, BLK, width)
    raw = lax.optimization_barrier(jnp.sum(solution * psi_win.astype(jnp.float32), axis=0)) / math.sqrt(width)
    gradient = jnp.dot(smoother, raw.reshape(NX, -1), precision=lax.Precision.HIGHEST).reshape(raw.shape)
    return (solution, correlations, gradient)
```

```python
import functools
import math

import jax
import jax.numpy as jnp
from jax import lax
from jax.experimental import pallas as pl
from jax.experimental.pallas import tpu as pltpu
from jax.sharding import PartitionSpec as P

ITERS = 3
VMEM_LIMIT = 40 * 1024 * 1024
NT = (((1,), (1,)), ((), ()))


def project(resid_b, blocks, part_ref, scale):
    start = 0
    for ref in blocks:
        rows = ref.shape[0]
        part_ref[:, start : start + rows] = (
            lax.dot_general(resid_b, ref[...], NT, preferred_element_type=jnp.float32) * scale
        )
        start += rows


def first_kernel(scale, rhs_ref, *refs):
    *blocks, part_ref = refs
    project(rhs_ref[...].astype(jnp.bfloat16), blocks, part_ref, scale)


def resid_kernel(scale, row, x_ref, sib_ref, off_ref, rhs_ref, diag_ref, *refs):
    *blocks, resid_ref, part_ref, rb_ref = refs
    cells = x_ref.shape[1]
    lane = lax.broadcasted_iota(jnp.int32, (x_ref.shape[0], row), 1)
    for at in range(0, cells, row):
        here = slice(at, at + row)
        x = x_ref[:, here]
        beside = sib_ref[:, here].astype(jnp.float32) + off_ref[:, here].astype(jnp.float32)
        if at > 0:
            beside = beside + x_ref[:, at - row : at]
        if at + row < cells:
            beside = beside + x_ref[:, at + row : at + 2 * row]
        beside = beside + jnp.where(lane == 0, 0.0, pltpu.roll(x, 1, 1))
        beside = beside + jnp.where(lane == row - 1, 0.0, pltpu.roll(x, row - 1, 1))
        resid = rhs_ref[:, here] - (diag_ref[:, here] * x - 0.5 * beside)
        resid_ref[:, here] = resid
        rb_ref[:, here] = resid.astype(jnp.bfloat16)
    project(rb_ref[...], blocks, part_ref, scale)


def update_kernel(scale, tile, has_x, last, coeff_ref, resid_ref, diag_ref, *refs):
    refs = list(refs)
    x_ref = refs.pop(0) if has_x else None
    psi_ref = refs.pop(0) if last else None
    *blocks, out_ref, side_ref = refs
    cells = resid_ref.shape[1]
    for at in range(0, cells, tile):
        here = slice(at, at + tile)
        corr = 0.0
        start = 0
        for ref in blocks:
            rows = ref.shape[0]
            corr = corr + jnp.dot(
                coeff_ref[:, start : start + rows], ref[:, here], preferred_element_type=jnp.float32
            )
            start += rows
        x = (resid_ref[:, here] - corr * scale) / diag_ref[:, here]
        if has_x:
            x = x + x_ref[:, here]
        out_ref[:, here] = x
        if last:
            side_ref[:, here] = jnp.sum(x * psi_ref[:, here].astype(jnp.float32), axis=0, keepdims=True)
        else:
            side_ref[:, here] = x.astype(jnp.bfloat16)


def call(kernel, out_shape, scratch=()):
    return pl.pallas_call(
        kernel,
        out_shape=out_shape,
        scratch_shapes=scratch,
        compiler_params=pltpu.CompilerParams(vmem_limit_bytes=VMEM_LIMIT),
    )


def per_device(rhs, potential, eigen_table, win_index, occupied, block_ids, psi_win, smoother):
    local_orbs, planes, rows_y, rows_z = rhs.shape
    n_dom = lax.axis_size("dom")
    n_orb = lax.axis_size("orb")
    cells = rows_y * rows_z
    wide = 2 * local_orbs
    width = local_orbs * n_orb
    scale = 1.0 / math.sqrt(planes * n_dom * rows_y * rows_z)
    n_occ = eigen_table.shape[0]
    per_dev, blk_rows = occupied.shape[:2]
    nproj = block_ids.shape[0]
    chips = n_orb // 2
    ring = chips // 2
    share = blk_rows // chips
    o = lax.axis_index("orb")
    core = o % 2
    chip = o // 2
    low = core == 0
    groups = [[2 * k + c for k in range(chips)] for c in range(2)]

    def chip_perm(target):
        return [(2 * k + c, 2 * target(k) + c) for k in range(chips) for c in range(2)]

    swap_core = [(i, i ^ 1) for i in range(n_orb)]
    swap_x = chip_perm(lambda k: (k + ring) % chips)
    up_y = chip_perm(lambda k: k // ring * ring + (k + 1) % ring)
    down_y = chip_perm(lambda k: k // ring * ring + (k - 1) % ring)

    def permute(value, pairs):
        return lax.ppermute(value, "orb", pairs)

    def pair(own, other):
        return jnp.concatenate([jnp.where(low, own, other), jnp.where(low, other, own)], axis=0)

    def plane_of(slot, plane):
        got = lax.dynamic_slice(
            occupied, (slot, 0, plane, 0, 0), (1, blk_rows, 1, rows_y, rows_z)
        )
        return got.reshape(blk_rows, rows_y, rows_z)

    last_id = per_dev * n_orb - 1
    middle = jnp.logical_and(block_ids != 0, block_ids != last_id)
    rank = jnp.cumsum(middle.astype(jnp.int32)) - 1
    mids = [jnp.sum(jnp.where(jnp.logical_and(middle, rank == k), block_ids, 0)) for k in range(nproj - 2)]
    order = jnp.where(block_ids == 0, 0, jnp.where(block_ids == last_id, 1, 2 + rank))

    ends = jnp.logical_or(o == 0, o == n_orb - 1)
    over = permute(plane_of(core * (per_dev - 1), 1 - core), [(0, 1), (n_orb - 1, n_orb - 2)])
    fixed = jnp.where(ends, plane_of(core * (per_dev - 1), core), over)
    fixed = fixed.reshape(chips, share, rows_y, rows_z)
    at_zero = fixed[0]
    at_last = fixed[chips - 1]
    for s in range(1, chips):
        piece = lax.dynamic_index_in_dim(fixed, jnp.where(chip == 0, s, chips - 1 - s), 0, keepdims=False)
        pairs = [(c, 2 * s + c) for c in range(2)]
        pairs += [(n_orb - 2 + c, 2 * (chips - 1 - s) + c) for c in range(2)]
        got = permute(piece, pairs)
        at_zero = jnp.where(chip == s, got, at_zero)
        at_last = jnp.where(chip == chips - 1 - s, got, at_last)
    ends_share = jnp.concatenate([at_zero, at_last], axis=0).reshape(2 * share, cells)
    blocks_ends = lax.all_gather(ends_share, "orb", axis_index_groups=groups, tiled=True)

    offers = []
    for mid in mids:
        slot = mid % per_dev
        owner_core = (mid // per_dev) % 2
        other = permute(plane_of(slot, 1 - core), swap_core)
        offer = jnp.where(owner_core == core, plane_of(slot, core), other)
        offers.append(offer.reshape(chips, share, rows_y, rows_z))
    offered = lax.all_to_all(
        jnp.stack(offers, axis=1), "orb", 0, 0, axis_index_groups=groups, tiled=True
    )
    shares = []
    for k, mid in enumerate(mids):
        got = lax.dynamic_index_in_dim(offered[:, k], mid // (2 * per_dev), 0, keepdims=False)
        shares.append(got.reshape(share, cells))

    half = share // 2
    pieces = []
    places = []
    own = jnp.concatenate([shares[0], permute(shares[0], swap_x)], axis=0)
    above = permute(own, up_y)
    below = permute(own, down_y)
    far0 = permute(above[:share], up_y)
    far1 = permute(below[share:], down_y)
    pieces += [own, above, below, far0, far1]
    places += [(0, 0, 0), (0, 0, 1), (0, -1, 0), (0, -1, 1), (0, 1, 0), (0, 1, 1), (0, 2, 0), (0, 2, 1)]
    own = shares[1]
    above = permute(own, up_y)
    below = permute(own, down_y)
    far0 = permute(above[:half], up_y)
    far1 = permute(below[half:], down_y)
    line = jnp.concatenate([own, above, below], axis=0)
    far = jnp.concatenate([far0, far1], axis=0)
    pieces += [line, far, permute(line, swap_x), permute(far, swap_x)]
    places += [(1, dy, rx) for rx in range(2) for dy in (0, -1, 1, 2)]
    blocks_mid = jnp.concatenate(pieces, axis=0)
    blocks = [blocks_ends, blocks_mid]
    n_rows = nproj * blk_rows

    def both(field):
        mine = lax.dynamic_index_in_dim(field, core, 1, keepdims=False).reshape(local_orbs, cells)
        send = lax.dynamic_index_in_dim(field, 1 - core, 1, keepdims=False).reshape(local_orbs, cells)
        return pair(mine, permute(send, swap_core))

    picks = win_index[:, None] == jnp.arange(n_occ, dtype=jnp.int32)[None, :]
    eps = jnp.sum(jnp.where(picks, eigen_table[None, :], 0.0), axis=1)[:, None]
    eps = pair(eps, permute(eps, swap_core))
    plane_pot = lax.dynamic_index_in_dim(potential, core, 0, keepdims=True).reshape(1, cells)
    diag = 3.0 + plane_pot - eps
    rhs_wide = both(rhs)
    psi_wide = both(psi_win)

    part_shape = jax.ShapeDtypeStruct((wide, n_rows), jnp.float32)
    field_shape = jax.ShapeDtypeStruct((wide, cells), jnp.float32)
    halo_shape = jax.ShapeDtypeStruct((wide, cells), jnp.bfloat16)
    row_shape = jax.ShapeDtypeStruct((1, cells), jnp.float32)

    def total(part):
        first, second = part[:local_orbs], part[local_orbs:]
        mine = jnp.where(low, first, second) + permute(jnp.where(low, second, first), swap_core)
        spread = jnp.broadcast_to(mine.astype(jnp.bfloat16)[None], (n_dom,) + mine.shape)
        got = lax.all_to_all(spread, "dom", 0, 0, tiled=True)
        coeff = jnp.sum(got.astype(jnp.float32), axis=0)
        coeff_b = coeff.astype(jnp.bfloat16)
        return coeff, pair(coeff_b, permute(coeff_b, swap_core))

    across = []
    for d in range(n_dom - 1):
        for k in range(chips):
            left, right = d * n_orb + 2 * k + 1, (d + 1) * n_orb + 2 * k
            across += [(left, right), (right, left)]

    x = None
    for step in range(ITERS):
        if step == 0:
            resid = rhs_wide
            part = call(functools.partial(first_kernel, scale), part_shape)(rhs_wide, *blocks)
        else:
            sib = permute(x_b, swap_core)
            off = lax.ppermute(x_b, ("dom", "orb"), across)
            resid, part = call(
                functools.partial(resid_kernel, scale, rows_z),
                (field_shape, part_shape),
                (pltpu.VMEM((wide, cells), jnp.bfloat16),),
            )(x, sib, off, rhs_wide, diag, *blocks)
        coeff, coeff_b = total(part)
        final = step == ITERS - 1
        extra = ([x] if step else []) + ([psi_wide] if final else [])
        x, x_b = call(
            functools.partial(update_kernel, scale, 512, step > 0, final),
            (field_shape, row_shape if final else halo_shape),
        )(coeff_b, resid, diag, *extra, *blocks)

    raw = (x_b / math.sqrt(width)).reshape(n_dom, 1, rows_y // n_dom, rows_z)
    raw = jnp.broadcast_to(raw, (n_dom, n_orb) + raw.shape[2:])
    raw = raw.reshape(n_dom * n_orb, -1)
    terms = lax.all_to_all(raw, ("dom", "orb"), 0, 0, tiled=True)
    terms = jnp.sum(terms.reshape(n_dom, chips, 2, -1), axis=1).reshape(2 * n_dom, -1)
    smoothed = jnp.dot(smoother, terms, precision=lax.Precision.HIGHEST)
    smoothed = smoothed.reshape(2 * n_dom, rows_y // n_dom, rows_z)
    z_part = rows_z // n_orb
    gradient = lax.dynamic_slice_in_dim(smoothed, o * z_part, z_part, axis=2)

    first, second = x[:local_orbs], x[local_orbs:]
    mine = jnp.where(low, first, second)
    other = permute(jnp.where(low, second, first), swap_core)
    solution = jnp.stack([jnp.where(low, mine, other), jnp.where(low, other, mine)], axis=1)
    solution = solution.reshape(rhs.shape)

    table = coeff.T
    ends_rows = table[: 2 * blk_rows].reshape(chips, 2, share, local_orbs)
    mid_rows = table[2 * blk_rows :].reshape(len(places), share, local_orbs)
    y_of, x_of = chip % ring, chip // ring
    where_from = []
    for k in range(nproj - 2):
        for q in range(chips):
            index = jnp.int32(0)
            for i, (blk, dy, rx) in enumerate(places):
                if blk == k:
                    hit = jnp.logical_and((y_of + dy) % ring == q % ring, (x_of + rx) % 2 == q // ring)
                    index = jnp.where(hit, i, index)
            where_from.append(index)
    mid_rows = jnp.take(mid_rows, jnp.stack(where_from), axis=0)
    mid_rows = mid_rows.reshape(nproj - 2, blk_rows, local_orbs)
    ends_rows = ends_rows.transpose(1, 0, 2, 3).reshape(2, blk_rows, local_orbs)
    correlations = jnp.take(jnp.concatenate([ends_rows, mid_rows], axis=0), order, axis=0)
    return (solution, correlations, gradient)


def solution(mesh):
    return jax.shard_map(
        per_device,
        mesh=mesh,
        in_specs=(
            P("orb", "dom", None, None),
            P("dom", None, None),
            P(),
            P("orb"),
            P("orb", None, "dom", None, None),
            P(),
            P("orb", "dom", None, None),
            P(),
        ),
        out_specs=(P("orb", "dom", None, None), P(None, None, "orb"), P(None, "dom", "orb")),
        check_vma=False,
    )
```

```python
import functools
import math

import jax
import jax.numpy as jnp
from jax import lax
from jax.experimental import pallas as pl
from jax.experimental.pallas import tpu as pltpu
from jax.sharding import PartitionSpec as P

ITERS = 3
VMEM_LIMIT = 24 * 1024 * 1024
NT = (((1,), (1,)), ((), ()))
SMEM = pl.BlockSpec(memory_space=pltpu.SMEM)
ANY = pl.BlockSpec(memory_space=pl.ANY)
VMEM = pl.BlockSpec(memory_space=pltpu.VMEM)

MID, CHIP, SAME, SLOT, CORE, DEV, TABLE = 0, 2, 4, 5, 6, 7, 8


def shape(dims, dtype=jnp.float32):
    return jax.ShapeDtypeStruct(dims, dtype)


def plan_kernel(per_dev, n_orb, ids_ref, dev_ref, out_ref):
    nproj = ids_ref.shape[0]
    chips = n_orb // 2
    ring = chips // 2
    last = per_dev * n_orb - 1
    dev = dev_ref[0]
    chip = dev // 2
    seen = jnp.int32(0)
    mids = [jnp.int32(0)] * (nproj - 2)
    order = []
    for j in range(nproj):
        block = ids_ref[j]
        middle = jnp.logical_and(block != 0, block != last)
        for k in range(nproj - 2):
            mids[k] = jnp.where(jnp.logical_and(middle, seen == k), block, mids[k])
        order.append(jnp.where(block == 0, 0, jnp.where(block == last, 1, 2 + seen)))
        seen = seen + jnp.where(middle, 1, 0)
    owners = [mid // (2 * per_dev) for mid in mids]
    for k in range(nproj - 2):
        out_ref[MID + k] = mids[k]
        out_ref[CHIP + k] = owners[k]
    out_ref[SAME] = jnp.where(owners[0] == owners[1], 1, 0)
    offer = jnp.where(chip == owners[0], mids[0], mids[1])
    out_ref[SLOT] = offer % per_dev
    out_ref[CORE] = (offer // per_dev) % 2
    out_ref[DEV] = dev
    y, x = chip % ring, chip // ring
    for j in range(nproj):
        for q in range(chips):
            down = (q % ring + ring - y) % ring
            side = (q // ring + x) % 2
            out_ref[TABLE + j * chips + q] = order[j] * chips + down * 2 + side


def offer_kernel(plan_ref, occupied_ref, fixed_ref, offer_ref, sem):
    core = plan_ref[DEV] % 2
    last = occupied_ref.shape[0] - 1
    one = pltpu.make_async_copy(occupied_ref.at[core * last, :, 1 - core], fixed_ref, sem.at[0])
    two = pltpu.make_async_copy(occupied_ref.at[plan_ref[SLOT], :, 1 - core], offer_ref, sem.at[1])
    one.start()
    two.start()
    one.wait()
    two.wait()


def pick_kernel(chips, plan_ref, occupied_ref, fixed_ref, offer_ref, *refs):
    *piece_refs, out_ref, sem = refs
    dev = plan_ref[DEV]
    core = dev % 2
    chip = dev // 2
    last = occupied_ref.shape[0] - 1
    rows = piece_refs[0].shape[0]
    ends = jnp.logical_or(dev == 0, dev == 2 * chips - 1)

    def run(copies):
        for copy in copies:
            copy.start()
        for copy in copies:
            copy.wait()

    def pieces(source):
        copies = []
        for s, ref in enumerate(piece_refs):
            at = jnp.where(chip == 0, s, chips - 1 - s) * rows
            copies.append(pltpu.make_async_copy(source(pl.ds(at, rows)), ref, sem.at[s]))
        return copies

    mine = plan_ref[CORE] == core

    @pl.when(mine)
    def _():
        run([pltpu.make_async_copy(occupied_ref.at[plan_ref[SLOT], :, core], out_ref, sem.at[chips])])

    @pl.when(jnp.logical_not(mine))
    def _():
        run([pltpu.make_async_copy(offer_ref, out_ref, sem.at[chips])])

    @pl.when(ends)
    def _():
        run(pieces(lambda at: occupied_ref.at[core * last, at, core]))

    @pl.when(jnp.logical_not(ends))
    def _():
        run(pieces(lambda at: fixed_ref.at[at]))


def share_kernel(chips, plan_ref, *refs):
    *piece_refs, out_ref, sem = refs
    chip = plan_ref[DEV] // 2
    for s, ref in enumerate(piece_refs):

        @pl.when(chip == s)
        def _(ref=ref):
            copy = pltpu.make_async_copy(ref, out_ref.at[0], sem.at[0])
            copy.start()
            copy.wait()

        @pl.when(chip == chips - 1 - s)
        def _(ref=ref):
            copy = pltpu.make_async_copy(ref, out_ref.at[1], sem.at[1])
            copy.start()
            copy.wait()


def split(plan_ref, value, mine_ref, other_ref):
    half = value.shape[0] // 2
    low = plan_ref[DEV] % 2 == 0
    first, second = value[:half], value[half:]
    mine_ref[...] = jnp.where(low, first, second)
    other_ref[...] = jnp.where(low, second, first)


def project(scale, plan_ref, resid_b, blocks_ref, mine_ref, other_ref):
    part = lax.dot_general(resid_b, blocks_ref[...], NT, preferred_element_type=jnp.float32)
    split(plan_ref, part * scale, mine_ref, other_ref)


def first_kernel(scale, plan_ref, rhs_ref, blocks_ref, mine_ref, other_ref):
    project(scale, plan_ref, rhs_ref[...].astype(jnp.bfloat16), blocks_ref, mine_ref, other_ref)


def resid_kernel(
    scale, row, plan_ref, x_ref, sib_ref, off_ref, rhs_ref, diag_ref, blocks_ref,
    resid_ref, mine_ref, other_ref, rb_ref,
):
    cells = x_ref.shape[1]
    lane = lax.broadcasted_iota(jnp.int32, (x_ref.shape[0], row), 1)
    for at in range(0, cells, row):
        here = slice(at, at + row)
        x = x_ref[:, here]
        beside = sib_ref[:, here] + off_ref[:, here]
        if at > 0:
            beside = beside + x_ref[:, at - row : at]
        if at + row < cells:
            beside = beside + x_ref[:, at + row : at + 2 * row]
        beside = beside + jnp.where(lane == 0, 0.0, pltpu.roll(x, 1, 1))
        beside = beside + jnp.where(lane == row - 1, 0.0, pltpu.roll(x, row - 1, 1))
        resid = rhs_ref[:, here] - (diag_ref[:, here] * x - 0.5 * beside)
        resid_ref[:, here] = resid
        rb_ref[:, here] = resid.astype(jnp.bfloat16)
    project(scale, plan_ref, rb_ref[...], blocks_ref, mine_ref, other_ref)


def stacked(value):
    half = value.shape[1] // 2
    return jnp.concatenate([value[:, :half], value[:, half:]], axis=0)


def unstacked(value):
    half = value.shape[0] // 2
    return jnp.concatenate([value[:half], value[half:]], axis=1)


def spread_kernel(mine_ref, other_ref, out_ref):
    total = stacked(mine_ref[...] + other_ref[...]).astype(jnp.bfloat16)
    for d in range(out_ref.shape[0]):
        out_ref[d] = total


def total_kernel(parts_ref, coeff_ref, coeff_b_ref):
    total = parts_ref[0].astype(jnp.float32)
    for d in range(1, parts_ref.shape[0]):
        total = total + parts_ref[d].astype(jnp.float32)
    coeff_ref[...] = unstacked(total)
    coeff_b_ref[...] = total.astype(jnp.bfloat16)


def update_kernel(scale, tile, has_x, last, root, plan_ref, mine_ref, other_ref, resid_ref, diag_ref, *refs):
    refs = list(refs)
    x_ref = refs.pop(0) if has_x else None
    psi_ref = refs.pop(0) if last else None
    blocks_ref, *outs = refs
    low = plan_ref[DEV] % 2 == 0
    mine = unstacked(mine_ref[...].astype(jnp.float32))
    other = unstacked(other_ref[...].astype(jnp.float32))
    coeff = jnp.concatenate([jnp.where(low, mine, other), jnp.where(low, other, mine)], axis=0)
    coeff = coeff.astype(jnp.bfloat16)
    cells = resid_ref.shape[1]
    for at in range(0, cells, tile):
        here = slice(at, at + tile)
        corr = jnp.dot(coeff, blocks_ref[:, here], preferred_element_type=jnp.float32)
        x = (resid_ref[:, here] - corr * scale) / diag_ref[:, here]
        if has_x:
            x = x + x_ref[:, here]
        if last:
            half = x.shape[0] // 2
            outs[0][:, here] = jnp.where(low, x[:half], x[half:])
            outs[1][:, here] = jnp.where(low, x[half:], x[:half])
            raw = jnp.sum(x * psi_ref[:, here].astype(jnp.float32), axis=0, keepdims=True) / root
            wide = outs[2].shape[2]
            for k in range(tile // wide):
                row = raw[:, k * wide : (k + 1) * wide]
                outs[2][at // wide + k] = jnp.broadcast_to(row, outs[2].shape[1:])
        else:
            outs[0][:, here] = x


def table_kernel(plan_ref, coeff_ref, out_ref, rows_ref):
    rows_ref[...] = coeff_ref[...].T
    share = 16
    for j in range(out_ref.shape[0] // share):
        at = pl.multiple_of(plan_ref[TABLE + j] * share, share)
        out_ref[j * share : (j + 1) * share] = rows_ref[pl.ds(at, share)]


def call(kernel, out_shape, in_specs=None, out_specs=None, scratch=()):
    specs = {}
    if in_specs is not None:
        specs["in_specs"] = in_specs
    if out_specs is not None:
        specs["out_specs"] = out_specs
    return pl.pallas_call(
        kernel,
        out_shape=out_shape,
        scratch_shapes=scratch,
        compiler_params=pltpu.CompilerParams(vmem_limit_bytes=VMEM_LIMIT),
        **specs,
    )


def per_device(rhs, potential, eigen_table, win_index, occupied, block_ids, psi_win, smoother):
    local_orbs, planes, rows_y, rows_z = rhs.shape
    n_dom = lax.axis_size("dom")
    n_orb = lax.axis_size("orb")
    cells = rows_y * rows_z
    wide = 2 * local_orbs
    width = local_orbs * n_orb
    scale = 1.0 / math.sqrt(planes * n_dom * rows_y * rows_z)
    n_occ = eigen_table.shape[0]
    per_dev, blk_rows = occupied.shape[:2]
    nproj = block_ids.shape[0]
    chips = n_orb // 2
    ring = chips // 2
    share = blk_rows // chips
    n_rows = nproj * blk_rows
    o = lax.axis_index("orb")
    core = o % 2
    low = core == 0
    groups = [[2 * k + c for k in range(chips)] for c in range(2)]

    def chip_perm(target):
        return [(2 * k + c, 2 * target(k) + c) for k in range(chips) for c in range(2)]

    swap_core = [(i, i ^ 1) for i in range(n_orb)]
    swap_x = chip_perm(lambda k: (k + ring) % chips)
    up_y = chip_perm(lambda k: k // ring * ring + (k + 1) % ring)
    down_y = chip_perm(lambda k: k // ring * ring + (k - 1) % ring)

    def permute(value, pairs):
        return lax.ppermute(value, "orb", pairs)

    def pair(own, other):
        return jnp.concatenate([jnp.where(low, own, other), jnp.where(low, other, own)], axis=0)

    plan = call(
        functools.partial(plan_kernel, per_dev, n_orb),
        shape((TABLE + nproj * chips,), jnp.int32),
        [SMEM, SMEM],
        SMEM,
    )(block_ids, o.astype(jnp.int32).reshape(1))

    plane_shape = shape((blk_rows, rows_y, rows_z), jnp.bfloat16)
    piece_shape = shape((share, rows_y, rows_z), jnp.bfloat16)
    fixed, offer = call(
        offer_kernel, (plane_shape, plane_shape), [SMEM, ANY], (ANY, ANY),
        (pltpu.SemaphoreType.DMA((2,)),),
    )(plan, occupied)
    fixed = permute(fixed, [(0, 1), (n_orb - 1, n_orb - 2)])
    offer = permute(offer, swap_core)
    *pieces, offer = call(
        functools.partial(pick_kernel, chips),
        [piece_shape] * chips + [plane_shape],
        [SMEM, ANY, ANY, ANY],
        [ANY] * (chips + 1),
        (pltpu.SemaphoreType.DMA((chips + 1,)),),
    )(plan, occupied, fixed, offer)

    got = [pieces[0]]
    for s in range(1, chips):
        pairs = [(c, 2 * s + c) for c in range(2)]
        pairs += [(n_orb - 2 + c, 2 * (chips - 1 - s) + c) for c in range(2)]
        got.append(permute(pieces[s], pairs))
    fixed_shares = call(
        functools.partial(share_kernel, chips),
        shape((2, share, rows_y, rows_z), jnp.bfloat16),
        [SMEM] + [ANY] * chips,
        ANY,
        (pltpu.SemaphoreType.DMA((2,)),),
    )(plan, *got).reshape(2, share, cells)

    def scatter(value):
        value = value.reshape(chips, share, rows_y, rows_z)
        return lax.all_to_all(value, "orb", 0, 0, axis_index_groups=groups, tiled=True)

    def take(value, owner):
        return lax.dynamic_index_in_dim(value, owner, 0, keepdims=False).reshape(share, cells)

    def apart(plan, occupied, offer):
        offered = scatter(offer)
        return tuple(take(offered, plan[CHIP + k]) for k in range(nproj - 2))

    def together(plan, occupied, offer):
        def plane_of(slot, plane):
            dims = (1, blk_rows, 1, rows_y, rows_z)
            return lax.dynamic_slice(occupied, (slot, 0, plane, 0, 0), dims).reshape(offer.shape)

        out = [take(scatter(offer), plan[CHIP])]
        for k in range(1, nproj - 2):
            mid = plan[MID + k]
            other = permute(plane_of(mid % per_dev, 1 - core), swap_core)
            here = (mid // per_dev) % 2 == core
            again = jnp.where(here, plane_of(mid % per_dev, core), other)
            out.append(take(scatter(again), plan[CHIP + k]))
        return tuple(out)

    mid_shares = lax.cond(plan[SAME] == 1, together, apart, plan, occupied, offer)

    def gather(one, two):
        own = jnp.concatenate([one, permute(one, swap_x)], axis=0)
        above = permute(own, up_y)
        below = permute(own, down_y)
        near_y = permute(two, up_y)
        back_y = permute(two, down_y)
        far0 = permute(above[:share], up_y)
        far1 = permute(below[share:], down_y)
        half = share // 2
        line = jnp.concatenate([two, back_y, near_y], axis=0)
        line_x = permute(line, swap_x)
        far = jnp.concatenate([permute(near_y[:half], up_y), permute(back_y[half:], down_y)], axis=0)
        far_x = permute(far, swap_x)
        first = [own, below, far0, far1, above]
        second = [two, line_x[:share], back_y, line_x[share : 2 * share], far, far_x, near_y, line_x[2 * share :]]
        return first, second

    held = gather(fixed_shares[0], fixed_shares[1]) + gather(*mid_shares)
    blocks = jnp.concatenate([piece for part in held for piece in part], axis=0)

    def both(field):
        mine = lax.dynamic_index_in_dim(field, core, 1, keepdims=False).reshape(local_orbs, cells)
        send = lax.dynamic_index_in_dim(field, 1 - core, 1, keepdims=False).reshape(local_orbs, cells)
        return pair(mine, permute(send, swap_core))

    picks = win_index[:, None] == jnp.arange(n_occ, dtype=jnp.int32)[None, :]
    eps = jnp.sum(jnp.where(picks, eigen_table[None, :], 0.0), axis=1)[:, None]
    eps = pair(eps, permute(eps, swap_core))
    plane_pot = lax.dynamic_index_in_dim(potential, core, 0, keepdims=True).reshape(1, cells)
    diag = 3.0 + plane_pot - eps
    rhs_wide = both(rhs)
    psi_wide = both(psi_win)

    half_shape = shape((local_orbs, n_rows))
    field_shape = shape((wide, cells))
    flat_shape = (wide, n_rows // 2)

    def total(mine, other):
        other = permute(other, swap_core)
        spread = call(spread_kernel, shape((n_dom,) + flat_shape, jnp.bfloat16))(mine, other)
        parts = lax.all_to_all(spread, "dom", 0, 0, tiled=True)
        coeff, coeff_b = call(total_kernel, (half_shape, shape(flat_shape, jnp.bfloat16)))(parts)
        return coeff, coeff_b, permute(coeff_b, swap_core)

    across = []
    for d in range(n_dom - 1):
        for k in range(chips):
            left, right = d * n_orb + 2 * k + 1, (d + 1) * n_orb + 2 * k
            across += [(left, right), (right, left)]

    x = None
    for step in range(ITERS):
        if step == 0:
            resid = rhs_wide
            mine, other = call(
                functools.partial(first_kernel, scale),
                (half_shape, half_shape),
                [SMEM, VMEM, VMEM],
            )(plan, rhs_wide, blocks)
        else:
            sib = permute(x, swap_core)
            off = lax.ppermute(x, ("dom", "orb"), across)
            resid, mine, other = call(
                functools.partial(resid_kernel, scale, rows_z),
                (field_shape, half_shape, half_shape),
                [SMEM] + [VMEM] * 6,
                scratch=(pltpu.VMEM((wide, cells), jnp.bfloat16),),
            )(plan, x, sib, off, rhs_wide, diag, blocks)
        coeff, coeff_b, coeff_o = total(mine, other)
        final = step == ITERS - 1
        extra = ([x] if step else []) + ([psi_wide] if final else [])
        outs = [field_shape]
        if final:
            outs = [shape((local_orbs, cells))] * 2 + [shape((n_dom, n_orb, cells // n_dom))]
        x, *rest = call(
            functools.partial(update_kernel, scale, 512, step > 0, final, math.sqrt(width)),
            outs,
            [SMEM] + [VMEM] * (5 + len(extra)),
        )(plan, coeff_b, coeff_o, resid, diag, *extra, blocks)
    other, raw = rest

    weights = jnp.broadcast_to(
        smoother.reshape(2 * n_dom, n_dom, 1, 2), (2 * n_dom, n_dom, chips, 2)
    ).reshape(2 * n_dom, n_dom * n_orb)
    terms = lax.all_to_all(raw.reshape(n_dom * n_orb, -1), ("dom", "orb"), 0, 0, tiled=True)
    smoothed = jnp.dot(weights, terms, precision=lax.Precision.HIGHEST)
    smoothed = smoothed.reshape(2 * n_dom, rows_y // n_dom, rows_z)
    z_part = rows_z // n_orb
    gradient = lax.dynamic_slice_in_dim(smoothed, o * z_part, z_part, axis=2)

    other = permute(other, swap_core)
    solution = jnp.stack([jnp.where(low, x, other), jnp.where(low, other, x)], axis=1)
    solution = solution.reshape(rhs.shape)

    coeff, raw = lax.optimization_barrier((coeff, raw))
    correlations = call(
        table_kernel,
        shape((n_rows, local_orbs)),
        [SMEM, VMEM],
        scratch=(pltpu.VMEM((n_rows, local_orbs), jnp.float32),),
    )(plan, coeff).reshape(nproj, blk_rows, local_orbs)
    return (solution, correlations, gradient)


def solution(mesh):
    return jax.shard_map(
        per_device,
        mesh=mesh,
        in_specs=(
            P("orb", "dom", None, None),
            P("dom", None, None),
            P(),
            P("orb"),
            P("orb", None, "dom", None, None),
            P(),
            P("orb", "dom", None, None),
            P(),
        ),
        out_specs=(P("orb", "dom", None, None), P(None, None, "orb"), P(None, "dom", "orb")),
        check_vma=False,
    )
```

```python
import functools
import math

import jax
import jax.numpy as jnp
from jax import lax
from jax.experimental import pallas as pl
from jax.experimental.pallas import tpu as pltpu
from jax.sharding import PartitionSpec as P

ITERS = 3
VMEM_LIMIT = 16 * 1024 * 1024
NT = (((1,), (1,)), ((), ()))
SMEM = pl.BlockSpec(memory_space=pltpu.SMEM)
ANY = pl.BlockSpec(memory_space=pl.ANY)
VMEM = pl.BlockSpec(memory_space=pltpu.VMEM)

MID, CHIP, SAME, SLOT, CORE, DEV, TABLE = 0, 2, 4, 5, 6, 7, 8


def shape(dims, dtype=jnp.float32):
    return jax.ShapeDtypeStruct(dims, dtype)


def plan_kernel(per_dev, n_orb, ids_ref, dev_ref, out_ref):
    nproj = ids_ref.shape[0]
    chips = n_orb // 2
    ring = chips // 2
    last = per_dev * n_orb - 1
    dev = dev_ref[0]
    chip = dev // 2
    seen = jnp.int32(0)
    mids = [jnp.int32(0)] * (nproj - 2)
    order = []
    for j in range(nproj):
        block = ids_ref[j]
        middle = jnp.logical_and(block != 0, block != last)
        for k in range(nproj - 2):
            mids[k] = jnp.where(jnp.logical_and(middle, seen == k), block, mids[k])
        order.append(jnp.where(block == 0, 0, jnp.where(block == last, 1, 2 + seen)))
        seen = seen + jnp.where(middle, 1, 0)
    owners = [mid // (2 * per_dev) for mid in mids]
    for k in range(nproj - 2):
        out_ref[MID + k] = mids[k]
        out_ref[CHIP + k] = owners[k]
    out_ref[SAME] = jnp.where(owners[0] == owners[1], 1, 0)
    offer = jnp.where(chip == owners[0], mids[0], mids[1])
    out_ref[SLOT] = offer % per_dev
    out_ref[CORE] = (offer // per_dev) % 2
    out_ref[DEV] = dev
    y, x = chip % ring, chip // ring
    for j in range(nproj):
        for q in range(chips):
            down = (q % ring + ring - y) % ring
            side = (q // ring + x) % 2
            first = jnp.where(down == 1, 4, jnp.where(down == 3, 8, jnp.where(down == 2, 12, 0))) + side * 2
            second = jnp.where(down == 1, 4, jnp.where(down == 3, 2, 0)) + side * 6
            second = 16 + jnp.where(down == 2, 12 + side * 2, second)
            out_ref[TABLE + j * chips + q] = jnp.where(order[j] % 2 == 0, first, second) + order[j] // 2


def offer_kernel(plan_ref, occupied_ref, fixed_ref, offer_ref, sem):
    core = plan_ref[DEV] % 2
    last = occupied_ref.shape[0] - 1
    one = pltpu.make_async_copy(occupied_ref.at[core * last, :, 1 - core], fixed_ref, sem.at[0])
    two = pltpu.make_async_copy(occupied_ref.at[plan_ref[SLOT], :, 1 - core], offer_ref, sem.at[1])
    one.start()
    two.start()
    one.wait()
    two.wait()


def pick_kernel(chips, plan_ref, occupied_ref, fixed_ref, offer_ref, *refs):
    *piece_refs, out_ref, sem = refs
    dev = plan_ref[DEV]
    core = dev % 2
    chip = dev // 2
    last = occupied_ref.shape[0] - 1
    rows = piece_refs[0].shape[0]

    def at(s):
        return pl.ds(jnp.where(chip == 0, s, chips - 1 - s) * rows, rows)

    @pl.when(plan_ref[CORE] == core)
    def _():
        copy = pltpu.make_async_copy(occupied_ref.at[plan_ref[SLOT], :, core], out_ref, sem.at[chips])
        copy.start()
        copy.wait()

    @pl.when(plan_ref[CORE] != core)
    def _():
        @pl.loop(0, chips)
        def _(k):
            here = pl.ds(k * rows, rows)
            out_ref[here] = offer_ref[here]

    @pl.when(jnp.logical_or(dev == 0, dev == 2 * chips - 1))
    def _():
        copies = [
            pltpu.make_async_copy(occupied_ref.at[core * last, at(s), core], ref, sem.at[s])
            for s, ref in enumerate(piece_refs)
        ]
        for copy in copies:
            copy.start()
        for copy in copies:
            copy.wait()

    @pl.when(jnp.logical_or(dev == 1, dev == 2 * chips - 2))
    def _():
        for s, ref in enumerate(piece_refs):
            ref[...] = fixed_ref[at(s)]


def share_kernel(chips, plan_ref, *refs):
    *piece_refs, zero_ref, last_ref = refs
    chip = plan_ref[DEV] // 2
    for s, ref in enumerate(piece_refs):

        @pl.when(chip == s)
        def _(ref=ref):
            zero_ref[...] = ref[...]

        @pl.when(chip == chips - 1 - s)
        def _(ref=ref):
            last_ref[...] = ref[...]


def split(plan_ref, value, mine_ref, other_ref):
    half = value.shape[0] // 2
    low = plan_ref[DEV] % 2 == 0
    first, second = value[:half], value[half:]
    mine_ref[...] = jnp.where(low, first, second)
    other_ref[...] = jnp.where(low, second, first)


def project(scale, plan_ref, resid_b, block_refs, mine_ref, other_ref):
    parts = [
        lax.dot_general(resid_b, ref[...], NT, preferred_element_type=jnp.float32) for ref in block_refs
    ]
    split(plan_ref, jnp.concatenate(parts, axis=1) * scale, mine_ref, other_ref)


def first_kernel(scale, plan_ref, rhs_ref, first_ref, second_ref, mine_ref, other_ref):
    blocks = (first_ref, second_ref)
    project(scale, plan_ref, rhs_ref[...].astype(jnp.bfloat16), blocks, mine_ref, other_ref)


def resid_kernel(
    scale, row, plan_ref, x_ref, sib_ref, off_ref, rhs_ref, diag_ref, first_ref, second_ref,
    resid_ref, mine_ref, other_ref, rb_ref,
):
    cells = x_ref.shape[1]
    lane = lax.broadcasted_iota(jnp.int32, (x_ref.shape[0], row), 1)
    for at in range(0, cells, row):
        here = slice(at, at + row)
        x = x_ref[:, here]
        beside = sib_ref[:, here] + off_ref[:, here]
        if at > 0:
            beside = beside + x_ref[:, at - row : at]
        if at + row < cells:
            beside = beside + x_ref[:, at + row : at + 2 * row]
        beside = beside + jnp.where(lane == 0, 0.0, pltpu.roll(x, 1, 1))
        beside = beside + jnp.where(lane == row - 1, 0.0, pltpu.roll(x, row - 1, 1))
        resid = rhs_ref[:, here] - (diag_ref[:, here] * x - 0.5 * beside)
        resid_ref[:, here] = resid
        rb_ref[:, here] = resid.astype(jnp.bfloat16)
    project(scale, plan_ref, rb_ref[...], (first_ref, second_ref), mine_ref, other_ref)


def stacked(value):
    half = value.shape[1] // 2
    return jnp.concatenate([value[:, :half], value[:, half:]], axis=0)


def unstacked(value):
    half = value.shape[0] // 2
    return jnp.concatenate([value[:half], value[half:]], axis=1)


def spread_kernel(mine_ref, other_ref, out_ref):
    total = mine_ref[...] + other_ref[...]
    for d in range(out_ref.shape[0]):
        out_ref[d] = total


def total_kernel(parts_ref, coeff_ref, coeff_b_ref):
    total = parts_ref[0]
    for d in range(1, parts_ref.shape[0]):
        total = total + parts_ref[d]
    coeff_ref[...] = total
    coeff_b_ref[...] = stacked(total).astype(jnp.bfloat16)


def update_kernel(scale, tile, has_x, last, root, plan_ref, mine_ref, other_ref, resid_ref, diag_ref, *refs):
    refs = list(refs)
    x_ref = refs.pop(0) if has_x else None
    psi_ref = refs.pop(0) if last else None
    first_ref, second_ref, *outs = refs
    low = plan_ref[DEV] % 2 == 0
    mine = unstacked(mine_ref[...].astype(jnp.float32))
    other = unstacked(other_ref[...].astype(jnp.float32))
    coeff = jnp.concatenate([jnp.where(low, mine, other), jnp.where(low, other, mine)], axis=0)
    coeff = coeff.astype(jnp.bfloat16)
    cells = resid_ref.shape[1]
    for at in range(0, cells, tile):
        here = slice(at, at + tile)
        corr = 0.0
        start = 0
        for ref in (first_ref, second_ref):
            rows = ref.shape[0]
            some = coeff[:, start : start + rows]
            corr = corr + jnp.dot(some, ref[:, here], preferred_element_type=jnp.float32)
            start += rows
        x = (resid_ref[:, here] - corr * scale) / diag_ref[:, here]
        if has_x:
            x = x + x_ref[:, here]
        if last:
            half = x.shape[0] // 2
            outs[0][:, here] = jnp.where(low, x[:half], x[half:])
            outs[1][:, here] = jnp.where(low, x[half:], x[:half])
            raw = jnp.sum(x * psi_ref[:, here].astype(jnp.float32), axis=0, keepdims=True) / root
            rows, wide = outs[2].shape[2:]
            for k in range(tile // wide):
                row = raw[:, k * wide : (k + 1) * wide]
                spot = at // wide + k
                outs[2][spot // rows, :, spot % rows, :] = jnp.broadcast_to(row, (outs[2].shape[1], wide))
        else:
            outs[0][:, here] = x


def table_kernel(plan_ref, coeff_ref, out_ref, rows_ref):
    rows_ref[...] = coeff_ref[...].T
    share = 16
    for j in range(out_ref.shape[0] // share):
        at = pl.multiple_of(plan_ref[TABLE + j] * share, share)
        out_ref[j * share : (j + 1) * share] = rows_ref[pl.ds(at, share)]


def finish_kernel(z_part, plan_ref, weights_ref, terms_ref, out_ref):
    width = terms_ref.shape[2]
    shift = lax.rem(width - plan_ref[DEV] * z_part, width)
    for k in range(terms_ref.shape[1]):
        rows = lax.dot_general(
            weights_ref[...], terms_ref[:, k, :], (((1,), (0,)), ((), ())),
            precision=lax.Precision.HIGHEST, preferred_element_type=jnp.float32,
        )
        out_ref[:, k, :] = pltpu.roll(rows, shift, 1)[:, :z_part]


def call(kernel, out_shape, in_specs=None, out_specs=None, scratch=()):
    specs = {}
    if in_specs is not None:
        specs["in_specs"] = in_specs
    if out_specs is not None:
        specs["out_specs"] = out_specs
    return pl.pallas_call(
        kernel,
        out_shape=out_shape,
        scratch_shapes=scratch,
        compiler_params=pltpu.CompilerParams(vmem_limit_bytes=VMEM_LIMIT),
        **specs,
    )


def per_device(rhs, potential, eigen_table, win_index, occupied, block_ids, psi_win, smoother):
    local_orbs, planes, rows_y, rows_z = rhs.shape
    n_dom = lax.axis_size("dom")
    n_orb = lax.axis_size("orb")
    cells = rows_y * rows_z
    wide = 2 * local_orbs
    width = local_orbs * n_orb
    scale = 1.0 / math.sqrt(planes * n_dom * rows_y * rows_z)
    n_occ = eigen_table.shape[0]
    per_dev, blk_rows = occupied.shape[:2]
    nproj = block_ids.shape[0]
    chips = n_orb // 2
    ring = chips // 2
    share = blk_rows // chips
    n_rows = nproj * blk_rows
    o = lax.axis_index("orb")
    core = o % 2
    low = core == 0
    groups = [[2 * k + c for k in range(chips)] for c in range(2)]

    def chip_perm(target):
        return [(2 * k + c, 2 * target(k) + c) for k in range(chips) for c in range(2)]

    swap_core = [(i, i ^ 1) for i in range(n_orb)]
    swap_x = chip_perm(lambda k: (k + ring) % chips)
    up_y = chip_perm(lambda k: k // ring * ring + (k + 1) % ring)
    down_y = chip_perm(lambda k: k // ring * ring + (k - 1) % ring)

    def permute(value, pairs):
        return lax.ppermute(value, "orb", pairs)

    def pair(own, other):
        return jnp.concatenate([jnp.where(low, own, other), jnp.where(low, other, own)], axis=0)

    plan = call(
        functools.partial(plan_kernel, per_dev, n_orb),
        shape((TABLE + nproj * chips,), jnp.int32),
        [SMEM, SMEM],
        SMEM,
    )(block_ids, o.astype(jnp.int32).reshape(1))

    plane_shape = shape((blk_rows, rows_y, rows_z), jnp.bfloat16)
    piece_shape = shape((share, rows_y, rows_z), jnp.bfloat16)
    fixed, offer = call(
        offer_kernel, (plane_shape, plane_shape), [SMEM, ANY], (VMEM, VMEM),
        (pltpu.SemaphoreType.DMA((2,)),),
    )(plan, occupied)
    fixed = permute(fixed, [(0, 1), (n_orb - 1, n_orb - 2)])
    offer = permute(offer, swap_core)
    *pieces, offer = call(
        functools.partial(pick_kernel, chips),
        [piece_shape] * chips + [plane_shape],
        [SMEM, ANY, VMEM, VMEM],
        [VMEM] * (chips + 1),
        (pltpu.SemaphoreType.DMA((chips + 1,)),),
    )(plan, occupied, fixed, offer)

    got = [pieces[0]]
    for s in range(1, chips):
        pairs = [(c, 2 * s + c) for c in range(2)]
        pairs += [(n_orb - 2 + c, 2 * (chips - 1 - s) + c) for c in range(2)]
        got.append(permute(pieces[s], pairs))
    fixed_shares = call(
        functools.partial(share_kernel, chips),
        (piece_shape, piece_shape),
        [SMEM] + [VMEM] * chips,
    )(plan, *got)

    def scatter(value):
        value = value.reshape(chips, share, rows_y, rows_z)
        return lax.all_to_all(value, "orb", 0, 0, axis_index_groups=groups, tiled=True)

    def take(value, owner):
        return lax.dynamic_index_in_dim(value, owner, 0, keepdims=False)

    def apart(plan, occupied, offered):
        return take(offered, plan[CHIP + 1])

    def together(plan, occupied, offered):
        def plane_of(slot, plane):
            dims = (1, blk_rows, 1, rows_y, rows_z)
            return lax.dynamic_slice(occupied, (slot, 0, plane, 0, 0), dims).reshape(plane_shape.shape)

        mid = plan[MID + 1]
        other = permute(plane_of(mid % per_dev, 1 - core), swap_core)
        here = (mid // per_dev) % 2 == core
        again = scatter(jnp.where(here, plane_of(mid % per_dev, core), other))
        return take(again, plan[CHIP + 1])

    offered = scatter(offer)
    mid_shares = [
        take(offered, plan[CHIP]),
        lax.cond(plan[SAME] == 1, together, apart, plan, occupied, offered),
    ]

    def flat(one, two):
        return jnp.concatenate([one, two], axis=0).reshape(2 * share, cells)

    xs = flat(fixed_shares[0], mid_shares[0])
    ys = flat(fixed_shares[1], mid_shares[1])
    xs, ys = lax.optimization_barrier((xs, ys))
    xs_x = permute(xs, swap_x)
    ys_up = permute(ys, up_y)
    ys_down = permute(ys, down_y)
    xs_x, ys_up, ys_down = lax.optimization_barrier((xs_x, ys_up, ys_down))
    own = jnp.concatenate([xs, xs_x], axis=0)
    line = jnp.concatenate([ys, ys_up, ys_down], axis=0)
    line_x = permute(line, swap_x)
    above = permute(own, up_y)
    below = permute(own, down_y)
    far_up = permute(ys_up[:share], up_y)
    far_down = permute(ys_down[share:], down_y)
    line_x, above, below, far_up, far_down = lax.optimization_barrier(
        (line_x, above, below, far_up, far_down)
    )
    far = jnp.concatenate([far_up, far_down], axis=0)
    far_x = permute(far, swap_x)
    own_up = permute(above[: 2 * share], up_y)
    own_down = permute(below[2 * share :], down_y)
    blocks = [
        jnp.concatenate([own, below, above, own_up, own_down], axis=0),
        jnp.concatenate([line, line_x, far, far_x], axis=0),
    ]

    def both(field):
        mine = lax.dynamic_index_in_dim(field, core, 1, keepdims=False).reshape(local_orbs, cells)
        send = lax.dynamic_index_in_dim(field, 1 - core, 1, keepdims=False).reshape(local_orbs, cells)
        return pair(mine, permute(send, swap_core))

    picks = win_index[:, None] == jnp.arange(n_occ, dtype=jnp.int32)[None, :]
    eps = jnp.sum(jnp.where(picks, eigen_table[None, :], 0.0), axis=1)[:, None]
    eps = pair(eps, permute(eps, swap_core))
    plane_pot = lax.dynamic_index_in_dim(potential, core, 0, keepdims=True).reshape(1, cells)
    diag = 3.0 + plane_pot - eps
    rhs_wide = both(rhs)
    psi_wide = both(psi_win)

    half_shape = shape((local_orbs, n_rows))
    field_shape = shape((wide, cells))
    flat_shape = (wide, n_rows // 2)

    def total(mine, other):
        other = permute(other, swap_core)
        spread = call(spread_kernel, shape((n_dom,) + half_shape.shape))(mine, other)
        parts = lax.all_to_all(spread, "dom", 0, 0, tiled=True)
        coeff, coeff_b = call(total_kernel, (half_shape, shape(flat_shape, jnp.bfloat16)))(parts)
        return coeff, coeff_b, permute(coeff_b, swap_core)

    across = []
    for d in range(n_dom - 1):
        for k in range(chips):
            left, right = d * n_orb + 2 * k + 1, (d + 1) * n_orb + 2 * k
            across += [(left, right), (right, left)]

    x = None
    for step in range(ITERS):
        if step == 0:
            resid = rhs_wide
            mine, other = call(
                functools.partial(first_kernel, scale),
                (half_shape, half_shape),
                [SMEM] + [VMEM] * 3,
            )(plan, rhs_wide, *blocks)
        else:
            sib = permute(x, swap_core)
            off = lax.ppermute(x, ("dom", "orb"), across)
            resid, mine, other = call(
                functools.partial(resid_kernel, scale, rows_z),
                (field_shape, half_shape, half_shape),
                [SMEM] + [VMEM] * 7,
                scratch=(pltpu.VMEM((wide, cells), jnp.bfloat16),),
            )(plan, x, sib, off, rhs_wide, diag, *blocks)
        coeff, coeff_b, coeff_o = total(mine, other)
        final = step == ITERS - 1
        extra = ([x] if step else []) + ([psi_wide] if final else [])
        outs = [field_shape]
        if final:
            outs = [shape((local_orbs, cells))] * 2 + [shape((n_dom, n_orb, rows_y // n_dom, rows_z))]
        x, *rest = call(
            functools.partial(update_kernel, scale, 512, step > 0, final, math.sqrt(width)),
            outs,
            [SMEM] + [VMEM] * (6 + len(extra)),
        )(plan, coeff_b, coeff_o, resid, diag, *extra, *blocks)
    other, raw = rest

    weights = jnp.broadcast_to(
        smoother.reshape(2 * n_dom, n_dom, 1, 2), (2 * n_dom, n_dom, chips, 2)
    ).reshape(2 * n_dom, n_dom * n_orb)
    terms = lax.all_to_all(
        raw.reshape((n_dom * n_orb,) + raw.shape[2:]), ("dom", "orb"), 0, 0, tiled=True
    )
    z_part = rows_z // n_orb
    gradient = call(
        functools.partial(finish_kernel, z_part),
        shape((2 * n_dom, rows_y // n_dom, z_part)),
        [SMEM, VMEM, VMEM],
    )(plan, weights, terms)

    other = permute(other, swap_core)
    solution = jnp.stack([jnp.where(low, x, other), jnp.where(low, other, x)], axis=1)
    solution = solution.reshape(rhs.shape)

    coeff, raw = lax.optimization_barrier((coeff, raw))
    correlations = call(
        table_kernel,
        shape((n_rows, local_orbs)),
        [SMEM, VMEM],
        scratch=(pltpu.VMEM((n_rows, local_orbs), jnp.float32),),
    )(plan, coeff).reshape(nproj, blk_rows, local_orbs)
    return (solution, correlations, gradient)


def solution(mesh):
    return jax.shard_map(
        per_device,
        mesh=mesh,
        in_specs=(
            P("orb", "dom", None, None),
            P("dom", None, None),
            P(),
            P("orb"),
            P("orb", None, "dom", None, None),
            P(),
            P("orb", "dom", None, None),
            P(),
        ),
        out_specs=(P("orb", "dom", None, None), P(None, None, "orb"), P(None, "dom", "orb")),
        check_vma=False,
    )
```

```python
import functools
import math

import jax
import jax.numpy as jnp
from jax import lax
from jax.experimental import pallas as pl
from jax.experimental.pallas import tpu as pltpu
from jax.sharding import PartitionSpec as P

ITERS = 3
VMEM_LIMIT = 16 * 1024 * 1024
NT = (((1,), (1,)), ((), ()))
SMEM = pl.BlockSpec(memory_space=pltpu.SMEM)
ANY = pl.BlockSpec(memory_space=pl.ANY)
VMEM = pl.BlockSpec(memory_space=pltpu.VMEM)

MID, CHIP, SAME, SLOT, CORE, DEV, TABLE = 0, 2, 4, 5, 6, 7, 8


def shape(dims, dtype=jnp.float32):
    return jax.ShapeDtypeStruct(dims, dtype)


def plan_kernel(per_dev, n_orb, ids_ref, dev_ref, out_ref):
    nproj = ids_ref.shape[0]
    chips = n_orb // 2
    ring = chips // 2
    last = per_dev * n_orb - 1
    dev = dev_ref[0]
    chip = dev // 2
    seen = jnp.int32(0)
    mids = [jnp.int32(0)] * (nproj - 2)
    order = []
    for j in range(nproj):
        block = ids_ref[j]
        middle = jnp.logical_and(block != 0, block != last)
        for k in range(nproj - 2):
            mids[k] = jnp.where(jnp.logical_and(middle, seen == k), block, mids[k])
        order.append(jnp.where(block == 0, 0, jnp.where(block == last, 1, 2 + seen)))
        seen = seen + jnp.where(middle, 1, 0)
    owners = [mid // (2 * per_dev) for mid in mids]
    for k in range(nproj - 2):
        out_ref[MID + k] = mids[k]
        out_ref[CHIP + k] = owners[k]
    out_ref[SAME] = jnp.where(owners[0] == owners[1], 1, 0)
    offer = jnp.where(chip == owners[0], mids[0], mids[1])
    out_ref[SLOT] = offer % per_dev
    out_ref[CORE] = (offer // per_dev) % 2
    out_ref[DEV] = dev
    y, x = chip % ring, chip // ring
    for j in range(nproj):
        for q in range(chips):
            down = (q // 2 + ring - y) % ring
            first = jnp.where(down == 1, 4, jnp.where(down == 3, 8, jnp.where(down == 2, 12, 0)))
            first = first + (order[j] + x) % 2 * 2 + q % 2
            down = (q % ring + ring - y) % ring
            side = (q // ring + x) % 2
            second = jnp.where(down == 1, 4, jnp.where(down == 3, 2, 0)) + side * 6
            second = 14 + jnp.where(down == 2, 12 + side * 2, second) + order[j]
            out_ref[TABLE + j * chips + q] = jnp.where(order[j] < 2, first, second)


def copies(source, target, sem):
    parts = sem.shape[0]
    rows = target.shape[0] // parts
    return [
        pltpu.make_async_copy(source(k * rows, rows), target.at[pl.ds(k * rows, rows)], sem.at[k])
        for k in range(parts)
    ]


def run(started):
    for copy in started:
        copy.start()
    for copy in started:
        copy.wait()


def offer_kernel(plan_ref, occupied_ref, fixed_ref, offer_ref, fixed_sem, offer_sem):
    core = plan_ref[DEV] % 2
    last = occupied_ref.shape[0] - 1

    def plane(slot):
        return lambda at, rows: occupied_ref.at[slot, pl.ds(at, rows), 1 - core]

    run(
        copies(plane(plan_ref[SLOT]), offer_ref, offer_sem)
        + copies(plane(core * last), fixed_ref, fixed_sem)
    )


def pick_kernel(chips, plan_ref, occupied_ref, fixed_ref, offer_ref, *refs):
    *piece_refs, out_ref, sem, piece_sem = refs
    dev = plan_ref[DEV]
    core = dev % 2
    last = occupied_ref.shape[0] - 1
    ring = len(piece_refs)
    rows = piece_refs[0].shape[0]

    def at(s):
        return pl.ds(jnp.where(dev < chips, s, (ring - 1 + s) % ring) * rows, rows)

    @pl.when(plan_ref[CORE] == core)
    def _():
        run(copies(lambda k, n: occupied_ref.at[plan_ref[SLOT], pl.ds(k, n), core], out_ref, sem))

    @pl.when(plan_ref[CORE] != core)
    def _():
        step = out_ref.shape[0] // chips

        @pl.loop(0, chips)
        def _(k):
            here = pl.ds(k * step, step)
            out_ref[here] = offer_ref[here]

    @pl.when(jnp.logical_or(dev == 0, dev == 2 * chips - 1))
    def _():
        run([
            pltpu.make_async_copy(occupied_ref.at[core * last, at(s), core], ref, piece_sem.at[s])
            for s, ref in enumerate(piece_refs)
        ])

    @pl.when(jnp.logical_or(dev == 1, dev == 2 * chips - 2))
    def _():
        for s, ref in enumerate(piece_refs):
            ref[...] = fixed_ref[at(s)]


def share_kernel(plan_ref, *refs):
    *piece_refs, out_ref = refs
    ring = len(piece_refs)
    chip = plan_ref[DEV] // 2
    y, x = chip % ring, chip // ring
    away = (y + x) % ring
    for s, ref in enumerate(piece_refs):

        @pl.when(away == s)
        def _(ref=ref):
            out_ref[...] = ref[...]


def core_mask(low_ref, width):
    return jnp.concatenate([low_ref[...]] * (width // low_ref.shape[1]), axis=1) > 0.5


def split(low_ref, value, mine_ref, other_ref):
    half = value.shape[0] // 2
    low = core_mask(low_ref, value.shape[1])
    first, second = value[:half], value[half:]
    mine_ref[...] = jnp.where(low, first, second)
    other_ref[...] = jnp.where(low, second, first)


def project(scale, low_ref, resid_b, block_refs, mine_ref, other_ref):
    parts = [
        lax.dot_general(resid_b, ref[...], NT, preferred_element_type=jnp.float32) for ref in block_refs
    ]
    split(low_ref, jnp.concatenate(parts, axis=1) * scale, mine_ref, other_ref)


def first_kernel(scale, low_ref, rhs_ref, first_ref, second_ref, mine_ref, other_ref):
    blocks = (first_ref, second_ref)
    project(scale, low_ref, rhs_ref[...].astype(jnp.bfloat16), blocks, mine_ref, other_ref)


def resid_kernel(
    scale, row, low_ref, x_ref, sib_ref, off_ref, rhs_ref, diag_ref, first_ref, second_ref,
    resid_ref, mine_ref, other_ref, rb_ref,
):
    cells = x_ref.shape[1]
    lane = lax.broadcasted_iota(jnp.int32, (x_ref.shape[0], row), 1)
    for at in range(0, cells, row):
        here = slice(at, at + row)
        x = x_ref[:, here]
        beside = sib_ref[:, here] + off_ref[:, here].astype(jnp.float32)
        if at > 0:
            beside = beside + x_ref[:, at - row : at]
        if at + row < cells:
            beside = beside + x_ref[:, at + row : at + 2 * row]
        beside = beside + jnp.where(lane == 0, 0.0, pltpu.roll(x, 1, 1))
        beside = beside + jnp.where(lane == row - 1, 0.0, pltpu.roll(x, row - 1, 1))
        resid = rhs_ref[:, here] - (diag_ref[:, here] * x - 0.5 * beside)
        resid_ref[:, here] = resid
        rb_ref[:, here] = resid.astype(jnp.bfloat16)
    project(scale, low_ref, rb_ref[...], (first_ref, second_ref), mine_ref, other_ref)


def stacked(value):
    half = value.shape[1] // 2
    return jnp.concatenate([value[:, :half], value[:, half:]], axis=0)


def unstacked(value):
    half = value.shape[0] // 2
    return jnp.concatenate([value[:half], value[half:]], axis=1)


def spread_kernel(mine_ref, other_ref, out_ref):
    total = mine_ref[...] + other_ref[...]
    for d in range(out_ref.shape[0]):
        out_ref[d] = total


def total_kernel(parts_ref, *out_refs):
    total = parts_ref[0]
    for d in range(1, parts_ref.shape[0]):
        total = total + parts_ref[d]
    out_refs[0][...] = stacked(total).astype(jnp.bfloat16)
    if len(out_refs) > 1:
        out_refs[1][...] = total


def update_kernel(scale, tile, has_x, last, root, low_ref, mine_ref, other_ref, resid_ref, diag_ref, *refs):
    refs = list(refs)
    x_ref = refs.pop(0) if has_x else None
    psi_ref = refs.pop(0) if last else None
    first_ref, second_ref, *outs = refs
    low = core_mask(low_ref, 2 * mine_ref.shape[1])
    mine = unstacked(mine_ref[...].astype(jnp.float32))
    other = unstacked(other_ref[...].astype(jnp.float32))
    coeff = jnp.concatenate([jnp.where(low, mine, other), jnp.where(low, other, mine)], axis=0)
    coeff = coeff.astype(jnp.bfloat16)
    cells = resid_ref.shape[1]
    for at in range(0, cells, tile):
        here = slice(at, at + tile)
        corr = 0.0
        start = 0
        for ref in (first_ref, second_ref):
            rows = ref.shape[0]
            some = coeff[:, start : start + rows]
            corr = corr + jnp.dot(some, ref[:, here], preferred_element_type=jnp.float32)
            start += rows
        x = (resid_ref[:, here] - corr * scale) / diag_ref[:, here]
        if has_x:
            x = x + x_ref[:, here]
        if last:
            half = x.shape[0] // 2
            low = core_mask(low_ref, tile)
            outs[0][:, here] = jnp.where(low, x[:half], x[half:])
            outs[1][:, here] = jnp.where(low, x[half:], x[:half])
            raw = jnp.sum(x * psi_ref[:, here].astype(jnp.float32), axis=0, keepdims=True) / root
            rows, wide = outs[2].shape[2:]
            for k in range(tile // wide):
                row = raw[:, k * wide : (k + 1) * wide]
                spot = at // wide + k
                outs[2][spot // rows, :, spot % rows, :] = jnp.broadcast_to(row, (outs[2].shape[1], wide))
        else:
            outs[0][:, here] = x
            outs[1][:, here] = x.astype(jnp.bfloat16)


def table_kernel(plan_ref, coeff_ref, out_ref, rows_ref):
    rows_ref[...] = coeff_ref[...].T
    share = 16
    for j in range(out_ref.shape[0] // share):
        at = pl.multiple_of(plan_ref[TABLE + j] * share, share)
        out_ref[j * share : (j + 1) * share] = rows_ref[pl.ds(at, share)]


def finish_kernel(weights_ref, pick_ref, terms_ref, out_ref):
    def product(one, two):
        return lax.dot_general(
            one, two, (((1,), (0,)), ((), ())),
            precision=lax.Precision.HIGHEST, preferred_element_type=jnp.float32,
        )

    for k in range(terms_ref.shape[1]):
        out_ref[:, k, :] = product(product(weights_ref[...], terms_ref[:, k, :]), pick_ref[...])


def call(kernel, out_shape, in_specs=None, out_specs=None, scratch=()):
    specs = {}
    if in_specs is not None:
        specs["in_specs"] = in_specs
    if out_specs is not None:
        specs["out_specs"] = out_specs
    return pl.pallas_call(
        kernel,
        out_shape=out_shape,
        scratch_shapes=scratch,
        compiler_params=pltpu.CompilerParams(vmem_limit_bytes=VMEM_LIMIT),
        **specs,
    )


def per_device(rhs, potential, eigen_table, win_index, occupied, block_ids, psi_win, smoother):
    local_orbs, planes, rows_y, rows_z = rhs.shape
    n_dom = lax.axis_size("dom")
    n_orb = lax.axis_size("orb")
    cells = rows_y * rows_z
    wide = 2 * local_orbs
    width = local_orbs * n_orb
    scale = 1.0 / math.sqrt(planes * n_dom * rows_y * rows_z)
    n_occ = eigen_table.shape[0]
    per_dev, blk_rows = occupied.shape[:2]
    nproj = block_ids.shape[0]
    chips = n_orb // 2
    ring = chips // 2
    share = blk_rows // chips
    n_rows = nproj * blk_rows
    o = lax.axis_index("orb")
    core = o % 2
    low = core == 0
    groups = [[2 * k + c for k in range(chips)] for c in range(2)]

    def chip_perm(target):
        return [(2 * k + c, 2 * target(k) + c) for k in range(chips) for c in range(2)]

    swap_core = [(i, i ^ 1) for i in range(n_orb)]
    swap_x = chip_perm(lambda k: (k + ring) % chips)
    up_y = chip_perm(lambda k: k // ring * ring + (k + 1) % ring)
    down_y = chip_perm(lambda k: k // ring * ring + (k - 1) % ring)

    def permute(value, pairs):
        return lax.ppermute(value, "orb", pairs)

    def pair(own, other):
        return jnp.concatenate([jnp.where(low, own, other), jnp.where(low, other, own)], axis=0)

    plan = call(
        functools.partial(plan_kernel, per_dev, n_orb),
        shape((TABLE + nproj * chips,), jnp.int32),
        [SMEM, SMEM],
        SMEM,
    )(block_ids, o.astype(jnp.int32).reshape(1))

    plane_shape = shape((blk_rows, rows_y, rows_z), jnp.bfloat16)
    piece_shape = shape((2 * share, rows_y, rows_z), jnp.bfloat16)
    fixed, offer = call(
        offer_kernel, (plane_shape, plane_shape), [SMEM, ANY], (VMEM, VMEM),
        (pltpu.SemaphoreType.DMA((4,)), pltpu.SemaphoreType.DMA((4,))),
    )(plan, occupied)
    fixed = permute(fixed, [(0, 1), (n_orb - 1, n_orb - 2)])
    offer = permute(offer, swap_core)
    *pieces, offer = call(
        functools.partial(pick_kernel, chips),
        [piece_shape] * ring + [plane_shape],
        [SMEM, ANY, VMEM, VMEM],
        [VMEM] * (ring + 1),
        (pltpu.SemaphoreType.DMA((4,)), pltpu.SemaphoreType.DMA((ring,))),
    )(plan, occupied, fixed, offer)

    got = [pieces[0]]
    for s in range(1, ring):
        pairs = [(c, 2 * s + c) for c in range(2)]
        pairs += [(n_orb - 2 + c, 2 * (ring + (ring - 1 + s) % ring) + c) for c in range(2)]
        got.append(permute(pieces[s], pairs))
    fixed = call(share_kernel, piece_shape, [SMEM] + [VMEM] * ring, VMEM)(plan, *got)

    def scatter(value):
        value = value.reshape(chips, share, rows_y, rows_z)
        return lax.all_to_all(value, "orb", 0, 0, axis_index_groups=groups, tiled=True)

    def take(value, owner):
        return lax.dynamic_index_in_dim(value, owner, 0, keepdims=False)

    def apart(plan, occupied):
        return jnp.zeros((share, rows_y, rows_z), jnp.bfloat16)

    def together(plan, occupied):
        def plane_of(slot, plane):
            dims = (1, blk_rows, 1, rows_y, rows_z)
            return lax.dynamic_slice(occupied, (slot, 0, plane, 0, 0), dims).reshape(plane_shape.shape)

        mid = plan[MID + 1]
        other = permute(plane_of(mid % per_dev, 1 - core), swap_core)
        here = (mid // per_dev) % 2 == core
        again = scatter(jnp.where(here, plane_of(mid % per_dev, core), other))
        return take(again, plan[CHIP + 1])

    same = plan[SAME] == 1
    offered = scatter(offer)
    second = lax.cond(same, together, apart, plan, occupied)
    second = jnp.where(same, second, take(offered, plan[CHIP + 1]))
    mids = jnp.concatenate([take(offered, plan[CHIP]), second], axis=0)

    xs = fixed.reshape(2 * share, cells)
    ys = mids.reshape(2 * share, cells)
    xs, ys = lax.optimization_barrier((xs, ys))
    xs_x = permute(xs, swap_x)
    ys_up = permute(ys, up_y)
    ys_down = permute(ys, down_y)
    xs_x, ys_up, ys_down = lax.optimization_barrier((xs_x, ys_up, ys_down))
    own = jnp.concatenate([xs, xs_x], axis=0)
    line = jnp.concatenate([ys, ys_up, ys_down], axis=0)
    line_x = permute(line, swap_x)
    above = permute(own, up_y)
    below = permute(own, down_y)
    far_up = permute(ys_up[:share], up_y)
    far_down = permute(ys_down[share:], down_y)
    line_x, above, below, far_up, far_down = lax.optimization_barrier(
        (line_x, above, below, far_up, far_down)
    )
    far = jnp.concatenate([far_up, far_down], axis=0)
    far_x = permute(far, swap_x)
    own_up = permute(above[: 2 * share], up_y)
    own_down = permute(below[2 * share :], down_y)
    blocks = [
        jnp.concatenate([own, below, above, own_up, own_down], axis=0),
        jnp.concatenate([line, line_x, far, far_x], axis=0),
    ]

    def both(field):
        mine = lax.dynamic_index_in_dim(field, core, 1, keepdims=False).reshape(local_orbs, cells)
        send = lax.dynamic_index_in_dim(field, 1 - core, 1, keepdims=False).reshape(local_orbs, cells)
        return pair(mine, permute(send, swap_core))

    picks = win_index[:, None] == jnp.arange(n_occ, dtype=jnp.int32)[None, :]
    eps = jnp.sum(jnp.where(picks, eigen_table[None, :], 0.0), axis=1)[:, None]
    eps = pair(eps, permute(eps, swap_core))
    plane_pot = lax.dynamic_index_in_dim(potential, core, 0, keepdims=True).reshape(1, cells)
    diag = 3.0 + plane_pot - eps
    rhs_wide = both(rhs)
    psi_wide = both(psi_win)

    low_mask = jnp.broadcast_to(jnp.where(low, 1.0, 0.0), (local_orbs, 128))
    half_shape = shape((local_orbs, n_rows))
    field_shape = shape((wide, cells))
    flat_shape = (wide, n_rows // 2)

    def total(mine, other, outs):
        other = permute(other, swap_core)
        spread = call(spread_kernel, shape((n_dom,) + half_shape.shape))(mine, other)
        parts = lax.all_to_all(spread, "dom", 0, 0, tiled=True)
        coeff_b, *coeff = call(total_kernel, outs)(parts)
        return coeff, coeff_b, permute(coeff_b, swap_core)

    across = []
    for d in range(n_dom - 1):
        for k in range(chips):
            left, right = d * n_orb + 2 * k + 1, (d + 1) * n_orb + 2 * k
            across += [(left, right), (right, left)]

    x = None
    for step in range(ITERS):
        if step == 0:
            resid = rhs_wide
            mine, other = call(
                functools.partial(first_kernel, scale),
                (half_shape, half_shape),
            )(low_mask, rhs_wide, *blocks)
        else:
            sib = permute(x, swap_core)
            off = lax.ppermute(x_b, ("dom", "orb"), across)
            resid, mine, other = call(
                functools.partial(resid_kernel, scale, rows_z),
                (field_shape, half_shape, half_shape),
                scratch=(pltpu.VMEM((wide, cells), jnp.bfloat16),),
            )(low_mask, x, sib, off, rhs_wide, diag, *blocks)
        final = step == ITERS - 1
        sums = [shape(flat_shape, jnp.bfloat16)] + ([half_shape] if final else [])
        coeff, coeff_b, coeff_o = total(mine, other, sums)
        extra = ([x] if step else []) + ([psi_wide] if final else [])
        outs = [field_shape, shape((wide, cells), jnp.bfloat16)]
        if final:
            outs = [shape((local_orbs, cells))] * 2 + [shape((n_dom, n_orb, rows_y // n_dom, rows_z))]
        x, x_b, *rest = call(
            functools.partial(update_kernel, scale, 512, step > 0, final, math.sqrt(width)),
            outs,
        )(low_mask, coeff_b, coeff_o, resid, diag, *extra, *blocks)
    other, raw = x_b, rest[0]

    weights = jnp.broadcast_to(
        smoother.reshape(2 * n_dom, n_dom, 1, 2), (2 * n_dom, n_dom, chips, 2)
    ).reshape(2 * n_dom, n_dom * n_orb)
    terms = lax.all_to_all(
        raw.reshape((n_dom * n_orb,) + raw.shape[2:]), ("dom", "orb"), 0, 0, tiled=True
    )
    z_part = rows_z // n_orb
    z_mine = o * z_part + jnp.arange(z_part)[None, :]
    pick = (jnp.arange(rows_z)[:, None] == z_mine).astype(jnp.float32)
    gradient = call(finish_kernel, shape((2 * n_dom, rows_y // n_dom, z_part)))(weights, pick, terms)

    other = permute(other, swap_core)
    solution = jnp.stack([jnp.where(low, x, other), jnp.where(low, other, x)], axis=1)
    solution = solution.reshape(rhs.shape)

    coeff, raw = lax.optimization_barrier((coeff[0], raw))
    correlations = call(
        table_kernel,
        shape((n_rows, local_orbs)),
        [SMEM, VMEM],
        scratch=(pltpu.VMEM((n_rows, local_orbs), jnp.float32),),
    )(plan, coeff).reshape(nproj, blk_rows, local_orbs)
    return (solution, correlations, gradient)


def solution(mesh):
    return jax.shard_map(
        per_device,
        mesh=mesh,
        in_specs=(
            P("orb", "dom", None, None),
            P("dom", None, None),
            P(),
            P("orb"),
            P("orb", None, "dom", None, None),
            P(),
            P("orb", "dom", None, None),
            P(),
        ),
        out_specs=(P("orb", "dom", None, None), P(None, None, "orb"), P(None, "dom", "orb")),
        check_vma=False,
    )
```

```python
import functools
import math

import jax
import jax.numpy as jnp
from jax import lax
from jax.experimental import pallas as pl
from jax.experimental.pallas import tpu as pltpu
from jax.sharding import PartitionSpec as P

ITERS = 3
VMEM_LIMIT = 16 * 1024 * 1024
NT = (((1,), (1,)), ((), ()))
SMEM = pl.BlockSpec(memory_space=pltpu.SMEM)
ANY = pl.BlockSpec(memory_space=pl.ANY)
VMEM = pl.BlockSpec(memory_space=pltpu.VMEM)

MID, CHIP, SAME, SLOT, CORE, DEV, TABLE = 0, 2, 4, 5, 6, 7, 8


def shape(dims, dtype=jnp.float32):
    return jax.ShapeDtypeStruct(dims, dtype)


def plan(per_dev, n_orb, ids_ref, dev_ref, out_ref):
    nproj = ids_ref.shape[0]
    chips = n_orb // 2
    ring = chips // 2
    last = per_dev * n_orb - 1
    dev = dev_ref[0]
    chip = dev // 2
    seen = jnp.int32(0)
    mids = [jnp.int32(0)] * (nproj - 2)
    order = []
    for j in range(nproj):
        block = ids_ref[j]
        middle = jnp.logical_and(block != 0, block != last)
        for k in range(nproj - 2):
            mids[k] = jnp.where(jnp.logical_and(middle, seen == k), block, mids[k])
        order.append(jnp.where(block == 0, 0, jnp.where(block == last, 1, 2 + seen)))
        seen = seen + jnp.where(middle, 1, 0)
    owners = [mid // (2 * per_dev) for mid in mids]
    for k in range(nproj - 2):
        out_ref[MID + k] = mids[k]
        out_ref[CHIP + k] = owners[k]
    out_ref[SAME] = jnp.where(owners[0] == owners[1], 1, 0)
    offer = jnp.where(chip == owners[0], mids[0], mids[1])
    out_ref[SLOT] = offer % per_dev
    out_ref[CORE] = (offer // per_dev) % 2
    out_ref[DEV] = dev
    y, x = chip % ring, chip // ring
    for j in range(nproj):
        for q in range(chips):
            down = (q // 2 + ring - y) % ring
            first = jnp.where(down == 1, 4, jnp.where(down == 3, 8, jnp.where(down == 2, 12, 0)))
            first = first + (order[j] + x) % 2 * 2 + q % 2
            down = (q % ring + ring - y) % ring
            side = (q // ring + x) % 2
            second = jnp.where(down == 1, 4, jnp.where(down == 3, 2, 0)) + side * 6
            second = 14 + jnp.where(down == 2, 12 + side * 2, second) + order[j]
            out_ref[TABLE + j * chips + q] = jnp.where(order[j] < 2, first, second)


def copies(source, target, sem):
    parts = sem.shape[0]
    rows = target.shape[0] // parts
    return [
        pltpu.make_async_copy(source(k * rows, rows), target.at[pl.ds(k * rows, rows)], sem.at[k])
        for k in range(parts)
    ]


def run(started):
    for copy in started:
        copy.start()
    for copy in started:
        copy.wait()


def offer_kernel(per_dev, n_orb, ids_ref, dev_ref, occupied_ref, plan_ref, offer_ref, sem):
    plan(per_dev, n_orb, ids_ref, dev_ref, plan_ref)
    core = plan_ref[DEV] % 2
    run(copies(lambda at, n: occupied_ref.at[plan_ref[SLOT], pl.ds(at, n), 1 - core], offer_ref, sem))


def fixed_kernel(plan_ref, occupied_ref, fixed_ref, sem):
    core = plan_ref[DEV] % 2
    slot = core * (occupied_ref.shape[0] - 1)
    run(copies(lambda at, n: occupied_ref.at[slot, pl.ds(at, n), 1 - core], fixed_ref, sem))


def pick_kernel(plan_ref, occupied_ref, offer_ref, out_ref, sem):
    core = plan_ref[DEV] % 2

    @pl.when(plan_ref[CORE] == core)
    def _():
        run(copies(lambda at, n: occupied_ref.at[plan_ref[SLOT], pl.ds(at, n), core], out_ref, sem))

    @pl.when(plan_ref[CORE] != core)
    def _():
        step = 16

        @pl.loop(0, out_ref.shape[0] // step)
        def _(k):
            here = pl.ds(k * step, step)
            out_ref[here] = offer_ref[here]


def pieces_kernel(n_orb, plan_ref, occupied_ref, fixed_ref, *refs):
    *piece_refs, sem = refs
    dev = plan_ref[DEV]
    core = dev % 2
    last = occupied_ref.shape[0] - 1
    ring = len(piece_refs)
    rows = piece_refs[0].shape[0]

    def at(s):
        return pl.ds(jnp.where(dev < n_orb // 2, s, (ring - 1 + s) % ring) * rows, rows)

    @pl.when(jnp.logical_or(dev == 0, dev == n_orb - 1))
    def _():
        run([
            pltpu.make_async_copy(occupied_ref.at[core * last, at(s), core], ref, sem.at[s])
            for s, ref in enumerate(piece_refs)
        ])

    @pl.when(jnp.logical_or(dev == 1, dev == n_orb - 2))
    def _():
        for s, ref in enumerate(piece_refs):
            ref[...] = fixed_ref[at(s)]


def share_kernel(plan_ref, *refs):
    *piece_refs, out_ref = refs
    ring = len(piece_refs)
    chip = plan_ref[DEV] // 2
    y, x = chip % ring, chip // ring
    away = (y + x) % ring
    for s, ref in enumerate(piece_refs):

        @pl.when(away == s)
        def _(ref=ref):
            out_ref[...] = ref[...]


def core_mask(low_ref, width):
    return jnp.concatenate([low_ref[...]] * (width // low_ref.shape[1]), axis=1) > 0.5


def split(low_ref, value, mine_ref, other_ref):
    half = value.shape[0] // 2
    low = core_mask(low_ref, value.shape[1])
    first, second = value[:half], value[half:]
    mine_ref[...] = jnp.where(low, first, second)
    other_ref[...] = jnp.where(low, second, first)


def project(scale, low_ref, resid_b, block_refs, mine_ref, other_ref):
    parts = [
        lax.dot_general(resid_b, ref[...], NT, preferred_element_type=jnp.float32) for ref in block_refs
    ]
    split(low_ref, jnp.concatenate(parts, axis=1) * scale, mine_ref, other_ref)


def fields_kernel(low_ref, field_ref, mine_ref, other_ref, *all_refs):
    rows_y, rows_z = field_ref.shape[2:]
    low = low_ref[...] > 0.5
    half = field_ref.shape[0]
    for y in range(rows_y):
        first, second = field_ref[:, 0, y, :], field_ref[:, 1, y, :]
        here = slice(y * rows_z, (y + 1) * rows_z)
        mine_ref[:, here] = jnp.where(low, first, second)
        other_ref[:, here] = jnp.where(low, second, first)
    if all_refs:
        (all_ref,) = all_refs
        wide = all_ref.shape[2]
        step = rows_y * rows_z // wide
        for plane in range(2):
            for y in range(rows_y // step):
                parts = [field_ref[:, plane, y + k * (rows_y // step), :] for k in range(step)]
                rows = jnp.concatenate(parts, axis=0).astype(jnp.bfloat16)
                for d in range(plane, all_ref.shape[0], 2):
                    all_ref[d, :, y * rows_z : (y + 1) * rows_z] = rows


def shares_kernel(scale, all_ref, ends_ref, mids_ref, out_ref):
    sources, rows, wide = all_ref.shape
    every = all_ref[...].reshape(sources * rows, wide)
    parts = rows // out_ref.shape[1]
    for at, ref in ((0, ends_ref), (ends_ref.shape[0], mids_ref)):
        n = ref.shape[0]
        total = 0.0
        for k in range(parts):
            cells = ref[:, k * wide : (k + 1) * wide]
            got = lax.dot_general(every, cells, NT, preferred_element_type=jnp.float32)
            got = got.reshape(sources, parts, rows // parts, n)
            total = total + got[:, k]
        out_ref[:, :, at : at + n] = total * scale


def spread_shares_kernel(parts_ref, out_ref):
    total = jnp.concatenate(
        [parts_ref[k] + parts_ref[k + 1] for k in range(0, parts_ref.shape[0], 2)], axis=1
    )
    for d in range(out_ref.shape[0]):
        out_ref[d] = total


def resid_kernel(
    scale, row, low_ref, x_ref, sib_ref, off_ref, rhs_ref, diag_ref, first_ref, second_ref,
    resid_ref, mine_ref, other_ref, rb_ref,
):
    cells = x_ref.shape[1]
    lane = lax.broadcasted_iota(jnp.int32, (x_ref.shape[0], row), 1)
    for at in range(0, cells, row):
        here = slice(at, at + row)
        x = x_ref[:, here]
        beside = sib_ref[:, here] + off_ref[:, here].astype(jnp.float32)
        if at > 0:
            beside = beside + x_ref[:, at - row : at]
        if at + row < cells:
            beside = beside + x_ref[:, at + row : at + 2 * row]
        beside = beside + jnp.where(lane == 0, 0.0, pltpu.roll(x, 1, 1))
        beside = beside + jnp.where(lane == row - 1, 0.0, pltpu.roll(x, row - 1, 1))
        resid = rhs_ref[:, here] - (diag_ref[:, here] * x - 0.5 * beside)
        resid_ref[:, here] = resid
        rb_ref[:, here] = resid.astype(jnp.bfloat16)
    project(scale, low_ref, rb_ref[...], (first_ref, second_ref), mine_ref, other_ref)


def stacked(value):
    half = value.shape[1] // 2
    return jnp.concatenate([value[:, :half], value[:, half:]], axis=0)


def unstacked(value):
    half = value.shape[0] // 2
    return jnp.concatenate([value[:half], value[half:]], axis=1)


def spread_kernel(mine_ref, other_ref, out_ref):
    total = mine_ref[...] + other_ref[...]
    for d in range(out_ref.shape[0]):
        out_ref[d] = total


def total_kernel(parts_ref, *out_refs):
    total = parts_ref[0]
    for d in range(1, parts_ref.shape[0]):
        total = total + parts_ref[d]
    out_refs[0][...] = stacked(total).astype(jnp.bfloat16)
    if len(out_refs) > 1:
        out_refs[1][...] = total


def update_kernel(scale, tile, has_x, last, root, low_ref, mine_ref, other_ref, resid_ref, diag_ref, *refs):
    refs = list(refs)
    x_ref = refs.pop(0) if has_x else None
    move_ref = None if has_x else refs.pop(0)
    psi_ref = refs.pop(0) if last else None
    first_ref, second_ref, *outs = refs
    low = core_mask(low_ref, 2 * mine_ref.shape[1])
    mine = unstacked(mine_ref[...].astype(jnp.float32))
    other = unstacked(other_ref[...].astype(jnp.float32))
    coeff = jnp.concatenate([jnp.where(low, mine, other), jnp.where(low, other, mine)], axis=0)
    coeff = coeff.astype(jnp.bfloat16)
    if not has_x:
        coeff = jnp.dot(coeff, move_ref[...], preferred_element_type=jnp.float32).astype(jnp.bfloat16)
    cells = resid_ref.shape[1]
    for at in range(0, cells, tile):
        here = slice(at, at + tile)
        corr = 0.0
        start = 0
        for ref in (first_ref, second_ref):
            rows = ref.shape[0]
            some = coeff[:, start : start + rows]
            corr = corr + jnp.dot(some, ref[:, here], preferred_element_type=jnp.float32)
            start += rows
        x = (resid_ref[:, here] - corr * scale) / diag_ref[:, here]
        if has_x:
            x = x + x_ref[:, here]
        if last:
            half = x.shape[0] // 2
            low = core_mask(low_ref, tile)
            outs[0][:, here] = jnp.where(low, x[:half], x[half:])
            outs[1][:, here] = jnp.where(low, x[half:], x[:half])
            raw = jnp.sum(x * psi_ref[:, here].astype(jnp.float32), axis=0, keepdims=True) / root
            rows, wide = outs[2].shape[2:]
            for k in range(tile // wide):
                row = raw[:, k * wide : (k + 1) * wide]
                spot = at // wide + k
                outs[2][spot // rows, :, spot % rows, :] = jnp.broadcast_to(row, (outs[2].shape[1], wide))
        else:
            outs[0][:, here] = x
            outs[1][:, here] = x.astype(jnp.bfloat16)


def table_kernel(plan_ref, coeff_ref, out_ref, rows_ref):
    rows_ref[...] = coeff_ref[...].T
    share = 16
    for j in range(out_ref.shape[0] // share):
        at = pl.multiple_of(plan_ref[TABLE + j] * share, share)
        out_ref[j * share : (j + 1) * share] = rows_ref[pl.ds(at, share)]


def finish_kernel(weights_ref, pick_ref, terms_ref, out_ref):
    def product(one, two):
        return lax.dot_general(
            one, two, (((1,), (0,)), ((), ())),
            precision=lax.Precision.HIGHEST, preferred_element_type=jnp.float32,
        )

    for k in range(terms_ref.shape[1]):
        out_ref[:, k, :] = product(product(weights_ref[...], terms_ref[:, k, :]), pick_ref[...])


def call(kernel, out_shape, in_specs=None, out_specs=None, scratch=()):
    specs = {}
    if in_specs is not None:
        specs["in_specs"] = in_specs
    if out_specs is not None:
        specs["out_specs"] = out_specs
    return pl.pallas_call(
        kernel,
        out_shape=out_shape,
        scratch_shapes=scratch,
        compiler_params=pltpu.CompilerParams(vmem_limit_bytes=VMEM_LIMIT),
        **specs,
    )


def per_device(rhs, potential, eigen_table, win_index, occupied, block_ids, psi_win, smoother):
    local_orbs, planes, rows_y, rows_z = rhs.shape
    n_dom = lax.axis_size("dom")
    n_orb = lax.axis_size("orb")
    cells = rows_y * rows_z
    wide = 2 * local_orbs
    width = local_orbs * n_orb
    scale = 1.0 / math.sqrt(planes * n_dom * rows_y * rows_z)
    n_occ = eigen_table.shape[0]
    per_dev, blk_rows = occupied.shape[:2]
    nproj = block_ids.shape[0]
    chips = n_orb // 2
    ring = chips // 2
    share = blk_rows // chips
    n_rows = nproj * blk_rows
    o = lax.axis_index("orb")
    core = o % 2
    low = core == 0
    groups = [[2 * k + c for k in range(chips)] for c in range(2)]

    def chip_perm(target):
        return [(2 * k + c, 2 * target(k) + c) for k in range(chips) for c in range(2)]

    swap_core = [(i, i ^ 1) for i in range(n_orb)]
    swap_x = chip_perm(lambda k: (k + ring) % chips)
    up_y = chip_perm(lambda k: k // ring * ring + (k + 1) % ring)
    down_y = chip_perm(lambda k: k // ring * ring + (k - 1) % ring)

    def permute(value, pairs):
        return lax.ppermute(value, "orb", pairs)

    def pair(own, other):
        return jnp.concatenate([jnp.where(low, own, other), jnp.where(low, other, own)], axis=0)

    low_mask = jnp.broadcast_to(jnp.where(low, 1.0, 0.0), (local_orbs, 128))
    four = (pltpu.SemaphoreType.DMA((4,)),)

    plane_shape = shape((blk_rows, rows_y, rows_z), jnp.bfloat16)
    piece_shape = shape((2 * share, rows_y, rows_z), jnp.bfloat16)
    plan, offer = call(
        functools.partial(offer_kernel, per_dev, n_orb),
        (shape((TABLE + nproj * chips,), jnp.int32), plane_shape),
        [SMEM, SMEM, ANY],
        (SMEM, VMEM),
        four,
    )(block_ids, o.astype(jnp.int32).reshape(1), occupied)
    offer = permute(offer, swap_core)

    flat_field = shape((local_orbs, cells))
    rhs_mine, rhs_other, rhs_all = call(
        fields_kernel, (flat_field, flat_field, shape((n_orb, 2 * local_orbs, cells // 2), jnp.bfloat16))
    )(low_mask, rhs)
    rhs_all = lax.all_to_all(rhs_all, "orb", 0, 0, tiled=True)
    rhs_wide = pair(rhs_mine, permute(rhs_other, swap_core))

    offer = call(pick_kernel, plane_shape, [SMEM, ANY, VMEM], VMEM, four)(plan, occupied, offer)
    fixed = call(fixed_kernel, plane_shape, [SMEM, ANY], VMEM, four)(plan, occupied)
    fixed = permute(fixed, [(0, 1), (n_orb - 1, n_orb - 2)])
    pieces = call(
        functools.partial(pieces_kernel, n_orb),
        [piece_shape] * ring,
        [SMEM, ANY, VMEM],
        [VMEM] * ring,
        (pltpu.SemaphoreType.DMA((ring,)),),
    )(plan, occupied, fixed)

    got = [pieces[0]]
    for s in range(1, ring):
        pairs = [(c, 2 * s + c) for c in range(2)]
        pairs += [(n_orb - 2 + c, 2 * (ring + (ring - 1 + s) % ring) + c) for c in range(2)]
        got.append(permute(pieces[s], pairs))
    fixed = call(share_kernel, piece_shape, [SMEM] + [VMEM] * ring, VMEM)(plan, *got)

    def scatter(value):
        value = value.reshape(chips, share, rows_y, rows_z)
        return lax.all_to_all(value, "orb", 0, 0, axis_index_groups=groups, tiled=True)

    def take(value, owner):
        return lax.dynamic_index_in_dim(value, owner, 0, keepdims=False)

    def apart(plan, occupied):
        return jnp.zeros((share, rows_y, rows_z), jnp.bfloat16)

    def together(plan, occupied):
        def plane_of(slot, plane):
            dims = (1, blk_rows, 1, rows_y, rows_z)
            return lax.dynamic_slice(occupied, (slot, 0, plane, 0, 0), dims).reshape(plane_shape.shape)

        mid = plan[MID + 1]
        other = permute(plane_of(mid % per_dev, 1 - core), swap_core)
        here = (mid // per_dev) % 2 == core
        again = scatter(jnp.where(here, plane_of(mid % per_dev, core), other))
        return take(again, plan[CHIP + 1])

    same = plan[SAME] == 1
    offered = scatter(offer)
    later, _ = lax.optimization_barrier((plan, got[1]))
    second = lax.cond(later[SAME] == 1, together, apart, later, occupied)
    second = jnp.where(same, second, take(offered, plan[CHIP + 1]))
    mids = jnp.concatenate([take(offered, plan[CHIP]), second], axis=0)

    xs = fixed.reshape(2 * share, cells)
    ys = mids.reshape(2 * share, cells)
    xs, ys = lax.optimization_barrier((xs, ys))
    xs_x = permute(xs, swap_x)
    ys_up = permute(ys, up_y)
    ys_down = permute(ys, down_y)
    xs_x, ys_up, ys_down = lax.optimization_barrier((xs_x, ys_up, ys_down))
    own = jnp.concatenate([xs, xs_x], axis=0)
    line = jnp.concatenate([ys, ys_up, ys_down], axis=0)
    line_x = permute(line, swap_x)
    above = permute(own, up_y)
    below = permute(own, down_y)
    far_up = permute(ys_up[:share], up_y)
    far_down = permute(ys_down[share:], down_y)
    line_x, above, below, far_up, far_down = lax.optimization_barrier(
        (line_x, above, below, far_up, far_down)
    )
    far = jnp.concatenate([far_up, far_down], axis=0)
    far_x = permute(far, swap_x)
    own_up = permute(above[: 2 * share], up_y)
    own_down = permute(below[2 * share :], down_y)
    blocks = [
        jnp.concatenate([own, below, above, own_up, own_down], axis=0),
        jnp.concatenate([line, line_x, far, far_x], axis=0),
    ]

    picks = win_index[:, None] == jnp.arange(n_occ, dtype=jnp.int32)[None, :]
    eps = jnp.sum(jnp.where(picks, eigen_table[None, :], 0.0), axis=1)[:, None]
    eps = pair(eps, permute(eps, swap_core))
    plane_pot = lax.dynamic_index_in_dim(potential, core, 0, keepdims=True).reshape(1, cells)
    diag = 3.0 + plane_pot - eps
    psi_mine, psi_other = call(fields_kernel, (flat_field, flat_field))(
        low_mask, psi_win.astype(jnp.float32)
    )
    psi_other = permute(psi_other.astype(jnp.bfloat16), swap_core)
    psi_wide = pair(psi_mine.astype(jnp.bfloat16), psi_other)

    half_shape = shape((local_orbs, n_rows))
    spread_shape = shape((n_dom, local_orbs, n_rows))
    field_shape = shape((wide, cells))
    flat_shape = (wide, n_rows // 2)

    def total(spread, outs):
        parts = lax.all_to_all(spread, "dom", 0, 0, tiled=True)
        coeff_b, *coeff = call(total_kernel, outs)(parts)
        return coeff, coeff_b, permute(coeff_b, swap_core)

    own_rows = 4 * share
    share_parts = call(
        functools.partial(shares_kernel, scale), shape((n_orb, local_orbs, own_rows))
    )(rhs_all, xs, ys)
    share_parts = lax.all_to_all(share_parts, "orb", 0, 0, tiled=True)
    first_spread = call(spread_shares_kernel, spread_shape)(share_parts)
    row = jnp.arange(n_rows)
    within = row % (2 * share)
    down = jnp.array([0, 0, 1, 1, 3, 3, 2, 2, 0, 3, 1, 0, 3, 1, 2, 2])
    side = jnp.array([0, 1, 0, 1, 0, 1, 0, 1, 0, 0, 0, 1, 1, 1, 0, 1])
    chip = o // 2
    chip_from = (chip // ring + side) % 2 * ring + (chip % ring + down) % ring
    at = chip_from * own_rows + jnp.where(jnp.arange(16) < 8, 0, 2 * share)
    at = jnp.repeat(at, 2 * share) + within
    move = (row[:, None] == at[None, :]).astype(jnp.bfloat16)

    across = []
    for d in range(n_dom - 1):
        for k in range(chips):
            left, right = d * n_orb + 2 * k + 1, (d + 1) * n_orb + 2 * k
            across += [(left, right), (right, left)]

    x = None
    for step in range(ITERS):
        final = step == ITERS - 1
        sums = [shape(flat_shape, jnp.bfloat16)] + ([half_shape] if final else [])
        if step == 0:
            resid, spread = rhs_wide, first_spread
        else:
            sib = permute(x, swap_core)
            off = lax.ppermute(x_b, ("dom", "orb"), across)
            resid, mine, other = call(
                functools.partial(resid_kernel, scale, rows_z),
                (field_shape, half_shape, half_shape),
                scratch=(pltpu.VMEM((wide, cells), jnp.bfloat16),),
            )(low_mask, x, sib, off, rhs_wide, diag, *blocks)
            spread = call(spread_kernel, spread_shape)(mine, permute(other, swap_core))
        coeff, coeff_b, coeff_o = total(spread, sums)
        extra = ([x] if step else [move]) + ([psi_wide] if final else [])
        outs = [field_shape, shape((wide, cells), jnp.bfloat16)]
        if final:
            outs = [shape((local_orbs, cells))] * 2 + [shape((n_dom, n_orb, rows_y // n_dom, rows_z))]
        x, x_b, *rest = call(
            functools.partial(update_kernel, scale, 512, step > 0, final, math.sqrt(width)),
            outs,
        )(low_mask, coeff_b, coeff_o, resid, diag, *extra, *blocks)
    other, raw = x_b, rest[0]

    weights = jnp.broadcast_to(
        smoother.reshape(2 * n_dom, n_dom, 1, 2), (2 * n_dom, n_dom, chips, 2)
    ).reshape(2 * n_dom, n_dom * n_orb)
    terms = lax.all_to_all(
        raw.reshape((n_dom * n_orb,) + raw.shape[2:]), ("dom", "orb"), 0, 0, tiled=True
    )
    z_part = rows_z // n_orb
    z_mine = o * z_part + jnp.arange(z_part)[None, :]
    pick = (jnp.arange(rows_z)[:, None] == z_mine).astype(jnp.float32)
    gradient = call(finish_kernel, shape((2 * n_dom, rows_y // n_dom, z_part)))(weights, pick, terms)

    other = permute(other, swap_core)
    solution = jnp.stack([jnp.where(low, x, other), jnp.where(low, other, x)], axis=1)
    solution = solution.reshape(rhs.shape)

    coeff, raw = lax.optimization_barrier((coeff[0], raw))
    correlations = call(
        table_kernel,
        shape((n_rows, local_orbs)),
        [SMEM, VMEM],
        scratch=(pltpu.VMEM((n_rows, local_orbs), jnp.float32),),
    )(plan, coeff).reshape(nproj, blk_rows, local_orbs)
    return (solution, correlations, gradient)


def solution(mesh):
    return jax.shard_map(
        per_device,
        mesh=mesh,
        in_specs=(
            P("orb", "dom", None, None),
            P("dom", None, None),
            P(),
            P("orb"),
            P("orb", None, "dom", None, None),
            P(),
            P("orb", "dom", None, None),
            P(),
        ),
        out_specs=(P("orb", "dom", None, None), P(None, None, "orb"), P(None, "dom", "orb")),
        check_vma=False,
    )
```

```python
import functools
import math

import jax
import jax.numpy as jnp
from jax import lax
from jax.experimental import pallas as pl
from jax.experimental.pallas import tpu as pltpu
from jax.sharding import PartitionSpec as P

ITERS = 3
VMEM_LIMIT = 16 * 1024 * 1024
NT = (((1,), (1,)), ((), ()))
SMEM = pl.BlockSpec(memory_space=pltpu.SMEM)
ANY = pl.BlockSpec(memory_space=pl.ANY)
VMEM = pl.BlockSpec(memory_space=pltpu.VMEM)

MID, CHIP, SAME, SLOT, CORE, DEV, TABLE = 0, 2, 4, 5, 6, 7, 8


def shape(dims, dtype=jnp.float32):
    return jax.ShapeDtypeStruct(dims, dtype)


def plan(per_dev, n_orb, ids_ref, dev_ref, out_ref):
    nproj = ids_ref.shape[0]
    chips = n_orb // 2
    ring = chips // 2
    last = per_dev * n_orb - 1
    dev = dev_ref[0]
    chip = dev // 2
    seen = jnp.int32(0)
    mids = [jnp.int32(0)] * (nproj - 2)
    order = []
    for j in range(nproj):
        block = ids_ref[j]
        middle = jnp.logical_and(block != 0, block != last)
        for k in range(nproj - 2):
            mids[k] = jnp.where(jnp.logical_and(middle, seen == k), block, mids[k])
        order.append(jnp.where(block == 0, 0, jnp.where(block == last, 1, 2 + seen)))
        seen = seen + jnp.where(middle, 1, 0)
    owners = [mid // (2 * per_dev) for mid in mids]
    for k in range(nproj - 2):
        out_ref[MID + k] = mids[k]
        out_ref[CHIP + k] = owners[k]
    out_ref[SAME] = jnp.where(owners[0] == owners[1], 1, 0)
    offer = jnp.where(chip == owners[0], mids[0], mids[1])
    out_ref[SLOT] = offer % per_dev
    out_ref[CORE] = (offer // per_dev) % 2
    out_ref[DEV] = dev
    y, x = chip % ring, chip // ring
    for j in range(nproj):
        for q in range(chips):
            down = (q // 2 + ring - y) % ring
            first = jnp.where(down == 1, 4, jnp.where(down == 3, 8, jnp.where(down == 2, 12, 0)))
            first = first + (order[j] + x) % 2 * 2 + q % 2
            down = (q % ring + ring - y) % ring
            side = (q // ring + x) % 2
            second = jnp.where(down == 1, 4, jnp.where(down == 3, 2, 0)) + side * 6
            second = 14 + jnp.where(down == 2, 12 + side * 2, second) + order[j]
            out_ref[TABLE + j * chips + q] = jnp.where(order[j] < 2, first, second)


def copies(source, target, sem):
    parts = sem.shape[0]
    rows = target.shape[0] // parts
    return [
        pltpu.make_async_copy(source(k * rows, rows), target.at[pl.ds(k * rows, rows)], sem.at[k])
        for k in range(parts)
    ]


def run(started):
    for copy in started:
        copy.start()
    for copy in started:
        copy.wait()


def offer_kernel(per_dev, n_orb, ids_ref, dev_ref, occupied_ref, plan_ref, same_ref, offer_ref, sem):
    plan(per_dev, n_orb, ids_ref, dev_ref, plan_ref)
    same_ref[0] = plan_ref[SAME]
    core = plan_ref[DEV] % 2
    run(copies(lambda at, n: occupied_ref.at[plan_ref[SLOT], pl.ds(at, n), 1 - core], offer_ref, sem))


def fixed_kernel(plan_ref, occupied_ref, fixed_ref, sem):
    core = plan_ref[DEV] % 2
    slot = core * (occupied_ref.shape[0] - 1)
    run(copies(lambda at, n: occupied_ref.at[slot, pl.ds(at, n), 1 - core], fixed_ref, sem))


def pick_kernel(plan_ref, occupied_ref, offer_ref, out_ref, sem):
    core = plan_ref[DEV] % 2

    @pl.when(plan_ref[CORE] == core)
    def _():
        run(copies(lambda at, n: occupied_ref.at[plan_ref[SLOT], pl.ds(at, n), core], out_ref, sem))

    @pl.when(plan_ref[CORE] != core)
    def _():
        step = 16

        @pl.loop(0, out_ref.shape[0] // step)
        def _(k):
            here = pl.ds(k * step, step)
            out_ref[here] = offer_ref[here]


def pieces_kernel(n_orb, plan_ref, occupied_ref, fixed_ref, *refs):
    *piece_refs, sem = refs
    dev = plan_ref[DEV]
    core = dev % 2
    last = occupied_ref.shape[0] - 1
    ring = len(piece_refs)
    rows = piece_refs[0].shape[0]

    def at(s):
        return pl.ds(jnp.where(dev < n_orb // 2, s, (ring - 1 + s) % ring) * rows, rows)

    @pl.when(jnp.logical_or(dev == 0, dev == n_orb - 1))
    def _():
        run([
            pltpu.make_async_copy(occupied_ref.at[core * last, at(s), core], ref, sem.at[s])
            for s, ref in enumerate(piece_refs)
        ])

    @pl.when(jnp.logical_or(dev == 1, dev == n_orb - 2))
    def _():
        for s, ref in enumerate(piece_refs):
            ref[...] = fixed_ref[at(s)]


def share_kernel(plan_ref, *refs):
    *piece_refs, out_ref = refs
    ring = len(piece_refs)
    chip = plan_ref[DEV] // 2
    y, x = chip % ring, chip // ring
    away = (y + x) % ring
    for s, ref in enumerate(piece_refs):

        @pl.when(away == s)
        def _(ref=ref):
            out_ref[...] = ref[...]


def core_mask(low_ref, width):
    return jnp.concatenate([low_ref[...]] * (width // low_ref.shape[1]), axis=1) > 0.5


def split(low_ref, value, mine_ref, other_ref):
    half = value.shape[0] // 2
    low = core_mask(low_ref, value.shape[1])
    first, second = value[:half], value[half:]
    mine_ref[...] = jnp.where(low, first, second)
    other_ref[...] = jnp.where(low, second, first)


def project(scale, low_ref, resid_b, block_refs, mine_ref, other_ref):
    parts = [
        lax.dot_general(resid_b, ref[...], NT, preferred_element_type=jnp.float32) for ref in block_refs
    ]
    split(low_ref, jnp.concatenate(parts, axis=1) * scale, mine_ref, other_ref)


def fields_kernel(low_ref, field_ref, mine_ref, other_ref, *both_refs):
    rows_y, rows_z = field_ref.shape[2:]
    low = low_ref[...] > 0.5
    for y in range(rows_y):
        first, second = field_ref[:, 0, y, :], field_ref[:, 1, y, :]
        here = slice(y * rows_z, (y + 1) * rows_z)
        mine_ref[:, here] = jnp.where(low, first, second)
        other_ref[:, here] = jnp.where(low, second, first)
        for ref in both_refs:
            ref[:, here] = jnp.concatenate([first, second], axis=0).astype(jnp.bfloat16)


def pair_kernel(low_ref, mine_ref, other_ref, out_ref):
    half = mine_ref.shape[0]
    low = core_mask(low_ref, mine_ref.shape[1])
    mine, other = mine_ref[...], other_ref[...]
    out_ref[:half] = jnp.where(low, mine, other)
    out_ref[half:] = jnp.where(low, other, mine)


def take_kernel(plan_ref, offered_ref, second_ref, out_ref):
    rows = offered_ref.shape[1]
    out_ref[:rows] = offered_ref[plan_ref[CHIP]]

    @pl.when(plan_ref[SAME] == 1)
    def _():
        out_ref[rows:] = second_ref[...]

    @pl.when(plan_ref[SAME] != 1)
    def _():
        out_ref[rows:] = offered_ref[plan_ref[CHIP + 1]]


def shares_kernel(scale, low_ref, all_ref, ends_ref, mids_ref, out_ref):
    devices, orbs = out_ref.shape[:2]
    low = low_ref[0:1, 0:1] > 0.5
    for at, ref in ((0, ends_ref), (ends_ref.shape[0], mids_ref)):
        n = ref.shape[0]
        got = lax.dot_general(all_ref[...], ref[...], NT, preferred_element_type=jnp.float32)
        got = got.reshape(devices, 2 * orbs, n)
        got = jnp.where(low[None], got[:, :orbs], got[:, orbs:])
        out_ref[:, :, at : at + n] = got * scale


def spread_shares_kernel(parts_ref, out_ref):
    total = jnp.concatenate(
        [parts_ref[k] + parts_ref[k + 1] for k in range(0, parts_ref.shape[0], 2)], axis=1
    )
    for d in range(out_ref.shape[0]):
        out_ref[d] = total


def resid_kernel(
    scale, row, low_ref, x_ref, sib_ref, off_ref, rhs_ref, diag_ref, first_ref, second_ref,
    resid_ref, mine_ref, other_ref, rb_ref,
):
    cells = x_ref.shape[1]
    lane = lax.broadcasted_iota(jnp.int32, (x_ref.shape[0], row), 1)
    for at in range(0, cells, row):
        here = slice(at, at + row)
        x = x_ref[:, here]
        beside = sib_ref[:, here] + off_ref[:, here].astype(jnp.float32)
        if at > 0:
            beside = beside + x_ref[:, at - row : at]
        if at + row < cells:
            beside = beside + x_ref[:, at + row : at + 2 * row]
        beside = beside + jnp.where(lane == 0, 0.0, pltpu.roll(x, 1, 1))
        beside = beside + jnp.where(lane == row - 1, 0.0, pltpu.roll(x, row - 1, 1))
        resid = rhs_ref[:, here] - (diag_ref[:, here] * x - 0.5 * beside)
        resid_ref[:, here] = resid
        rb_ref[:, here] = resid.astype(jnp.bfloat16)
    project(scale, low_ref, rb_ref[...], (first_ref, second_ref), mine_ref, other_ref)


def stacked(value):
    half = value.shape[1] // 2
    return jnp.concatenate([value[:, :half], value[:, half:]], axis=0)


def unstacked(value):
    half = value.shape[0] // 2
    return jnp.concatenate([value[:half], value[half:]], axis=1)


def spread_kernel(mine_ref, other_ref, out_ref):
    total = mine_ref[...] + other_ref[...]
    for d in range(out_ref.shape[0]):
        out_ref[d] = total


def total_kernel(parts_ref, *out_refs):
    total = parts_ref[0]
    for d in range(1, parts_ref.shape[0]):
        total = total + parts_ref[d]
    out_refs[0][...] = stacked(total).astype(jnp.bfloat16)
    if len(out_refs) > 1:
        out_refs[1][...] = total


def pack_kernel(splits, *refs):
    pieces, outs = refs[: sum(splits)], refs[sum(splits) :]
    for count, out_ref in zip(splits, outs):
        at = 0
        for ref in pieces[:count]:
            rows = ref.shape[0]
            out_ref[at : at + rows] = ref[...]
            at += rows
        pieces = pieces[count:]


def update_kernel(scale, tile, has_x, last, root, splits, low_ref, mine_ref, other_ref, resid_ref, diag_ref, *refs):
    refs = list(refs)
    x_ref = refs.pop(0) if has_x else None
    move_ref = None if has_x else refs.pop(0)
    psi_ref = refs.pop(0) if last else None
    if has_x:
        first_ref, second_ref, *outs = refs
    else:
        *refs, x_out, x_b_out, first_ref, second_ref = refs
        outs = [x_out, x_b_out]
    low = core_mask(low_ref, 2 * mine_ref.shape[1])
    mine = unstacked(mine_ref[...].astype(jnp.float32))
    other = unstacked(other_ref[...].astype(jnp.float32))
    coeff = jnp.concatenate([jnp.where(low, mine, other), jnp.where(low, other, mine)], axis=0)
    coeff = coeff.astype(jnp.bfloat16)
    if not has_x:
        coeff = jnp.dot(coeff, move_ref[...], preferred_element_type=jnp.float32).astype(jnp.bfloat16)
        pack_kernel(splits, *refs, first_ref, second_ref)
    cells = resid_ref.shape[1]
    for at in range(0, cells, tile):
        here = slice(at, at + tile)
        corr = 0.0
        start = 0
        for ref in (first_ref, second_ref):
            rows = ref.shape[0]
            some = coeff[:, start : start + rows]
            corr = corr + jnp.dot(some, ref[:, here], preferred_element_type=jnp.float32)
            start += rows
        x = (resid_ref[:, here] - corr * scale) / diag_ref[:, here]
        if has_x:
            x = x + x_ref[:, here]
        if last:
            half = x.shape[0] // 2
            low = core_mask(low_ref, tile)
            outs[0][:, here] = jnp.where(low, x[:half], x[half:])
            outs[1][:, here] = jnp.where(low, x[half:], x[:half])
            raw = jnp.sum(x * psi_ref[:, here].astype(jnp.float32), axis=0, keepdims=True) / root
            rows, wide = outs[2].shape[2:]
            for k in range(tile // wide):
                row = raw[:, k * wide : (k + 1) * wide]
                spot = at // wide + k
                outs[2][spot // rows, :, spot % rows, :] = jnp.broadcast_to(row, (outs[2].shape[1], wide))
        else:
            outs[0][:, here] = x
            outs[1][:, here] = x.astype(jnp.bfloat16)


def table_kernel(plan_ref, coeff_ref, out_ref, rows_ref):
    rows_ref[...] = coeff_ref[...].T
    share = 16
    for j in range(out_ref.shape[0] // share):
        at = pl.multiple_of(plan_ref[TABLE + j] * share, share)
        out_ref[j * share : (j + 1) * share] = rows_ref[pl.ds(at, share)]


def finish_kernel(weights_ref, pick_ref, terms_ref, out_ref):
    def product(one, two):
        return lax.dot_general(
            one, two, (((1,), (0,)), ((), ())),
            precision=lax.Precision.HIGHEST, preferred_element_type=jnp.float32,
        )

    for k in range(terms_ref.shape[1]):
        out_ref[:, k, :] = product(product(weights_ref[...], terms_ref[:, k, :]), pick_ref[...])


def call(kernel, out_shape, in_specs=None, out_specs=None, scratch=()):
    specs = {}
    if in_specs is not None:
        specs["in_specs"] = in_specs
    if out_specs is not None:
        specs["out_specs"] = out_specs
    return pl.pallas_call(
        kernel,
        out_shape=out_shape,
        scratch_shapes=scratch,
        compiler_params=pltpu.CompilerParams(vmem_limit_bytes=VMEM_LIMIT),
        **specs,
    )


def per_device(rhs, potential, eigen_table, win_index, occupied, block_ids, psi_win, smoother):
    local_orbs, planes, rows_y, rows_z = rhs.shape
    n_dom = lax.axis_size("dom")
    n_orb = lax.axis_size("orb")
    cells = rows_y * rows_z
    wide = 2 * local_orbs
    width = local_orbs * n_orb
    scale = 1.0 / math.sqrt(planes * n_dom * rows_y * rows_z)
    n_occ = eigen_table.shape[0]
    per_dev, blk_rows = occupied.shape[:2]
    nproj = block_ids.shape[0]
    chips = n_orb // 2
    ring = chips // 2
    share = blk_rows // chips
    n_rows = nproj * blk_rows
    o = lax.axis_index("orb")
    core = o % 2
    low = core == 0
    groups = [[2 * k + c for k in range(chips)] for c in range(2)]

    def chip_perm(target):
        return [(2 * k + c, 2 * target(k) + c) for k in range(chips) for c in range(2)]

    swap_core = [(i, i ^ 1) for i in range(n_orb)]
    swap_x = chip_perm(lambda k: (k + ring) % chips)
    up_y = chip_perm(lambda k: k // ring * ring + (k + 1) % ring)
    down_y = chip_perm(lambda k: k // ring * ring + (k - 1) % ring)

    def permute(value, pairs):
        return lax.ppermute(value, "orb", pairs)

    def pair(own, other):
        return jnp.concatenate([jnp.where(low, own, other), jnp.where(low, other, own)], axis=0)

    low_mask = jnp.broadcast_to(jnp.where(low, 1.0, 0.0), (local_orbs, 128))
    four = (pltpu.SemaphoreType.DMA((4,)),)

    plane_shape = shape((blk_rows, rows_y, rows_z), jnp.bfloat16)
    piece_shape = shape((2 * share, rows_y, rows_z), jnp.bfloat16)
    plan, same, offer = call(
        functools.partial(offer_kernel, per_dev, n_orb),
        (shape((TABLE + nproj * chips,), jnp.int32), shape((1,), jnp.int32), plane_shape),
        [SMEM, SMEM, ANY],
        (SMEM, SMEM, VMEM),
        four,
    )(block_ids, o.astype(jnp.int32).reshape(1), occupied)
    offer = permute(offer, swap_core)

    flat_field = shape((local_orbs, cells))
    field_shape = shape((wide, cells))
    rhs_mine, rhs_other, rhs_b = call(
        fields_kernel, (flat_field, flat_field, shape((wide, cells), jnp.bfloat16))
    )(low_mask, rhs)
    rhs_all = lax.all_gather(rhs_b, "orb", tiled=True)
    rhs_wide = call(pair_kernel, field_shape)(low_mask, rhs_mine, permute(rhs_other, swap_core))

    offer = call(pick_kernel, plane_shape, [SMEM, ANY, VMEM], VMEM, four)(plan, occupied, offer)
    fixed = call(fixed_kernel, plane_shape, [SMEM, ANY], VMEM, four)(plan, occupied)
    fixed = permute(fixed, [(0, 1), (n_orb - 1, n_orb - 2)])
    offer, fixed = lax.optimization_barrier((offer, fixed))
    pieces = call(
        functools.partial(pieces_kernel, n_orb),
        [piece_shape] * ring,
        [SMEM, ANY, VMEM],
        [VMEM] * ring,
        (pltpu.SemaphoreType.DMA((ring,)),),
    )(plan, occupied, fixed)

    got = [pieces[0]]
    for s in range(1, ring):
        pairs = [(c, 2 * s + c) for c in range(2)]
        pairs += [(n_orb - 2 + c, 2 * (ring + (ring - 1 + s) % ring) + c) for c in range(2)]
        got.append(permute(pieces[s], pairs))
    fixed = call(share_kernel, piece_shape, [SMEM] + [VMEM] * ring, VMEM)(plan, *got)

    def scatter(value):
        value = value.reshape(chips, share, rows_y, rows_z)
        return lax.all_to_all(value, "orb", 0, 0, axis_index_groups=groups, tiled=True)

    def take(value, owner):
        return lax.dynamic_index_in_dim(value, owner, 0, keepdims=False)

    def apart(plan, occupied):
        return jnp.zeros((share, rows_y, rows_z), jnp.bfloat16)

    def together(plan, occupied):
        def plane_of(slot, plane):
            dims = (1, blk_rows, 1, rows_y, rows_z)
            return lax.dynamic_slice(occupied, (slot, 0, plane, 0, 0), dims).reshape(plane_shape.shape)

        mid = plan[MID + 1]
        other = permute(plane_of(mid % per_dev, 1 - core), swap_core)
        here = (mid // per_dev) % 2 == core
        again = scatter(jnp.where(here, plane_of(mid % per_dev, core), other))
        return take(again, plan[CHIP + 1])

    offered = scatter(offer)
    second = lax.cond(same[0] == 1, together, apart, plan, occupied)
    mids = call(
        take_kernel, shape((2 * share, rows_y, rows_z), jnp.bfloat16), [SMEM, VMEM, VMEM], VMEM
    )(plan, offered, second)

    xs = fixed.reshape(2 * share, cells)
    ys = mids.reshape(2 * share, cells)
    xs, ys = lax.optimization_barrier((xs, ys))
    xs_x = permute(xs, swap_x)
    ys_up = permute(ys, up_y)
    ys_down = permute(ys, down_y)
    own_rows = 4 * share
    half_shape = shape((local_orbs, n_rows))
    spread_shape = shape((n_dom, local_orbs, n_rows))
    parts = call(functools.partial(shares_kernel, scale), shape((n_orb, local_orbs, own_rows)))(
        low_mask, rhs_all, xs, ys
    )
    parts = lax.all_to_all(parts, "orb", 0, 0, tiled=True)
    xs_x, ys_up, ys_down, parts = lax.optimization_barrier((xs_x, ys_up, ys_down, parts))
    own, line = call(
        functools.partial(pack_kernel, (2, 3)),
        (shape((4 * share, cells), jnp.bfloat16), shape((6 * share, cells), jnp.bfloat16)),
    )(xs, xs_x, ys, ys_up, ys_down)
    line_x = permute(line, swap_x)
    above = permute(own, up_y)
    below = permute(own, down_y)
    far_up = permute(ys_up[:share], up_y)
    far_down = permute(ys_down[share:], down_y)
    first_parts = lax.all_to_all(
        call(spread_shares_kernel, spread_shape)(parts), "dom", 0, 0, tiled=True
    )
    line_x, above, below, far_up, far_down, first_parts = lax.optimization_barrier(
        (line_x, above, below, far_up, far_down, first_parts)
    )
    far = jnp.concatenate([far_up, far_down], axis=0)
    far_x = permute(far, swap_x)
    own_up = permute(above[: 2 * share], up_y)
    own_down = permute(below[2 * share :], down_y)
    pieces = [own, below, above, own_up, own_down, line, line_x, far, far_x]
    blocks_shape = [shape((n_rows // 2, cells), jnp.bfloat16)] * 2

    picks = win_index[:, None] == jnp.arange(n_occ, dtype=jnp.int32)[None, :]
    eps = jnp.sum(jnp.where(picks, eigen_table[None, :], 0.0), axis=1)[:, None]
    eps = pair(eps, permute(eps, swap_core))
    plane_pot = lax.dynamic_index_in_dim(potential, core, 0, keepdims=True).reshape(1, cells)
    diag = 3.0 + plane_pot - eps
    psi_mine, psi_other = call(fields_kernel, (flat_field, flat_field))(
        low_mask, psi_win.astype(jnp.float32)
    )
    psi_wide = call(pair_kernel, field_shape)(
        low_mask, psi_mine, permute(psi_other.astype(jnp.bfloat16), swap_core).astype(jnp.float32)
    )
    flat_shape = (wide, n_rows // 2)

    def total(parts, outs):
        coeff_b, *coeff = call(total_kernel, outs)(parts)
        return coeff, coeff_b, permute(coeff_b, swap_core)

    row = jnp.arange(n_rows)
    within = row % (2 * share)
    down = jnp.array([0, 0, 1, 1, 3, 3, 2, 2, 0, 3, 1, 0, 3, 1, 2, 2])
    side = jnp.array([0, 1, 0, 1, 0, 1, 0, 1, 0, 0, 0, 1, 1, 1, 0, 1])
    chip = o // 2
    chip_from = (chip // ring + side) % 2 * ring + (chip % ring + down) % ring
    at = chip_from * own_rows + jnp.where(jnp.arange(16) < 8, 0, 2 * share)
    at = jnp.repeat(at, 2 * share) + within
    move = (row[:, None] == at[None, :]).astype(jnp.bfloat16)

    across = []
    for d in range(n_dom - 1):
        for k in range(chips):
            left, right = d * n_orb + 2 * k + 1, (d + 1) * n_orb + 2 * k
            across += [(left, right), (right, left)]

    x = None
    for step in range(ITERS):
        final = step == ITERS - 1
        sums = [shape(flat_shape, jnp.bfloat16)] + ([half_shape] if final else [])
        if step == 0:
            resid, parts = rhs_wide, first_parts
        else:
            sib = permute(x, swap_core)
            off = lax.ppermute(x_b, ("dom", "orb"), across)
            resid, mine, other = call(
                functools.partial(resid_kernel, scale, rows_z),
                (field_shape, half_shape, half_shape),
                scratch=(pltpu.VMEM((wide, cells), jnp.bfloat16),),
            )(low_mask, x, sib, off, rhs_wide, diag, *blocks)
            spread = call(spread_kernel, spread_shape)(mine, permute(other, swap_core))
            parts = lax.all_to_all(spread, "dom", 0, 0, tiled=True)
        coeff, coeff_b, coeff_o = total(parts, sums)
        extra = ([x] if step else [move]) + ([psi_wide] if final else [])
        outs = [field_shape, shape((wide, cells), jnp.bfloat16)]
        if final:
            outs = [shape((local_orbs, cells))] * 2 + [shape((n_dom, n_orb, rows_y // n_dom, rows_z))]
        if step == 0:
            outs, blocks = outs + blocks_shape, pieces
        x, x_b, *rest = call(
            functools.partial(update_kernel, scale, 512, step > 0, final, math.sqrt(width), (5, 4)),
            outs,
        )(low_mask, coeff_b, coeff_o, resid, diag, *extra, *blocks)
        if step == 0:
            blocks = rest
    other, raw = x_b, rest[0]

    weights = jnp.broadcast_to(
        smoother.reshape(2 * n_dom, n_dom, 1, 2), (2 * n_dom, n_dom, chips, 2)
    ).reshape(2 * n_dom, n_dom * n_orb)
    terms = lax.all_to_all(
        raw.reshape((n_dom * n_orb,) + raw.shape[2:]), ("dom", "orb"), 0, 0, tiled=True
    )
    z_part = rows_z // n_orb
    z_mine = o * z_part + jnp.arange(z_part)[None, :]
    pick = (jnp.arange(rows_z)[:, None] == z_mine).astype(jnp.float32)
    gradient = call(finish_kernel, shape((2 * n_dom, rows_y // n_dom, z_part)))(weights, pick, terms)

    other = permute(other, swap_core)
    solution = jnp.stack([jnp.where(low, x, other), jnp.where(low, other, x)], axis=1)
    solution = solution.reshape(rhs.shape)

    coeff, raw = lax.optimization_barrier((coeff[0], raw))
    correlations = call(
        table_kernel,
        shape((n_rows, local_orbs)),
        [SMEM, VMEM],
        scratch=(pltpu.VMEM((n_rows, local_orbs), jnp.float32),),
    )(plan, coeff).reshape(nproj, blk_rows, local_orbs)
    return (solution, correlations, gradient)


def solution(mesh):
    return jax.shard_map(
        per_device,
        mesh=mesh,
        in_specs=(
            P("orb", "dom", None, None),
            P("dom", None, None),
            P(),
            P("orb"),
            P("orb", None, "dom", None, None),
            P(),
            P("orb", "dom", None, None),
            P(),
        ),
        out_specs=(P("orb", "dom", None, None), P(None, None, "orb"), P(None, "dom", "orb")),
        check_vma=False,
    )
```

```python
import functools
import math

import jax
import jax.numpy as jnp
from jax import lax
from jax.experimental import pallas as pl
from jax.experimental.pallas import tpu as pltpu
from jax.sharding import PartitionSpec as P

ITERS = 3
VMEM_LIMIT = 16 * 1024 * 1024
NT = (((1,), (1,)), ((), ()))
SMEM = pl.BlockSpec(memory_space=pltpu.SMEM)
ANY = pl.BlockSpec(memory_space=pl.ANY)
VMEM = pl.BlockSpec(memory_space=pltpu.VMEM)
HBM = pl.BlockSpec(memory_space=pltpu.HBM)

MID, CHIP, SAME, SLOT, CORE, DEV, TABLE = 0, 2, 4, 5, 6, 7, 8


def shape(dims, dtype=jnp.float32):
    return jax.ShapeDtypeStruct(dims, dtype)


def plan(per_dev, n_orb, ids_ref, dev_ref, out_ref):
    nproj = ids_ref.shape[0]
    chips = n_orb // 2
    ring = chips // 2
    last = per_dev * n_orb - 1
    dev = dev_ref[0]
    chip = dev // 2
    seen = jnp.int32(0)
    mids = [jnp.int32(0)] * (nproj - 2)
    order = []
    for j in range(nproj):
        block = ids_ref[j]
        middle = jnp.logical_and(block != 0, block != last)
        for k in range(nproj - 2):
            mids[k] = jnp.where(jnp.logical_and(middle, seen == k), block, mids[k])
        order.append(jnp.where(block == 0, 0, jnp.where(block == last, 1, 2 + seen)))
        seen = seen + jnp.where(middle, 1, 0)
    owners = [mid // (2 * per_dev) for mid in mids]
    for k in range(nproj - 2):
        out_ref[MID + k] = mids[k]
        out_ref[CHIP + k] = owners[k]
    out_ref[SAME] = jnp.where(owners[0] == owners[1], 1, 0)
    offer = jnp.where(chip == owners[0], mids[0], mids[1])
    out_ref[SLOT] = offer % per_dev
    out_ref[CORE] = (offer // per_dev) % 2
    out_ref[DEV] = dev
    y, x = chip % ring, chip // ring
    for j in range(nproj):
        for q in range(chips):
            down = (q // 2 + ring - y) % ring
            first = jnp.where(down == 1, 4, jnp.where(down == 3, 8, jnp.where(down == 2, 12, 0)))
            first = first + (order[j] + x) % 2 * 2 + q % 2
            down = (q % ring + ring - y) % ring
            side = (q // ring + x) % 2
            second = jnp.where(down == 1, 4, jnp.where(down == 3, 2, 0)) + side * 6
            second = 14 + jnp.where(down == 2, 12 + side * 2, second) + order[j]
            out_ref[TABLE + j * chips + q] = jnp.where(order[j] < 2, first, second)


def copies(source, target, sem):
    parts = sem.shape[0]
    rows = target.shape[0] // parts
    return [
        pltpu.make_async_copy(source(k * rows, rows), target.at[pl.ds(k * rows, rows)], sem.at[k])
        for k in range(parts)
    ]


def run(started):
    for copy in started:
        copy.start()
    for copy in started:
        copy.wait()


def offer_kernel(per_dev, n_orb, ids_ref, dev_ref, occupied_ref, plan_ref, same_ref, offer_ref, sem):
    plan(per_dev, n_orb, ids_ref, dev_ref, plan_ref)
    same_ref[0] = plan_ref[SAME]
    core = plan_ref[DEV] % 2
    run(copies(lambda at, n: occupied_ref.at[plan_ref[SLOT], pl.ds(at, n), 1 - core], offer_ref, sem))


def fixed_kernel(plan_ref, occupied_ref, fixed_ref, sem):
    core = plan_ref[DEV] % 2
    slot = core * (occupied_ref.shape[0] - 1)
    run(copies(lambda at, n: occupied_ref.at[slot, pl.ds(at, n), 1 - core], fixed_ref, sem))


def pick_kernel(plan_ref, occupied_ref, offer_ref, out_ref, sem):
    core = plan_ref[DEV] % 2

    @pl.when(plan_ref[CORE] == core)
    def _():
        run(copies(lambda at, n: occupied_ref.at[plan_ref[SLOT], pl.ds(at, n), core], out_ref, sem))

    @pl.when(plan_ref[CORE] != core)
    def _():
        step = 16

        @pl.loop(0, out_ref.shape[0] // step)
        def _(k):
            here = pl.ds(k * step, step)
            out_ref[here] = offer_ref[here]


def pieces_kernel(n_orb, plan_ref, occupied_ref, fixed_ref, *refs):
    *piece_refs, sem = refs
    dev = plan_ref[DEV]
    core = dev % 2
    last = occupied_ref.shape[0] - 1
    ring = len(piece_refs)
    rows = piece_refs[0].shape[0]

    def at(s):
        return pl.ds(jnp.where(dev < n_orb // 2, s, (ring - 1 + s) % ring) * rows, rows)

    @pl.when(jnp.logical_or(dev == 0, dev == n_orb - 1))
    def _():
        run([
            pltpu.make_async_copy(occupied_ref.at[core * last, at(s), core], ref, sem.at[s])
            for s, ref in enumerate(piece_refs)
        ])

    @pl.when(jnp.logical_or(dev == 1, dev == n_orb - 2))
    def _():
        for s, ref in enumerate(piece_refs):
            ref[...] = fixed_ref[at(s)]


def share_kernel(plan_ref, *refs):
    *piece_refs, out_ref = refs
    ring = len(piece_refs)
    chip = plan_ref[DEV] // 2
    y, x = chip % ring, chip // ring
    away = (y + x) % ring
    for s, ref in enumerate(piece_refs):

        @pl.when(away == s)
        def _(ref=ref):
            out_ref[...] = ref[...]


def core_mask(low_ref, width):
    return jnp.concatenate([low_ref[...]] * (width // low_ref.shape[1]), axis=1) > 0.5


def split(low_ref, value, mine_ref, other_ref):
    half = value.shape[0] // 2
    low = core_mask(low_ref, value.shape[1])
    first, second = value[:half], value[half:]
    mine_ref[...] = jnp.where(low, first, second)
    other_ref[...] = jnp.where(low, second, first)


def project(scale, low_ref, resid_b, block_refs, mine_ref, other_ref):
    parts = [
        lax.dot_general(resid_b, ref[...], NT, preferred_element_type=jnp.float32) for ref in block_refs
    ]
    split(low_ref, jnp.concatenate(parts, axis=1) * scale, mine_ref, other_ref)


def fields_kernel(low_ref, field_ref, mine_ref, other_ref):
    rows_y, rows_z = field_ref.shape[2:]
    low = low_ref[...] > 0.5
    for y in range(rows_y):
        first, second = field_ref[:, 0, y, :], field_ref[:, 1, y, :]
        here = slice(y * rows_z, (y + 1) * rows_z)
        mine_ref[:, here] = jnp.where(low, first, second)
        other_ref[:, here] = jnp.where(low, second, first)


def pair_kernel(low_ref, mine_ref, other_ref, out_ref, *rounded_refs):
    half = mine_ref.shape[0]
    low = core_mask(low_ref, mine_ref.shape[1])
    mine, other = mine_ref[...], other_ref[...]
    both = jnp.concatenate([jnp.where(low, mine, other), jnp.where(low, other, mine)], axis=0)
    out_ref[...] = both
    for ref in rounded_refs:
        ref[...] = both.astype(jnp.bfloat16)


def take_kernel(plan_ref, offered_ref, second_ref, out_ref):
    rows = offered_ref.shape[1]
    out_ref[:rows] = offered_ref[plan_ref[CHIP]]

    @pl.when(plan_ref[SAME] == 1)
    def _():
        out_ref[rows:] = second_ref[...]

    @pl.when(plan_ref[SAME] != 1)
    def _():
        out_ref[rows:] = offered_ref[plan_ref[CHIP + 1]]


def shares_kernel(scale, places, plan_ref, *refs):
    *field_refs, ends_ref, mids_ref, out_ref = refs
    devices, orbs, lanes = out_ref.shape
    ring = devices // 4
    chip = plan_ref[DEV] // 2
    y, x = chip % ring, chip // ring
    spare = lanes - ends_ref.shape[0] - mids_ref.shape[0]
    for down, field_ref in zip(places, field_refs):
        field = field_ref[...]
        got = [
            lax.dot_general(field, ref[...], NT, preferred_element_type=jnp.float32)
            for ref in (ends_ref, mids_ref)
        ]
        rows = jnp.concatenate(got + [jnp.zeros((field.shape[0], spare), jnp.float32)], axis=1) * scale
        for k in range(rows.shape[0] // (2 * orbs)):
            side = down[1] + k
            to = 2 * ((x + side) % 2 * ring + (y + down[0]) % ring)
            at = k * 2 * orbs
            out_ref[pl.ds(to, 1)] = rows[at : at + orbs][None]
            out_ref[pl.ds(to + 1, 1)] = rows[at + orbs : at + 2 * orbs][None]


def spread_shares_kernel(parts_ref, out_ref):
    rows = out_ref.shape[2] * 2 // parts_ref.shape[0]
    total = jnp.concatenate(
        [(parts_ref[k] + parts_ref[k + 1])[:, :rows] for k in range(0, parts_ref.shape[0], 2)], axis=1
    )
    for d in range(out_ref.shape[0]):
        out_ref[d] = total


def resid_kernel(
    scale, row, low_ref, x_ref, sib_ref, off_ref, rhs_ref, diag_ref, first_ref, second_ref,
    resid_ref, mine_ref, other_ref, rb_ref,
):
    cells = x_ref.shape[1]
    lane = lax.broadcasted_iota(jnp.int32, (x_ref.shape[0], row), 1)
    for at in range(0, cells, row):
        here = slice(at, at + row)
        x = x_ref[:, here]
        beside = sib_ref[:, here] + off_ref[:, here].astype(jnp.float32)
        if at > 0:
            beside = beside + x_ref[:, at - row : at]
        if at + row < cells:
            beside = beside + x_ref[:, at + row : at + 2 * row]
        beside = beside + jnp.where(lane == 0, 0.0, pltpu.roll(x, 1, 1))
        beside = beside + jnp.where(lane == row - 1, 0.0, pltpu.roll(x, row - 1, 1))
        resid = rhs_ref[:, here] - (diag_ref[:, here] * x - 0.5 * beside)
        resid_ref[:, here] = resid
        rb_ref[:, here] = resid.astype(jnp.bfloat16)
    project(scale, low_ref, rb_ref[...], (first_ref, second_ref), mine_ref, other_ref)


def stacked(value):
    half = value.shape[1] // 2
    return jnp.concatenate([value[:, :half], value[:, half:]], axis=0)


def unstacked(value):
    half = value.shape[0] // 2
    return jnp.concatenate([value[:half], value[half:]], axis=1)


def spread_kernel(mine_ref, other_ref, out_ref):
    total = mine_ref[...] + other_ref[...]
    for d in range(out_ref.shape[0]):
        out_ref[d] = total


def total_kernel(parts_ref, *out_refs):
    total = parts_ref[0]
    for d in range(1, parts_ref.shape[0]):
        total = total + parts_ref[d]
    out_refs[0][...] = stacked(total).astype(jnp.bfloat16)
    if len(out_refs) > 1:
        out_refs[1][...] = total


def pack_kernel(splits, *refs):
    pieces, outs = refs[: sum(splits)], refs[sum(splits) :]
    for count, out_ref in zip(splits, outs):
        at = 0
        for ref in pieces[:count]:
            rows = ref.shape[0]
            out_ref[at : at + rows] = ref[...]
            at += rows
        pieces = pieces[count:]


def packed(splits, *refs):
    *refs, sem = refs
    pieces, outs = refs[: sum(splits)], refs[sum(splits) :]
    moves = []
    for count, out_ref in zip(splits, outs):
        at = 0
        for ref in pieces[:count]:
            rows = ref.shape[0]
            moves.append(pltpu.make_async_copy(ref, out_ref.at[pl.ds(at, rows)], sem.at[len(moves)]))
            at += rows
        pieces = pieces[count:]
    return moves


def update_kernel(scale, tile, has_x, last, root, splits, low_ref, mine_ref, other_ref, resid_ref, diag_ref, *refs):
    refs = list(refs)
    x_ref = refs.pop(0) if has_x else None
    move_ref = None if has_x else refs.pop(0)
    psi_ref = refs.pop(0) if last else None
    if has_x:
        first_ref, second_ref, *outs = refs
    else:
        *refs, x_out, x_b_out, first_ref, second_ref, sem = refs
        outs = [x_out, x_b_out]
    low = core_mask(low_ref, 2 * mine_ref.shape[1])
    mine = unstacked(mine_ref[...].astype(jnp.float32))
    other = unstacked(other_ref[...].astype(jnp.float32))
    coeff = jnp.concatenate([jnp.where(low, mine, other), jnp.where(low, other, mine)], axis=0)
    coeff = coeff.astype(jnp.bfloat16)
    if not has_x:
        coeff = jnp.dot(coeff, move_ref[...], preferred_element_type=jnp.float32).astype(jnp.bfloat16)
        run(packed(splits, *refs, first_ref, second_ref, sem))
    cells = resid_ref.shape[1]
    for at in range(0, cells, tile):
        here = slice(at, at + tile)
        corr = 0.0
        start = 0
        for ref in (first_ref, second_ref):
            rows = ref.shape[0]
            some = coeff[:, start : start + rows]
            corr = corr + jnp.dot(some, ref[:, here], preferred_element_type=jnp.float32)
            start += rows
        x = (resid_ref[:, here] - corr * scale) / diag_ref[:, here]
        if has_x:
            x = x + x_ref[:, here]
        if last:
            half = x.shape[0] // 2
            low = core_mask(low_ref, tile)
            outs[0][:, here] = jnp.where(low, x[:half], x[half:])
            outs[1][:, here] = jnp.where(low, x[half:], x[:half])
            raw = jnp.sum(x * psi_ref[:, here].astype(jnp.float32), axis=0, keepdims=True) / root
            rows, wide = outs[2].shape[2:]
            for k in range(tile // wide):
                row = raw[:, k * wide : (k + 1) * wide]
                spot = at // wide + k
                outs[2][spot // rows, :, spot % rows, :] = jnp.broadcast_to(row, (outs[2].shape[1], wide))
        else:
            outs[0][:, here] = x
            outs[1][:, here] = x.astype(jnp.bfloat16)


def table_kernel(plan_ref, coeff_ref, out_ref, rows_ref):
    rows_ref[...] = coeff_ref[...].T
    share = 16
    for j in range(out_ref.shape[0] // share):
        at = pl.multiple_of(plan_ref[TABLE + j] * share, share)
        out_ref[j * share : (j + 1) * share] = rows_ref[pl.ds(at, share)]


def finish_kernel(weights_ref, pick_ref, terms_ref, out_ref):
    def product(one, two):
        return lax.dot_general(
            one, two, (((1,), (0,)), ((), ())),
            precision=lax.Precision.HIGHEST, preferred_element_type=jnp.float32,
        )

    for k in range(terms_ref.shape[1]):
        out_ref[:, k, :] = product(product(weights_ref[...], terms_ref[:, k, :]), pick_ref[...])


def call(kernel, out_shape, in_specs=None, out_specs=None, scratch=()):
    specs = {}
    if in_specs is not None:
        specs["in_specs"] = in_specs
    if out_specs is not None:
        specs["out_specs"] = out_specs
    return pl.pallas_call(
        kernel,
        out_shape=out_shape,
        scratch_shapes=scratch,
        compiler_params=pltpu.CompilerParams(vmem_limit_bytes=VMEM_LIMIT),
        **specs,
    )


def per_device(rhs, potential, eigen_table, win_index, occupied, block_ids, psi_win, smoother):
    local_orbs, planes, rows_y, rows_z = rhs.shape
    n_dom = lax.axis_size("dom")
    n_orb = lax.axis_size("orb")
    cells = rows_y * rows_z
    wide = 2 * local_orbs
    width = local_orbs * n_orb
    scale = 1.0 / math.sqrt(planes * n_dom * rows_y * rows_z)
    n_occ = eigen_table.shape[0]
    per_dev, blk_rows = occupied.shape[:2]
    nproj = block_ids.shape[0]
    chips = n_orb // 2
    ring = chips // 2
    share = blk_rows // chips
    n_rows = nproj * blk_rows
    o = lax.axis_index("orb")
    core = o % 2
    low = core == 0
    groups = [[2 * k + c for k in range(chips)] for c in range(2)]

    def chip_perm(target):
        return [(2 * k + c, 2 * target(k) + c) for k in range(chips) for c in range(2)]

    swap_core = [(i, i ^ 1) for i in range(n_orb)]
    swap_x = chip_perm(lambda k: (k + ring) % chips)
    up_y = chip_perm(lambda k: k // ring * ring + (k + 1) % ring)
    down_y = chip_perm(lambda k: k // ring * ring + (k - 1) % ring)

    def permute(value, pairs):
        return lax.ppermute(value, "orb", pairs)

    def pair(own, other):
        return jnp.concatenate([jnp.where(low, own, other), jnp.where(low, other, own)], axis=0)

    low_mask = jnp.broadcast_to(jnp.where(low, 1.0, 0.0), (local_orbs, 128))
    four = (pltpu.SemaphoreType.DMA((4,)),)

    plane_shape = shape((blk_rows, rows_y, rows_z), jnp.bfloat16)
    piece_shape = shape((2 * share, rows_y, rows_z), jnp.bfloat16)
    plan, same, offer = call(
        functools.partial(offer_kernel, per_dev, n_orb),
        (shape((TABLE + nproj * chips,), jnp.int32), shape((1,), jnp.int32), plane_shape),
        [SMEM, SMEM, ANY],
        (SMEM, SMEM, VMEM),
        four,
    )(block_ids, o.astype(jnp.int32).reshape(1), occupied)
    offer = permute(offer, swap_core)

    flat_field = shape((local_orbs, cells))
    field_shape = shape((wide, cells))
    rhs_mine, rhs_other = call(fields_kernel, (flat_field, flat_field))(low_mask, rhs)
    rhs_wide, rhs_b = call(pair_kernel, (field_shape, shape((wide, cells), jnp.bfloat16)))(
        low_mask, rhs_mine, permute(rhs_other, swap_core)
    )
    rhs_own = jnp.concatenate([rhs_b, permute(rhs_b, swap_x)], axis=0)
    offer, rhs_own = lax.optimization_barrier((offer, rhs_own))

    offer = call(pick_kernel, plane_shape, [SMEM, ANY, VMEM], VMEM, four)(plan, occupied, offer)
    fixed = call(fixed_kernel, plane_shape, [SMEM, ANY], VMEM, four)(plan, occupied)
    fixed = permute(fixed, [(0, 1), (n_orb - 1, n_orb - 2)])
    offer, fixed = lax.optimization_barrier((offer, fixed))
    pieces = call(
        functools.partial(pieces_kernel, n_orb),
        [piece_shape] * ring,
        [SMEM, ANY, VMEM],
        [VMEM] * ring,
        (pltpu.SemaphoreType.DMA((ring,)),),
    )(plan, occupied, fixed)

    got = [pieces[0]]
    for s in range(1, ring):
        pairs = [(c, 2 * s + c) for c in range(2)]
        pairs += [(n_orb - 2 + c, 2 * (ring + (ring - 1 + s) % ring) + c) for c in range(2)]
        got.append(permute(pieces[s], pairs))
    rhs_up, rhs_down = permute(rhs_own, up_y), permute(rhs_own, down_y)
    rhs_up, rhs_down, *got = lax.optimization_barrier((rhs_up, rhs_down, *got))
    rhs_far_up, rhs_far_down = permute(rhs_up[:wide], up_y), permute(rhs_down[wide:], down_y)
    fixed = call(share_kernel, piece_shape, [SMEM] + [VMEM] * ring, VMEM)(plan, *got)

    def scatter(value):
        value = value.reshape(chips, share, rows_y, rows_z)
        return lax.all_to_all(value, "orb", 0, 0, axis_index_groups=groups, tiled=True)

    def take(value, owner):
        return lax.dynamic_index_in_dim(value, owner, 0, keepdims=False)

    def apart(plan, occupied):
        return jnp.zeros((share, rows_y, rows_z), jnp.bfloat16)

    def together(plan, occupied):
        def plane_of(slot, plane):
            dims = (1, blk_rows, 1, rows_y, rows_z)
            return lax.dynamic_slice(occupied, (slot, 0, plane, 0, 0), dims).reshape(plane_shape.shape)

        mid = plan[MID + 1]
        other = permute(plane_of(mid % per_dev, 1 - core), swap_core)
        here = (mid // per_dev) % 2 == core
        again = scatter(jnp.where(here, plane_of(mid % per_dev, core), other))
        return take(again, plan[CHIP + 1])

    offered = scatter(offer)
    second = lax.cond(same[0] == 1, together, apart, plan, occupied)
    mids = call(
        take_kernel, shape((2 * share, rows_y, rows_z), jnp.bfloat16), [SMEM, VMEM, VMEM], VMEM
    )(plan, offered, second)

    xs = fixed.reshape(2 * share, cells)
    ys = mids.reshape(2 * share, cells)
    xs, ys = lax.optimization_barrier((xs, ys))
    xs_x = permute(xs, swap_x)
    ys_up = permute(ys, up_y)
    ys_down = permute(ys, down_y)
    own_rows = 4 * share
    half_shape = shape((local_orbs, n_rows))
    spread_shape = shape((n_dom, local_orbs, n_rows))
    rhs_places = ((0, 0), (ring - 1, 0), (1, 0), (2, 0), (2, 1))
    parts = call(
        functools.partial(shares_kernel, scale, rhs_places),
        shape((n_orb, local_orbs, 128)),
        [SMEM] + [VMEM] * 7,
    )(plan, rhs_own, rhs_up, rhs_down, rhs_far_up, rhs_far_down, xs, ys)
    parts = lax.all_to_all(parts, "orb", 0, 0, tiled=True)
    xs_x, ys_up, ys_down, parts = lax.optimization_barrier((xs_x, ys_up, ys_down, parts))
    own, line = call(
        functools.partial(pack_kernel, (2, 3)),
        (shape((4 * share, cells), jnp.bfloat16), shape((6 * share, cells), jnp.bfloat16)),
    )(xs, xs_x, ys, ys_up, ys_down)
    line_x = permute(line, swap_x)
    above = permute(own, up_y)
    below = permute(own, down_y)
    far_up = permute(ys_up[:share], up_y)
    far_down = permute(ys_down[share:], down_y)
    first_parts = lax.all_to_all(
        call(spread_shares_kernel, spread_shape)(parts), "dom", 0, 0, tiled=True
    )
    line_x, above, below, far_up, far_down, first_parts = lax.optimization_barrier(
        (line_x, above, below, far_up, far_down, first_parts)
    )
    far_up_x, far_down_x = permute(far_up, swap_x), permute(far_down, swap_x)
    own_up = permute(above[: 2 * share], up_y)
    own_down = permute(below[2 * share :], down_y)
    pieces = [own, below, above, own_up, own_down]
    pieces += [line, line_x, far_up, far_down, far_up_x, far_down_x]
    blocks_shape = [shape((n_rows // 2, cells), jnp.bfloat16)] * 2

    picks = win_index[:, None] == jnp.arange(n_occ, dtype=jnp.int32)[None, :]
    eps = jnp.sum(jnp.where(picks, eigen_table[None, :], 0.0), axis=1)[:, None]
    eps = pair(eps, permute(eps, swap_core))
    plane_pot = lax.dynamic_index_in_dim(potential, core, 0, keepdims=True).reshape(1, cells)
    diag = 3.0 + plane_pot - eps
    psi_mine, psi_other = call(fields_kernel, (flat_field, flat_field))(
        low_mask, psi_win.astype(jnp.float32)
    )
    psi_wide = call(pair_kernel, field_shape)(
        low_mask, psi_mine, permute(psi_other.astype(jnp.bfloat16), swap_core).astype(jnp.float32)
    )
    flat_shape = (wide, n_rows // 2)

    def total(parts, outs):
        coeff_b, *coeff = call(total_kernel, outs)(parts)
        return coeff, coeff_b, permute(coeff_b, swap_core)

    row = jnp.arange(n_rows)
    within = row % (2 * share)
    down = jnp.array([0, 0, 1, 1, 3, 3, 2, 2, 0, 3, 1, 0, 3, 1, 2, 2])
    side = jnp.array([0, 1, 0, 1, 0, 1, 0, 1, 0, 0, 0, 1, 1, 1, 0, 1])
    chip = o // 2
    chip_from = (chip // ring + side) % 2 * ring + (chip % ring + down) % ring
    at = chip_from * own_rows + jnp.where(jnp.arange(16) < 8, 0, 2 * share)
    at = jnp.repeat(at, 2 * share) + within
    move = (row[:, None] == at[None, :]).astype(jnp.bfloat16)

    across = []
    for d in range(n_dom - 1):
        for k in range(chips):
            left, right = d * n_orb + 2 * k + 1, (d + 1) * n_orb + 2 * k
            across += [(left, right), (right, left)]

    x = None
    for step in range(ITERS):
        final = step == ITERS - 1
        sums = [shape(flat_shape, jnp.bfloat16)] + ([half_shape] if final else [])
        if step == 0:
            resid, parts = rhs_wide, first_parts
        else:
            sib = permute(x, swap_core)
            off = lax.ppermute(x_b, ("dom", "orb"), across)
            resid, mine, other = call(
                functools.partial(resid_kernel, scale, rows_z),
                (field_shape, half_shape, half_shape),
                scratch=(pltpu.VMEM((wide, cells), jnp.bfloat16),),
            )(low_mask, x, sib, off, rhs_wide, diag, *blocks)
            spread = call(spread_kernel, spread_shape)(mine, permute(other, swap_core))
            parts = lax.all_to_all(spread, "dom", 0, 0, tiled=True)
        coeff, coeff_b, coeff_o = total(parts, sums)
        extra = ([x] if step else [move]) + ([psi_wide] if final else [])
        outs = [field_shape, shape((wide, cells), jnp.bfloat16)]
        if final:
            outs = [shape((local_orbs, cells))] * 2 + [shape((n_dom, n_orb, rows_y // n_dom, rows_z))]
        if step == 0:
            outs, blocks = outs + blocks_shape, pieces
            specs = [VMEM] * 6 + [HBM] * len(pieces), [VMEM] * 4
            sems = (pltpu.SemaphoreType.DMA((len(pieces),)),)
        else:
            specs, sems = (None, None), ()
        x, x_b, *rest = call(
            functools.partial(update_kernel, scale, 512, step > 0, final, math.sqrt(width), (5, 6)),
            outs,
            *specs,
            sems,
        )(low_mask, coeff_b, coeff_o, resid, diag, *extra, *blocks)
        if step == 0:
            blocks = rest
    other, raw = x_b, rest[0]

    weights = jnp.broadcast_to(
        smoother.reshape(2 * n_dom, n_dom, 1, 2), (2 * n_dom, n_dom, chips, 2)
    ).reshape(2 * n_dom, n_dom * n_orb)
    terms = lax.all_to_all(
        raw.reshape((n_dom * n_orb,) + raw.shape[2:]), ("dom", "orb"), 0, 0, tiled=True
    )
    z_part = rows_z // n_orb
    z_mine = o * z_part + jnp.arange(z_part)[None, :]
    pick = (jnp.arange(rows_z)[:, None] == z_mine).astype(jnp.float32)
    gradient = call(finish_kernel, shape((2 * n_dom, rows_y // n_dom, z_part)))(weights, pick, terms)

    other = permute(other, swap_core)
    solution = jnp.stack([jnp.where(low, x, other), jnp.where(low, other, x)], axis=1)
    solution = solution.reshape(rhs.shape)

    coeff, raw = lax.optimization_barrier((coeff[0], raw))
    correlations = call(
        table_kernel,
        shape((n_rows, local_orbs)),
        [SMEM, VMEM],
        scratch=(pltpu.VMEM((n_rows, local_orbs), jnp.float32),),
    )(plan, coeff).reshape(nproj, blk_rows, local_orbs)
    return (solution, correlations, gradient)


def solution(mesh):
    return jax.shard_map(
        per_device,
        mesh=mesh,
        in_specs=(
            P("orb", "dom", None, None),
            P("dom", None, None),
            P(),
            P("orb"),
            P("orb", None, "dom", None, None),
            P(),
            P("orb", "dom", None, None),
            P(),
        ),
        out_specs=(P("orb", "dom", None, None), P(None, None, "orb"), P(None, "dom", "orb")),
        check_vma=False,
    )
```

```python
import functools
import math

import jax
import jax.numpy as jnp
from jax import lax
from jax.experimental import pallas as pl
from jax.experimental.pallas import tpu as pltpu
from jax.sharding import PartitionSpec as P

ITERS = 3
VMEM_LIMIT = 16 * 1024 * 1024
NT = (((1,), (1,)), ((), ()))
SMEM = pl.BlockSpec(memory_space=pltpu.SMEM)
ANY = pl.BlockSpec(memory_space=pl.ANY)
VMEM = pl.BlockSpec(memory_space=pltpu.VMEM)
HBM = pl.BlockSpec(memory_space=pltpu.HBM)

MID, CHIP, SAME, SLOT, CORE, DEV, TABLE = 0, 2, 4, 5, 6, 7, 8


def shape(dims, dtype=jnp.float32):
    return jax.ShapeDtypeStruct(dims, dtype)


def plan(per_dev, n_orb, ids_ref, dev_ref, out_ref):
    nproj = ids_ref.shape[0]
    chips = n_orb // 2
    ring = chips // 2
    last = per_dev * n_orb - 1
    dev = dev_ref[0]
    chip = dev // 2
    seen = jnp.int32(0)
    mids = [jnp.int32(0)] * (nproj - 2)
    order = []
    for j in range(nproj):
        block = ids_ref[j]
        middle = jnp.logical_and(block != 0, block != last)
        for k in range(nproj - 2):
            mids[k] = jnp.where(jnp.logical_and(middle, seen == k), block, mids[k])
        order.append(jnp.where(block == 0, 0, jnp.where(block == last, 1, 2 + seen)))
        seen = seen + jnp.where(middle, 1, 0)
    owners = [mid // (2 * per_dev) for mid in mids]
    for k in range(nproj - 2):
        out_ref[MID + k] = mids[k]
        out_ref[CHIP + k] = owners[k]
    out_ref[SAME] = jnp.where(owners[0] == owners[1], 1, 0)
    offer = jnp.where(chip == owners[0], mids[0], mids[1])
    out_ref[SLOT] = offer % per_dev
    out_ref[CORE] = (offer // per_dev) % 2
    out_ref[DEV] = dev
    y, x = chip % ring, chip // ring
    for j in range(nproj):
        for q in range(chips):
            down = (q // 2 + ring - y) % ring
            first = jnp.where(down == 1, 4, jnp.where(down == 3, 8, jnp.where(down == 2, 12, 0)))
            first = first + (order[j] + x) % 2 * 2 + q % 2
            down = (q % ring + ring - y) % ring
            side = (q // ring + x) % 2
            second = jnp.where(down == 1, 4, jnp.where(down == 3, 2, 0)) + side * 6
            second = 14 + jnp.where(down == 2, 12 + side * 2, second) + order[j]
            out_ref[TABLE + j * chips + q] = jnp.where(order[j] < 2, first, second)


def copies(source, target, sem):
    parts = sem.shape[0]
    rows = target.shape[0] // parts
    return [
        pltpu.make_async_copy(source(k * rows, rows), target.at[pl.ds(k * rows, rows)], sem.at[k])
        for k in range(parts)
    ]


def run(started):
    for copy in started:
        copy.start()
    for copy in started:
        copy.wait()


def offer_kernel(per_dev, n_orb, ids_ref, dev_ref, occupied_ref, plan_ref, same_ref, offer_ref, sem):
    plan(per_dev, n_orb, ids_ref, dev_ref, plan_ref)
    same_ref[0] = plan_ref[SAME]
    core = plan_ref[DEV] % 2
    run(copies(lambda at, n: occupied_ref.at[plan_ref[SLOT], pl.ds(at, n), 1 - core], offer_ref, sem))


def fixed_kernel(n_orb, plan_ref, occupied_ref, fixed_ref, sem):
    dev = plan_ref[DEV]
    core = dev % 2
    slot = core * (occupied_ref.shape[0] - 1)

    @pl.when(jnp.logical_or(dev == 0, dev == n_orb - 1))
    def _():
        run(copies(lambda at, n: occupied_ref.at[slot, pl.ds(at, n), 1 - core], fixed_ref, sem))


def pick_kernel(plan_ref, occupied_ref, offer_ref, out_ref, sem):
    core = plan_ref[DEV] % 2

    @pl.when(plan_ref[CORE] == core)
    def _():
        run(copies(lambda at, n: occupied_ref.at[plan_ref[SLOT], pl.ds(at, n), core], out_ref, sem))

    @pl.when(plan_ref[CORE] != core)
    def _():
        step = 16

        @pl.loop(0, out_ref.shape[0] // step)
        def _(k):
            here = pl.ds(k * step, step)
            out_ref[here] = offer_ref[here]


def pieces_kernel(n_orb, plan_ref, occupied_ref, fixed_ref, *refs):
    *piece_refs, sem = refs
    dev = plan_ref[DEV]
    core = dev % 2
    last = occupied_ref.shape[0] - 1
    ring = len(piece_refs)
    rows = piece_refs[0].shape[0]

    def at(s):
        return pl.ds(jnp.where(dev < n_orb // 2, s, (ring - 1 + s) % ring) * rows, rows)

    @pl.when(jnp.logical_or(dev == 0, dev == n_orb - 1))
    def _():
        run([
            pltpu.make_async_copy(occupied_ref.at[core * last, at(s), core], ref, sem.at[s])
            for s, ref in enumerate(piece_refs)
        ])

    @pl.when(jnp.logical_or(dev == 1, dev == n_orb - 2))
    def _():
        for s, ref in enumerate(piece_refs):
            ref[...] = fixed_ref[at(s)]


def share_kernel(plan_ref, *refs):
    *piece_refs, out_ref = refs
    ring = len(piece_refs)
    chip = plan_ref[DEV] // 2
    y, x = chip % ring, chip // ring
    away = (y + x) % ring
    for s, ref in enumerate(piece_refs):

        @pl.when(away == s)
        def _(ref=ref):
            out_ref[...] = ref[...]


def core_mask(low_ref, width):
    return jnp.concatenate([low_ref[...]] * (width // low_ref.shape[1]), axis=1) > 0.5


def split(low_ref, value, mine_ref, other_ref):
    half = value.shape[0] // 2
    low = core_mask(low_ref, value.shape[1])
    first, second = value[:half], value[half:]
    mine_ref[...] = jnp.where(low, first, second)
    other_ref[...] = jnp.where(low, second, first)


def project(scale, low_ref, resid_b, block_refs, mine_ref, other_ref):
    parts = [
        lax.dot_general(resid_b, ref[...], NT, preferred_element_type=jnp.float32) for ref in block_refs
    ]
    split(low_ref, jnp.concatenate(parts, axis=1) * scale, mine_ref, other_ref)


def fields_kernel(low_ref, field_ref, mine_ref, other_ref):
    rows_y, rows_z = field_ref.shape[2:]
    low = low_ref[...] > 0.5
    for y in range(rows_y):
        first, second = field_ref[:, 0, y, :], field_ref[:, 1, y, :]
        here = slice(y * rows_z, (y + 1) * rows_z)
        mine_ref[:, here] = jnp.where(low, first, second)
        other_ref[:, here] = jnp.where(low, second, first)


def pair_kernel(low_ref, mine_ref, other_ref, out_ref, *rounded_refs):
    half = mine_ref.shape[0]
    low = core_mask(low_ref, mine_ref.shape[1])
    mine, other = mine_ref[...], other_ref[...]
    both = jnp.concatenate([jnp.where(low, mine, other), jnp.where(low, other, mine)], axis=0)
    out_ref[...] = both
    for ref in rounded_refs:
        ref[...] = both.astype(jnp.bfloat16)


def take_kernel(plan_ref, offered_ref, second_ref, out_ref):
    rows = offered_ref.shape[1]
    out_ref[:rows] = offered_ref[plan_ref[CHIP]]

    @pl.when(plan_ref[SAME] == 1)
    def _():
        out_ref[rows:] = second_ref[...]

    @pl.when(plan_ref[SAME] != 1)
    def _():
        out_ref[rows:] = offered_ref[plan_ref[CHIP + 1]]


def shares_kernel(scale, places, plan_ref, *refs):
    *field_refs, ends_ref, mids_ref, out_ref = refs
    devices, orbs, lanes = out_ref.shape
    ring = devices // 4
    chip = plan_ref[DEV] // 2
    y, x = chip % ring, chip // ring
    spare = lanes - ends_ref.shape[0] - mids_ref.shape[0]
    for place, field_ref in zip(places, field_refs):
        field = field_ref[...]
        got = [
            lax.dot_general(field, ref[...], NT, preferred_element_type=jnp.float32)
            for ref in (ends_ref, mids_ref)
        ]
        rows = jnp.concatenate(got + [jnp.zeros((field.shape[0], spare), jnp.float32)], axis=1) * scale
        for k, (down, side) in enumerate(place):
            to = 2 * ((x + side) % 2 * ring + (y + down) % ring)
            at = k * 2 * orbs
            out_ref[pl.ds(to, 1)] = rows[at : at + orbs][None]
            out_ref[pl.ds(to + 1, 1)] = rows[at + orbs : at + 2 * orbs][None]


def spread_shares_kernel(parts_ref, out_ref):
    rows = out_ref.shape[2] * 2 // parts_ref.shape[0]
    total = jnp.concatenate(
        [(parts_ref[k] + parts_ref[k + 1])[:, :rows] for k in range(0, parts_ref.shape[0], 2)], axis=1
    )
    for d in range(out_ref.shape[0]):
        out_ref[d] = total


def resid_kernel(
    scale, row, low_ref, x_ref, sib_ref, off_ref, rhs_ref, diag_ref, first_ref, second_ref,
    resid_ref, mine_ref, other_ref, rb_ref,
):
    cells = x_ref.shape[1]
    lane = lax.broadcasted_iota(jnp.int32, (x_ref.shape[0], row), 1)
    for at in range(0, cells, row):
        here = slice(at, at + row)
        x = x_ref[:, here]
        beside = sib_ref[:, here] + off_ref[:, here].astype(jnp.float32)
        if at > 0:
            beside = beside + x_ref[:, at - row : at]
        if at + row < cells:
            beside = beside + x_ref[:, at + row : at + 2 * row]
        beside = beside + jnp.where(lane == 0, 0.0, pltpu.roll(x, 1, 1))
        beside = beside + jnp.where(lane == row - 1, 0.0, pltpu.roll(x, row - 1, 1))
        resid = rhs_ref[:, here] - (diag_ref[:, here] * x - 0.5 * beside)
        resid_ref[:, here] = resid
        rb_ref[:, here] = resid.astype(jnp.bfloat16)
    project(scale, low_ref, rb_ref[...], (first_ref, second_ref), mine_ref, other_ref)


def stacked(value):
    half = value.shape[1] // 2
    return jnp.concatenate([value[:, :half], value[:, half:]], axis=0)


def unstacked(value):
    half = value.shape[0] // 2
    return jnp.concatenate([value[:half], value[half:]], axis=1)


def spread_kernel(mine_ref, other_ref, out_ref):
    total = mine_ref[...] + other_ref[...]
    for d in range(out_ref.shape[0]):
        out_ref[d] = total


def total_kernel(parts_ref, *out_refs):
    total = parts_ref[0]
    for d in range(1, parts_ref.shape[0]):
        total = total + parts_ref[d]
    out_refs[0][...] = stacked(total).astype(jnp.bfloat16)
    if len(out_refs) > 1:
        out_refs[1][...] = total


def pack_kernel(splits, *refs):
    pieces, outs = refs[: sum(splits)], refs[sum(splits) :]
    for count, out_ref in zip(splits, outs):
        at = 0
        for ref in pieces[:count]:
            rows = ref.shape[0]
            out_ref[at : at + rows] = ref[...]
            at += rows
        pieces = pieces[count:]


def packed(splits, *refs):
    *refs, sem = refs
    pieces, outs = refs[: sum(splits)], refs[sum(splits) :]
    moves = []
    for count, out_ref in zip(splits, outs):
        at = 0
        for ref in pieces[:count]:
            rows = ref.shape[0]
            moves.append(pltpu.make_async_copy(ref, out_ref.at[pl.ds(at, rows)], sem.at[len(moves)]))
            at += rows
        pieces = pieces[count:]
    return moves


def update_kernel(scale, tile, has_x, last, root, splits, low_ref, mine_ref, other_ref, resid_ref, diag_ref, *refs):
    refs = list(refs)
    x_ref = refs.pop(0) if has_x else None
    move_ref = None if has_x else refs.pop(0)
    psi_ref = refs.pop(0) if last else None
    if has_x:
        first_ref, second_ref, *outs = refs
    else:
        *refs, x_out, x_b_out, first_ref, second_ref, sem = refs
        outs = [x_out, x_b_out]
    low = core_mask(low_ref, 2 * mine_ref.shape[1])
    mine = unstacked(mine_ref[...].astype(jnp.float32))
    other = unstacked(other_ref[...].astype(jnp.float32))
    coeff = jnp.concatenate([jnp.where(low, mine, other), jnp.where(low, other, mine)], axis=0)
    coeff = coeff.astype(jnp.bfloat16)
    if not has_x:
        coeff = jnp.dot(coeff, move_ref[...], preferred_element_type=jnp.float32).astype(jnp.bfloat16)
        run(packed(splits, *refs, first_ref, second_ref, sem))
    cells = resid_ref.shape[1]
    for at in range(0, cells, tile):
        here = slice(at, at + tile)
        corr = 0.0
        start = 0
        for ref in (first_ref, second_ref):
            rows = ref.shape[0]
            some = coeff[:, start : start + rows]
            corr = corr + jnp.dot(some, ref[:, here], preferred_element_type=jnp.float32)
            start += rows
        x = (resid_ref[:, here] - corr * scale) / diag_ref[:, here]
        if has_x:
            x = x + x_ref[:, here]
        if last:
            half = x.shape[0] // 2
            low = core_mask(low_ref, tile)
            outs[0][:, here] = jnp.where(low, x[:half], x[half:])
            outs[1][:, here] = jnp.where(low, x[half:], x[:half])
            raw = jnp.sum(x * psi_ref[:, here].astype(jnp.float32), axis=0, keepdims=True) / root
            rows, wide = outs[2].shape[2:]
            for k in range(tile // wide):
                row = raw[:, k * wide : (k + 1) * wide]
                spot = at // wide + k
                outs[2][spot // rows, :, spot % rows, :] = jnp.broadcast_to(row, (outs[2].shape[1], wide))
        else:
            outs[0][:, here] = x
            outs[1][:, here] = x.astype(jnp.bfloat16)


def table_kernel(plan_ref, coeff_ref, out_ref, rows_ref):
    rows_ref[...] = coeff_ref[...].T
    share = 16
    for j in range(out_ref.shape[0] // share):
        at = pl.multiple_of(plan_ref[TABLE + j] * share, share)
        out_ref[j * share : (j + 1) * share] = rows_ref[pl.ds(at, share)]


def finish_kernel(weights_ref, pick_ref, terms_ref, out_ref):
    def product(one, two, dims):
        return lax.dot_general(
            one, two, (dims, ((), ())),
            precision=lax.Precision.HIGHEST, preferred_element_type=jnp.float32,
        )

    for k in range(terms_ref.shape[1]):
        mine = product(pick_ref[...], terms_ref[:, k, :], ((1,), (1,)))
        out_ref[k] = product(mine, weights_ref[...], ((1,), (1,)))


def call(kernel, out_shape, in_specs=None, out_specs=None, scratch=()):
    specs = {}
    if in_specs is not None:
        specs["in_specs"] = in_specs
    if out_specs is not None:
        specs["out_specs"] = out_specs
    return pl.pallas_call(
        kernel,
        out_shape=out_shape,
        scratch_shapes=scratch,
        compiler_params=pltpu.CompilerParams(vmem_limit_bytes=VMEM_LIMIT),
        **specs,
    )


def per_device(rhs, potential, eigen_table, win_index, occupied, block_ids, psi_win, smoother):
    local_orbs, planes, rows_y, rows_z = rhs.shape
    n_dom = lax.axis_size("dom")
    n_orb = lax.axis_size("orb")
    cells = rows_y * rows_z
    wide = 2 * local_orbs
    width = local_orbs * n_orb
    scale = 1.0 / math.sqrt(planes * n_dom * rows_y * rows_z)
    n_occ = eigen_table.shape[0]
    per_dev, blk_rows = occupied.shape[:2]
    nproj = block_ids.shape[0]
    chips = n_orb // 2
    ring = chips // 2
    share = blk_rows // chips
    n_rows = nproj * blk_rows
    o = lax.axis_index("orb")
    core = o % 2
    low = core == 0
    groups = [[2 * k + c for k in range(chips)] for c in range(2)]

    def chip_perm(target):
        return [(2 * k + c, 2 * target(k) + c) for k in range(chips) for c in range(2)]

    swap_core = [(i, i ^ 1) for i in range(n_orb)]
    swap_x = chip_perm(lambda k: (k + ring) % chips)
    up_y = chip_perm(lambda k: k // ring * ring + (k + 1) % ring)
    down_y = chip_perm(lambda k: k // ring * ring + (k - 1) % ring)

    def permute(value, pairs):
        return lax.ppermute(value, "orb", pairs)

    def pair(own, other):
        return jnp.concatenate([jnp.where(low, own, other), jnp.where(low, other, own)], axis=0)

    low_mask = jnp.broadcast_to(jnp.where(low, 1.0, 0.0), (local_orbs, 128))
    four = (pltpu.SemaphoreType.DMA((4,)),)

    plane_shape = shape((blk_rows, rows_y, rows_z), jnp.bfloat16)
    piece_shape = shape((2 * share, rows_y, rows_z), jnp.bfloat16)
    plan, same, offer = call(
        functools.partial(offer_kernel, per_dev, n_orb),
        (shape((TABLE + nproj * chips,), jnp.int32), shape((1,), jnp.int32), plane_shape),
        [SMEM, SMEM, ANY],
        (SMEM, SMEM, VMEM),
        four,
    )(block_ids, o.astype(jnp.int32).reshape(1), occupied)
    offer = permute(offer, swap_core)

    flat_field = shape((local_orbs, cells))
    field_shape = shape((wide, cells))
    rhs_mine, rhs_other = call(fields_kernel, (flat_field, flat_field))(low_mask, rhs)
    rhs_wide, rhs_b = call(pair_kernel, (field_shape, shape((wide, cells), jnp.bfloat16)))(
        low_mask, rhs_mine, permute(rhs_other, swap_core)
    )
    rhs_up, rhs_down = permute(rhs_b, up_y), permute(rhs_b, down_y)

    offer = call(pick_kernel, plane_shape, [SMEM, ANY, VMEM], VMEM, four)(plan, occupied, offer)
    fixed = call(functools.partial(fixed_kernel, n_orb), plane_shape, [SMEM, ANY], VMEM, four)(plan, occupied)
    fixed = permute(fixed, [(0, 1), (n_orb - 1, n_orb - 2)])
    offer, fixed = lax.optimization_barrier((offer, fixed))
    pieces = call(
        functools.partial(pieces_kernel, n_orb),
        [piece_shape] * ring,
        [SMEM, ANY, VMEM],
        [VMEM] * ring,
        (pltpu.SemaphoreType.DMA((ring,)),),
    )(plan, occupied, fixed)

    got = [pieces[0]]
    for s in range(1, ring):
        pairs = [(c, 2 * s + c) for c in range(2)]
        pairs += [(n_orb - 2 + c, 2 * (ring + (ring - 1 + s) % ring) + c) for c in range(2)]
        got.append(permute(pieces[s], pairs))
    rhs_up, rhs_down, got[1] = lax.optimization_barrier((rhs_up, rhs_down, got[1]))
    rhs_line = jnp.concatenate([rhs_b, rhs_up, rhs_down], axis=0)
    rhs_line_x = permute(rhs_line, swap_x)
    rhs_far = jnp.concatenate(
        [permute(rhs_up[:local_orbs], up_y), permute(rhs_down[local_orbs:], down_y)], axis=0
    )
    rhs_far_x = permute(rhs_far, swap_x)
    fixed = call(share_kernel, piece_shape, [SMEM] + [VMEM] * ring, VMEM)(plan, *got)

    def scatter(value):
        value = value.reshape(chips, share, rows_y, rows_z)
        return lax.all_to_all(value, "orb", 0, 0, axis_index_groups=groups, tiled=True)

    def take(value, owner):
        return lax.dynamic_index_in_dim(value, owner, 0, keepdims=False)

    def apart(plan, occupied):
        return jnp.zeros((share, rows_y, rows_z), jnp.bfloat16)

    def together(plan, occupied):
        def plane_of(slot, plane):
            dims = (1, blk_rows, 1, rows_y, rows_z)
            return lax.dynamic_slice(occupied, (slot, 0, plane, 0, 0), dims).reshape(plane_shape.shape)

        mid = plan[MID + 1]
        other = permute(plane_of(mid % per_dev, 1 - core), swap_core)
        here = (mid // per_dev) % 2 == core
        again = scatter(jnp.where(here, plane_of(mid % per_dev, core), other))
        return take(again, plan[CHIP + 1])

    offered = scatter(offer)
    second = lax.cond(same[0] == 1, together, apart, plan, occupied)
    mids = call(
        take_kernel, shape((2 * share, rows_y, rows_z), jnp.bfloat16), [SMEM, VMEM, VMEM], VMEM
    )(plan, offered, second)

    xs = fixed.reshape(2 * share, cells)
    ys = mids.reshape(2 * share, cells)
    xs, ys = lax.optimization_barrier((xs, ys))
    xs_x = permute(xs, swap_x)
    ys_up = permute(ys, up_y)
    ys_down = permute(ys, down_y)
    own_rows = 4 * share
    half_shape = shape((local_orbs, n_rows))
    spread_shape = shape((n_dom, local_orbs, n_rows))
    rhs_places = [[(0, k), (ring - 1, k), (1, k)] for k in range(2)] + [[(2, k)] for k in range(2)]
    parts = call(
        functools.partial(shares_kernel, scale, rhs_places),
        shape((n_orb, local_orbs, 128)),
        [SMEM] + [VMEM] * 6,
    )(plan, rhs_line, rhs_line_x, rhs_far, rhs_far_x, xs, ys)
    parts = lax.all_to_all(parts, "orb", 0, 0, tiled=True)
    xs_x, ys_up, ys_down = lax.optimization_barrier((xs_x, ys_up, ys_down))
    own, line = call(
        functools.partial(pack_kernel, (2, 3)),
        (shape((4 * share, cells), jnp.bfloat16), shape((6 * share, cells), jnp.bfloat16)),
    )(xs, xs_x, ys, ys_up, ys_down)
    line_x = permute(line, swap_x)
    above = permute(own, up_y)
    below = permute(own, down_y)
    far_up = permute(ys_up[:share], up_y)
    far_down = permute(ys_down[share:], down_y)
    parts, _ = lax.optimization_barrier((parts, line))
    first_parts = lax.all_to_all(
        call(spread_shares_kernel, spread_shape)(parts), "dom", 0, 0, tiled=True
    )
    line_x, above, below, far_up, far_down = lax.optimization_barrier(
        (line_x, above, below, far_up, far_down)
    )
    far_up_x, far_down_x = permute(far_up, swap_x), permute(far_down, swap_x)
    own_up = permute(above[: 2 * share], up_y)
    own_down = permute(below[2 * share :], down_y)
    pieces = [own, below, above, own_up, own_down]
    pieces += [line, line_x, far_up, far_down, far_up_x, far_down_x]
    blocks_shape = [shape((n_rows // 2, cells), jnp.bfloat16)] * 2

    picks = win_index[:, None] == jnp.arange(n_occ, dtype=jnp.int32)[None, :]
    eps = jnp.sum(jnp.where(picks, eigen_table[None, :], 0.0), axis=1)[:, None]
    eps = pair(eps, permute(eps, swap_core))
    plane_pot = lax.dynamic_index_in_dim(potential, core, 0, keepdims=True).reshape(1, cells)
    diag = 3.0 + plane_pot - eps
    psi_mine, psi_other = call(fields_kernel, (flat_field, flat_field))(
        low_mask, psi_win.astype(jnp.float32)
    )
    psi_wide = call(pair_kernel, field_shape)(
        low_mask, psi_mine, permute(psi_other.astype(jnp.bfloat16), swap_core).astype(jnp.float32)
    )
    flat_shape = (wide, n_rows // 2)

    def total(parts, outs):
        coeff_b, *coeff = call(total_kernel, outs)(parts)
        return coeff, coeff_b, permute(coeff_b, swap_core)

    row = jnp.arange(n_rows)
    within = row % (2 * share)
    down = jnp.array([0, 0, 1, 1, 3, 3, 2, 2, 0, 3, 1, 0, 3, 1, 2, 2])
    side = jnp.array([0, 1, 0, 1, 0, 1, 0, 1, 0, 0, 0, 1, 1, 1, 0, 1])
    chip = o // 2
    chip_from = (chip // ring + side) % 2 * ring + (chip % ring + down) % ring
    at = chip_from * own_rows + jnp.where(jnp.arange(16) < 8, 0, 2 * share)
    at = jnp.repeat(at, 2 * share) + within
    move = (row[:, None] == at[None, :]).astype(jnp.bfloat16)

    across = []
    for d in range(n_dom - 1):
        for k in range(chips):
            left, right = d * n_orb + 2 * k + 1, (d + 1) * n_orb + 2 * k
            across += [(left, right), (right, left)]

    x = None
    for step in range(ITERS):
        final = step == ITERS - 1
        sums = [shape(flat_shape, jnp.bfloat16)] + ([half_shape] if final else [])
        if step == 0:
            resid, parts = rhs_wide, first_parts
        else:
            sib = permute(x, swap_core)
            off = lax.ppermute(x_b, ("dom", "orb"), across)
            resid, mine, other = call(
                functools.partial(resid_kernel, scale, rows_z),
                (field_shape, half_shape, half_shape),
                scratch=(pltpu.VMEM((wide, cells), jnp.bfloat16),),
            )(low_mask, x, sib, off, rhs_wide, diag, *blocks)
            spread = call(spread_kernel, spread_shape)(mine, permute(other, swap_core))
            parts = lax.all_to_all(spread, "dom", 0, 0, tiled=True)
        coeff, coeff_b, coeff_o = total(parts, sums)
        extra = ([x] if step else [move]) + ([psi_wide] if final else [])
        outs = [field_shape, shape((wide, cells), jnp.bfloat16)]
        if final:
            outs = [shape((local_orbs, cells))] * 2 + [shape((n_dom, n_orb, rows_y // n_dom, rows_z))]
        if step == 0:
            outs, blocks = outs + blocks_shape, pieces
            specs = [VMEM] * 6 + [HBM] * len(pieces), [VMEM] * 4
            sems = (pltpu.SemaphoreType.DMA((len(pieces),)),)
        else:
            specs, sems = (None, None), ()
        x, x_b, *rest = call(
            functools.partial(update_kernel, scale, 512, step > 0, final, math.sqrt(width), (5, 6)),
            outs,
            *specs,
            sems,
        )(low_mask, coeff_b, coeff_o, resid, diag, *extra, *blocks)
        if step == 0:
            blocks = rest
    other, raw = x_b, rest[0]

    weights = jnp.broadcast_to(
        smoother.reshape(2 * n_dom, n_dom, 1, 2), (2 * n_dom, n_dom, chips, 2)
    ).reshape(2 * n_dom, n_dom * n_orb)
    terms = lax.all_to_all(
        raw.reshape((n_dom * n_orb,) + raw.shape[2:]), ("dom", "orb"), 0, 0, tiled=True
    )
    z_part = rows_z // n_orb
    z_mine = o * z_part + jnp.arange(z_part)[:, None]
    pick = (jnp.arange(rows_z)[None, :] == z_mine).astype(jnp.float32)
    gradient = call(finish_kernel, shape((rows_y // n_dom, z_part, 2 * n_dom)))(weights, pick, terms)
    gradient = jnp.transpose(gradient, (2, 0, 1))

    other = permute(other, swap_core)
    solution = jnp.stack([jnp.where(low, x, other), jnp.where(low, other, x)], axis=1)
    solution = solution.reshape(rhs.shape)

    coeff, raw = lax.optimization_barrier((coeff[0], raw))
    correlations = call(
        table_kernel,
        shape((n_rows, local_orbs)),
        [SMEM, VMEM],
        scratch=(pltpu.VMEM((n_rows, local_orbs), jnp.float32),),
    )(plan, coeff).reshape(nproj, blk_rows, local_orbs)
    return (solution, correlations, gradient)


def solution(mesh):
    return jax.shard_map(
        per_device,
        mesh=mesh,
        in_specs=(
            P("orb", "dom", None, None),
            P("dom", None, None),
            P(),
            P("orb"),
            P("orb", None, "dom", None, None),
            P(),
            P("orb", "dom", None, None),
            P(),
        ),
        out_specs=(P("orb", "dom", None, None), P(None, None, "orb"), P(None, "dom", "orb")),
        check_vma=False,
    )
```

```python
import functools
import math

import jax
import jax.numpy as jnp
from jax import lax
from jax.experimental import pallas as pl
from jax.experimental.pallas import tpu as pltpu
from jax.sharding import PartitionSpec as P

ITERS = 3
VMEM_LIMIT = 16 * 1024 * 1024
NT = (((1,), (1,)), ((), ()))
SMEM = pl.BlockSpec(memory_space=pltpu.SMEM)
ANY = pl.BlockSpec(memory_space=pl.ANY)
VMEM = pl.BlockSpec(memory_space=pltpu.VMEM)
HBM = pl.BlockSpec(memory_space=pltpu.HBM)

MID, CHIP, SAME, SLOT, CORE, DEV, TABLE = 0, 2, 4, 5, 6, 7, 8


def shape(dims, dtype=jnp.float32):
    return jax.ShapeDtypeStruct(dims, dtype)


def plan(per_dev, n_orb, ids_ref, dev_ref, out_ref):
    nproj = ids_ref.shape[0]
    chips = n_orb // 2
    ring = chips // 2
    last = per_dev * n_orb - 1
    dev = dev_ref[0]
    chip = dev // 2
    seen = jnp.int32(0)
    mids = [jnp.int32(0)] * (nproj - 2)
    order = []
    for j in range(nproj):
        block = ids_ref[j]
        middle = jnp.logical_and(block != 0, block != last)
        for k in range(nproj - 2):
            mids[k] = jnp.where(jnp.logical_and(middle, seen == k), block, mids[k])
        order.append(jnp.where(block == 0, 0, jnp.where(block == last, 1, 2 + seen)))
        seen = seen + jnp.where(middle, 1, 0)
    owners = [mid // (2 * per_dev) for mid in mids]
    for k in range(nproj - 2):
        out_ref[MID + k] = mids[k]
        out_ref[CHIP + k] = owners[k]
    out_ref[SAME] = jnp.where(owners[0] == owners[1], 1, 0)
    offer = jnp.where(chip == owners[0], mids[0], mids[1])
    out_ref[SLOT] = offer % per_dev
    out_ref[CORE] = (offer // per_dev) % 2
    out_ref[DEV] = dev
    y, x = chip % ring, chip // ring
    for j in range(nproj):
        for q in range(chips):
            down = (q // 2 + ring - y) % ring
            first = jnp.where(down == 1, 4, jnp.where(down == 3, 8, jnp.where(down == 2, 12, 0)))
            first = first + (order[j] + x) % 2 * 2 + q % 2
            down = (q % ring + ring - y) % ring
            side = (q // ring + x) % 2
            second = jnp.where(down == 1, 4, jnp.where(down == 3, 2, 0)) + side * 6
            second = 14 + jnp.where(down == 2, 12 + side * 2, second) + order[j]
            out_ref[TABLE + j * chips + q] = jnp.where(order[j] < 2, first, second)


def copies(source, target, sem):
    parts = sem.shape[0]
    rows = target.shape[0] // parts
    return [
        pltpu.make_async_copy(source(k * rows, rows), target.at[pl.ds(k * rows, rows)], sem.at[k])
        for k in range(parts)
    ]


def run(started):
    for copy in started:
        copy.start()
    for copy in started:
        copy.wait()


def offer_kernel(per_dev, n_orb, ids_ref, dev_ref, occupied_ref, *refs):
    plan_ref, same_ref, offer_ref, fixed_ref, sem, fixed_sem = refs
    plan(per_dev, n_orb, ids_ref, dev_ref, plan_ref)
    same_ref[0] = plan_ref[SAME]
    dev = plan_ref[DEV]
    core = dev % 2

    def plane(slot):
        return lambda at, n: occupied_ref.at[slot, pl.ds(at, n), 1 - core]

    @pl.when(jnp.logical_or(dev == 0, dev == n_orb - 1))
    def _():
        run(copies(plane(core * (occupied_ref.shape[0] - 1)), fixed_ref, fixed_sem))

    run(copies(plane(plan_ref[SLOT]), offer_ref, sem))


def pick_kernel(plan_ref, occupied_ref, offer_ref, out_ref, sem):
    core = plan_ref[DEV] % 2

    @pl.when(plan_ref[CORE] == core)
    def _():
        run(copies(lambda at, n: occupied_ref.at[plan_ref[SLOT], pl.ds(at, n), core], out_ref, sem))

    @pl.when(plan_ref[CORE] != core)
    def _():
        step = 16

        @pl.loop(0, out_ref.shape[0] // step)
        def _(k):
            here = pl.ds(k * step, step)
            out_ref[here] = offer_ref[here]


def pieces_kernel(n_orb, plan_ref, occupied_ref, fixed_ref, *refs):
    *piece_refs, sem = refs
    dev = plan_ref[DEV]
    core = dev % 2
    last = occupied_ref.shape[0] - 1
    ring = len(piece_refs)
    rows = piece_refs[0].shape[0]

    def at(s):
        return pl.ds(jnp.where(dev < n_orb // 2, s, (ring - 1 + s) % ring) * rows, rows)

    @pl.when(jnp.logical_or(dev == 0, dev == n_orb - 1))
    def _():
        run([
            pltpu.make_async_copy(occupied_ref.at[core * last, at(s), core], ref, sem.at[s])
            for s, ref in enumerate(piece_refs)
        ])

    @pl.when(jnp.logical_or(dev == 1, dev == n_orb - 2))
    def _():
        for s, ref in enumerate(piece_refs):
            ref[...] = fixed_ref[at(s)]


def share_kernel(plan_ref, *refs):
    *piece_refs, out_ref = refs
    ring = len(piece_refs)
    chip = plan_ref[DEV] // 2
    y, x = chip % ring, chip // ring
    away = (y + x) % ring
    for s, ref in enumerate(piece_refs):

        @pl.when(away == s)
        def _(ref=ref):
            out_ref[...] = ref[...]


def core_mask(low_ref, width):
    return jnp.concatenate([low_ref[...]] * (width // low_ref.shape[1]), axis=1) > 0.5


def split(low_ref, value, mine_ref, other_ref):
    half = value.shape[0] // 2
    low = core_mask(low_ref, value.shape[1])
    first, second = value[:half], value[half:]
    mine_ref[...] = jnp.where(low, first, second)
    other_ref[...] = jnp.where(low, second, first)


def project(scale, low_ref, resid_b, block_refs, mine_ref, other_ref):
    parts = [
        lax.dot_general(resid_b, ref[...], NT, preferred_element_type=jnp.float32) for ref in block_refs
    ]
    split(low_ref, jnp.concatenate(parts, axis=1) * scale, mine_ref, other_ref)


def fields_kernel(low_ref, field_ref, mine_ref, other_ref):
    rows_y, rows_z = field_ref.shape[2:]
    low = low_ref[...] > 0.5
    for y in range(rows_y):
        first, second = field_ref[:, 0, y, :], field_ref[:, 1, y, :]
        here = slice(y * rows_z, (y + 1) * rows_z)
        mine_ref[:, here] = jnp.where(low, first, second)
        other_ref[:, here] = jnp.where(low, second, first)


def pair_kernel(low_ref, mine_ref, other_ref, out_ref, *rounded_refs):
    half = mine_ref.shape[0]
    low = core_mask(low_ref, mine_ref.shape[1])
    mine, other = mine_ref[...], other_ref[...]
    both = jnp.concatenate([jnp.where(low, mine, other), jnp.where(low, other, mine)], axis=0)
    out_ref[...] = both
    for ref in rounded_refs:
        ref[...] = both.astype(jnp.bfloat16)


def take_kernel(plan_ref, offered_ref, second_ref, out_ref):
    rows = offered_ref.shape[1]
    out_ref[:rows] = offered_ref[plan_ref[CHIP]]

    @pl.when(plan_ref[SAME] == 1)
    def _():
        out_ref[rows:] = second_ref[...]

    @pl.when(plan_ref[SAME] != 1)
    def _():
        out_ref[rows:] = offered_ref[plan_ref[CHIP + 1]]


def shares_kernel(scale, places, plan_ref, *refs):
    *field_refs, ends_ref, mids_ref, out_ref = refs
    devices, orbs, lanes = out_ref.shape
    ring = devices // 4
    chip = plan_ref[DEV] // 2
    y, x = chip % ring, chip // ring
    spare = lanes - ends_ref.shape[0] - mids_ref.shape[0]
    for place, field_ref in zip(places, field_refs):
        field = field_ref[...]
        got = [
            lax.dot_general(field, ref[...], NT, preferred_element_type=jnp.float32)
            for ref in (ends_ref, mids_ref)
        ]
        rows = jnp.concatenate(got + [jnp.zeros((field.shape[0], spare), jnp.float32)], axis=1) * scale
        for k, (down, side) in enumerate(place):
            to = 2 * ((x + side) % 2 * ring + (y + down) % ring)
            at = k * 2 * orbs
            out_ref[pl.ds(to, 1)] = rows[at : at + orbs][None]
            out_ref[pl.ds(to + 1, 1)] = rows[at + orbs : at + 2 * orbs][None]


def spread_shares_kernel(parts_ref, out_ref):
    rows = out_ref.shape[2] * 2 // parts_ref.shape[0]
    total = jnp.concatenate(
        [(parts_ref[k] + parts_ref[k + 1])[:, :rows] for k in range(0, parts_ref.shape[0], 2)], axis=1
    )
    for d in range(out_ref.shape[0]):
        out_ref[d] = total


def resid_kernel(
    scale, row, low_ref, x_ref, sib_ref, off_ref, rhs_ref, diag_ref, first_ref, second_ref,
    resid_ref, mine_ref, other_ref, rb_ref,
):
    cells = x_ref.shape[1]
    lane = lax.broadcasted_iota(jnp.int32, (x_ref.shape[0], row), 1)
    for at in range(0, cells, row):
        here = slice(at, at + row)
        x = x_ref[:, here]
        beside = sib_ref[:, here] + off_ref[:, here].astype(jnp.float32)
        if at > 0:
            beside = beside + x_ref[:, at - row : at]
        if at + row < cells:
            beside = beside + x_ref[:, at + row : at + 2 * row]
        beside = beside + jnp.where(lane == 0, 0.0, pltpu.roll(x, 1, 1))
        beside = beside + jnp.where(lane == row - 1, 0.0, pltpu.roll(x, row - 1, 1))
        resid = rhs_ref[:, here] - (diag_ref[:, here] * x - 0.5 * beside)
        resid_ref[:, here] = resid
        rb_ref[:, here] = resid.astype(jnp.bfloat16)
    project(scale, low_ref, rb_ref[...], (first_ref, second_ref), mine_ref, other_ref)


def stacked(value):
    half = value.shape[1] // 2
    return jnp.concatenate([value[:, :half], value[:, half:]], axis=0)


def unstacked(value):
    half = value.shape[0] // 2
    return jnp.concatenate([value[:half], value[half:]], axis=1)


def spread_kernel(mine_ref, other_ref, out_ref):
    total = mine_ref[...] + other_ref[...]
    for d in range(out_ref.shape[0]):
        out_ref[d] = total


def total_kernel(parts_ref, *out_refs):
    total = parts_ref[0]
    for d in range(1, parts_ref.shape[0]):
        total = total + parts_ref[d]
    out_refs[0][...] = stacked(total).astype(jnp.bfloat16)
    if len(out_refs) > 1:
        out_refs[1][...] = total


def pack_kernel(splits, *refs):
    pieces, outs = refs[: sum(splits)], refs[sum(splits) :]
    for count, out_ref in zip(splits, outs):
        at = 0
        for ref in pieces[:count]:
            rows = ref.shape[0]
            out_ref[at : at + rows] = ref[...]
            at += rows
        pieces = pieces[count:]


def update_kernel(scale, tile, has_x, last, root, low_ref, mine_ref, other_ref, resid_ref, diag_ref, *refs):
    refs = list(refs)
    x_ref = refs.pop(0) if has_x else None
    move_ref = None if has_x else refs.pop(0)
    psi_ref = refs.pop(0) if last else None
    first_ref, second_ref, *outs = refs
    low = core_mask(low_ref, 2 * mine_ref.shape[1])
    mine = unstacked(mine_ref[...].astype(jnp.float32))
    other = unstacked(other_ref[...].astype(jnp.float32))
    coeff = jnp.concatenate([jnp.where(low, mine, other), jnp.where(low, other, mine)], axis=0)
    coeff = coeff.astype(jnp.bfloat16)
    if not has_x:
        coeff = jnp.dot(coeff, move_ref[...], preferred_element_type=jnp.float32).astype(jnp.bfloat16)
    cells = resid_ref.shape[1]
    for at in range(0, cells, tile):
        here = slice(at, at + tile)
        corr = 0.0
        start = 0
        for ref in (first_ref, second_ref):
            rows = ref.shape[0]
            some = coeff[:, start : start + rows]
            corr = corr + jnp.dot(some, ref[:, here], preferred_element_type=jnp.float32)
            start += rows
        x = (resid_ref[:, here] - corr * scale) / diag_ref[:, here]
        if has_x:
            x = x + x_ref[:, here]
        if last:
            half = x.shape[0] // 2
            low = core_mask(low_ref, tile)
            outs[0][:, here] = jnp.where(low, x[:half], x[half:])
            outs[1][:, here] = jnp.where(low, x[half:], x[:half])
            raw = jnp.sum(x * psi_ref[:, here].astype(jnp.float32), axis=0, keepdims=True) / root
            rows, wide = outs[2].shape[2:]
            for k in range(tile // wide):
                row = raw[:, k * wide : (k + 1) * wide]
                spot = at // wide + k
                outs[2][spot // rows, :, spot % rows, :] = jnp.broadcast_to(row, (outs[2].shape[1], wide))
        else:
            outs[0][:, here] = x
            outs[1][:, here] = x.astype(jnp.bfloat16)


def table_kernel(plan_ref, coeff_ref, out_ref, rows_ref):
    rows_ref[...] = coeff_ref[...].T
    share = 16
    for j in range(out_ref.shape[0] // share):
        at = pl.multiple_of(plan_ref[TABLE + j] * share, share)
        out_ref[j * share : (j + 1) * share] = rows_ref[pl.ds(at, share)]


def finish_kernel(weights_ref, pick_ref, terms_ref, out_ref):
    def product(one, two, dims):
        return lax.dot_general(
            one, two, (dims, ((), ())),
            precision=lax.Precision.HIGHEST, preferred_element_type=jnp.float32,
        )

    for k in range(terms_ref.shape[1]):
        mine = product(pick_ref[...], terms_ref[:, k, :], ((1,), (1,)))
        out_ref[k] = product(mine, weights_ref[...], ((1,), (1,)))


def call(kernel, out_shape, in_specs=None, out_specs=None, scratch=()):
    specs = {}
    if in_specs is not None:
        specs["in_specs"] = in_specs
    if out_specs is not None:
        specs["out_specs"] = out_specs
    return pl.pallas_call(
        kernel,
        out_shape=out_shape,
        scratch_shapes=scratch,
        compiler_params=pltpu.CompilerParams(vmem_limit_bytes=VMEM_LIMIT),
        **specs,
    )


def per_device(rhs, potential, eigen_table, win_index, occupied, block_ids, psi_win, smoother):
    local_orbs, planes, rows_y, rows_z = rhs.shape
    n_dom = lax.axis_size("dom")
    n_orb = lax.axis_size("orb")
    cells = rows_y * rows_z
    wide = 2 * local_orbs
    width = local_orbs * n_orb
    scale = 1.0 / math.sqrt(planes * n_dom * rows_y * rows_z)
    n_occ = eigen_table.shape[0]
    per_dev, blk_rows = occupied.shape[:2]
    nproj = block_ids.shape[0]
    chips = n_orb // 2
    ring = chips // 2
    share = blk_rows // chips
    n_rows = nproj * blk_rows
    o = lax.axis_index("orb")
    core = o % 2
    low = core == 0
    groups = [[2 * k + c for k in range(chips)] for c in range(2)]

    def chip_perm(target):
        return [(2 * k + c, 2 * target(k) + c) for k in range(chips) for c in range(2)]

    swap_core = [(i, i ^ 1) for i in range(n_orb)]
    swap_x = chip_perm(lambda k: (k + ring) % chips)
    up_y = chip_perm(lambda k: k // ring * ring + (k + 1) % ring)
    down_y = chip_perm(lambda k: k // ring * ring + (k - 1) % ring)

    def permute(value, pairs):
        return lax.ppermute(value, "orb", pairs)

    def pair(own, other):
        return jnp.concatenate([jnp.where(low, own, other), jnp.where(low, other, own)], axis=0)

    low_mask = jnp.broadcast_to(jnp.where(low, 1.0, 0.0), (local_orbs, 128))
    four = (pltpu.SemaphoreType.DMA((4,)),)

    plane_shape = shape((blk_rows, rows_y, rows_z), jnp.bfloat16)
    piece_shape = shape((2 * share, rows_y, rows_z), jnp.bfloat16)
    plan, same, offer, fixed = call(
        functools.partial(offer_kernel, per_dev, n_orb),
        (shape((TABLE + nproj * chips,), jnp.int32), shape((1,), jnp.int32), plane_shape, plane_shape),
        [SMEM, SMEM, ANY],
        (SMEM, SMEM, VMEM, VMEM),
        four * 2,
    )(block_ids, o.astype(jnp.int32).reshape(1), occupied)
    offer = permute(offer, swap_core)

    flat_field = shape((local_orbs, cells))
    field_shape = shape((wide, cells))
    rhs_mine, rhs_other = call(fields_kernel, (flat_field, flat_field))(low_mask, rhs)
    rhs_wide, rhs_b = call(pair_kernel, (field_shape, shape((wide, cells), jnp.bfloat16)))(
        low_mask, rhs_mine, permute(rhs_other, swap_core)
    )
    rhs_up, rhs_down = permute(rhs_b, up_y), permute(rhs_b, down_y)

    offer = call(pick_kernel, plane_shape, [SMEM, ANY, VMEM], VMEM, four)(plan, occupied, offer)
    fixed = permute(fixed, [(0, 1), (n_orb - 1, n_orb - 2)])
    offer, fixed = lax.optimization_barrier((offer, fixed))
    pieces = call(
        functools.partial(pieces_kernel, n_orb),
        [piece_shape] * ring,
        [SMEM, ANY, VMEM],
        [VMEM] * ring,
        (pltpu.SemaphoreType.DMA((ring,)),),
    )(plan, occupied, fixed)

    got = [pieces[0]]
    for s in range(1, ring):
        pairs = [(c, 2 * s + c) for c in range(2)]
        pairs += [(n_orb - 2 + c, 2 * (ring + (ring - 1 + s) % ring) + c) for c in range(2)]
        got.append(permute(pieces[s], pairs))
    rhs_up, rhs_down, got[1] = lax.optimization_barrier((rhs_up, rhs_down, got[1]))
    rhs_line = jnp.concatenate([rhs_b, rhs_up, rhs_down], axis=0)
    rhs_line_x = permute(rhs_line, swap_x)
    rhs_far = jnp.concatenate(
        [permute(rhs_up[:local_orbs], up_y), permute(rhs_down[local_orbs:], down_y)], axis=0
    )
    rhs_far_x = permute(rhs_far, swap_x)
    fixed = call(share_kernel, piece_shape, [SMEM] + [VMEM] * ring, VMEM)(plan, *got)

    def scatter(value):
        value = value.reshape(chips, share, rows_y, rows_z)
        return lax.all_to_all(value, "orb", 0, 0, axis_index_groups=groups, tiled=True)

    def take(value, owner):
        return lax.dynamic_index_in_dim(value, owner, 0, keepdims=False)

    def apart(plan, occupied):
        return jnp.zeros((share, rows_y, rows_z), jnp.bfloat16)

    def together(plan, occupied):
        def plane_of(slot, plane):
            dims = (1, blk_rows, 1, rows_y, rows_z)
            return lax.dynamic_slice(occupied, (slot, 0, plane, 0, 0), dims).reshape(plane_shape.shape)

        mid = plan[MID + 1]
        other = permute(plane_of(mid % per_dev, 1 - core), swap_core)
        here = (mid // per_dev) % 2 == core
        again = scatter(jnp.where(here, plane_of(mid % per_dev, core), other))
        return take(again, plan[CHIP + 1])

    offered = scatter(offer)
    second = lax.cond(same[0] == 1, together, apart, plan, occupied)
    mids = call(
        take_kernel, shape((2 * share, rows_y, rows_z), jnp.bfloat16), [SMEM, VMEM, VMEM], VMEM
    )(plan, offered, second)

    xs = fixed.reshape(2 * share, cells)
    ys = mids.reshape(2 * share, cells)
    xs, ys = lax.optimization_barrier((xs, ys))
    xs_x = permute(xs, swap_x)
    ys_x = permute(ys, swap_x)
    ys_up = permute(ys, up_y)
    ys_down = permute(ys, down_y)
    own_rows = 4 * share
    half_shape = shape((local_orbs, n_rows))
    spread_shape = shape((n_dom, local_orbs, n_rows))
    rhs_places = [[(0, k), (ring - 1, k), (1, k)] for k in range(2)] + [[(2, k)] for k in range(2)]
    parts = call(
        functools.partial(shares_kernel, scale, rhs_places),
        shape((n_orb, local_orbs, 128)),
        [SMEM] + [VMEM] * 6,
    )(plan, rhs_line, rhs_line_x, rhs_far, rhs_far_x, xs, ys)
    parts = lax.all_to_all(parts, "orb", 0, 0, tiled=True)
    xs_x, ys_x, ys_up, ys_down = lax.optimization_barrier((xs_x, ys_x, ys_up, ys_down))
    own, line = call(
        functools.partial(pack_kernel, (2, 2)), (shape((4 * share, cells), jnp.bfloat16),) * 2
    )(xs, xs_x, ys_up, ys_down)
    line_x = permute(line, swap_x)
    above = permute(own, up_y)
    below = permute(own, down_y)
    far_up = permute(ys_up[:share], up_y)
    far_down = permute(ys_down[share:], down_y)
    parts, _ = lax.optimization_barrier((parts, line))
    first_parts = lax.all_to_all(
        call(spread_shares_kernel, spread_shape)(parts), "dom", 0, 0, tiled=True
    )
    line_x, above, below, far_up, far_down = lax.optimization_barrier(
        (line_x, above, below, far_up, far_down)
    )
    far_up_x, far_down_x = permute(far_up, swap_x), permute(far_down, swap_x)
    own_up = permute(above[: 2 * share], up_y)
    own_down = permute(below[2 * share :], down_y)
    block_shape = shape((n_rows // 2, cells), jnp.bfloat16)
    blocks = call(functools.partial(pack_kernel, (3, 5)), [block_shape] * 2)(
        own, below, above, ys, line, ys_x, line_x, jnp.concatenate([far_up, far_down], axis=0)
    )
    blocks = list(blocks)
    late = ((own_up, own_down), (far_up_x, far_down_x))
    for k, pair_of in enumerate(late):
        at = n_rows // 2 - sum(piece.shape[0] for piece in pair_of)
        for piece in pair_of:
            blocks[k] = lax.dynamic_update_slice(blocks[k], piece, (at, 0))
            at += piece.shape[0]

    picks = win_index[:, None] == jnp.arange(n_occ, dtype=jnp.int32)[None, :]
    eps = jnp.sum(jnp.where(picks, eigen_table[None, :], 0.0), axis=1)[:, None]
    eps = pair(eps, permute(eps, swap_core))
    plane_pot = lax.dynamic_index_in_dim(potential, core, 0, keepdims=True).reshape(1, cells)
    diag = 3.0 + plane_pot - eps
    psi_mine, psi_other = call(fields_kernel, (flat_field, flat_field))(
        low_mask, psi_win.astype(jnp.float32)
    )
    psi_wide = call(pair_kernel, field_shape)(
        low_mask, psi_mine, permute(psi_other.astype(jnp.bfloat16), swap_core).astype(jnp.float32)
    )
    flat_shape = (wide, n_rows // 2)

    def total(parts, outs):
        coeff_b, *coeff = call(total_kernel, outs)(parts)
        return coeff, coeff_b, permute(coeff_b, swap_core)

    row = jnp.arange(n_rows)
    within = row % (2 * share)
    down = jnp.array([0, 0, 1, 1, 3, 3, 2, 2, 0, 3, 1, 0, 3, 1, 2, 2])
    side = jnp.array([0, 1, 0, 1, 0, 1, 0, 1, 0, 0, 0, 1, 1, 1, 0, 1])
    chip = o // 2
    chip_from = (chip // ring + side) % 2 * ring + (chip % ring + down) % ring
    at = chip_from * own_rows + jnp.where(jnp.arange(16) < 8, 0, 2 * share)
    at = jnp.repeat(at, 2 * share) + within
    move = (row[:, None] == at[None, :]).astype(jnp.bfloat16)

    across = []
    for d in range(n_dom - 1):
        for k in range(chips):
            left, right = d * n_orb + 2 * k + 1, (d + 1) * n_orb + 2 * k
            across += [(left, right), (right, left)]

    x = None
    for step in range(ITERS):
        final = step == ITERS - 1
        sums = [shape(flat_shape, jnp.bfloat16)] + ([half_shape] if final else [])
        if step == 0:
            resid, parts = rhs_wide, first_parts
        else:
            sib = permute(x, swap_core)
            off = lax.ppermute(x_b, ("dom", "orb"), across)
            resid, mine, other = call(
                functools.partial(resid_kernel, scale, rows_z),
                (field_shape, half_shape, half_shape),
                scratch=(pltpu.VMEM((wide, cells), jnp.bfloat16),),
            )(low_mask, x, sib, off, rhs_wide, diag, *blocks)
            spread = call(spread_kernel, spread_shape)(mine, permute(other, swap_core))
            parts = lax.all_to_all(spread, "dom", 0, 0, tiled=True)
        coeff, coeff_b, coeff_o = total(parts, sums)
        extra = ([x] if step else [move]) + ([psi_wide] if final else [])
        outs = [field_shape, shape((wide, cells), jnp.bfloat16)]
        if final:
            outs = [shape((local_orbs, cells))] * 2 + [shape((n_dom, n_orb, rows_y // n_dom, rows_z))]
        x, x_b, *rest = call(
            functools.partial(update_kernel, scale, 512, step > 0, final, math.sqrt(width)), outs
        )(low_mask, coeff_b, coeff_o, resid, diag, *extra, *blocks)
    other, raw = x_b, rest[0]

    weights = jnp.broadcast_to(
        smoother.reshape(2 * n_dom, n_dom, 1, 2), (2 * n_dom, n_dom, chips, 2)
    ).reshape(2 * n_dom, n_dom * n_orb)
    terms = lax.all_to_all(
        raw.reshape((n_dom * n_orb,) + raw.shape[2:]), ("dom", "orb"), 0, 0, tiled=True
    )
    z_part = rows_z // n_orb
    z_mine = o * z_part + jnp.arange(z_part)[:, None]
    pick = (jnp.arange(rows_z)[None, :] == z_mine).astype(jnp.float32)
    gradient = call(finish_kernel, shape((rows_y // n_dom, z_part, 2 * n_dom)))(weights, pick, terms)
    gradient = jnp.transpose(gradient, (2, 0, 1))

    other = permute(other, swap_core)
    solution = jnp.stack([jnp.where(low, x, other), jnp.where(low, other, x)], axis=1)
    solution = solution.reshape(rhs.shape)

    coeff, raw = lax.optimization_barrier((coeff[0], raw))
    correlations = call(
        table_kernel,
        shape((n_rows, local_orbs)),
        [SMEM, VMEM],
        scratch=(pltpu.VMEM((n_rows, local_orbs), jnp.float32),),
    )(plan, coeff).reshape(nproj, blk_rows, local_orbs)
    return (solution, correlations, gradient)


def solution(mesh):
    return jax.shard_map(
        per_device,
        mesh=mesh,
        in_specs=(
            P("orb", "dom", None, None),
            P("dom", None, None),
            P(),
            P("orb"),
            P("orb", None, "dom", None, None),
            P(),
            P("orb", "dom", None, None),
            P(),
        ),
        out_specs=(P("orb", "dom", None, None), P(None, None, "orb"), P(None, "dom", "orb")),
        check_vma=False,
    )
```

```python
import functools
import math

import jax
import jax.numpy as jnp
from jax import lax
from jax.experimental import pallas as pl
from jax.experimental.pallas import tpu as pltpu
from jax.sharding import PartitionSpec as P

ITERS = 3
VMEM_LIMIT = 16 * 1024 * 1024
NT = (((1,), (1,)), ((), ()))
SMEM = pl.BlockSpec(memory_space=pltpu.SMEM)
ANY = pl.BlockSpec(memory_space=pl.ANY)
VMEM = pl.BlockSpec(memory_space=pltpu.VMEM)
HBM = pl.BlockSpec(memory_space=pltpu.HBM)

MID, CHIP, SAME, SLOT, CORE, DEV, TABLE = 0, 2, 4, 5, 6, 7, 8


def shape(dims, dtype=jnp.float32):
    return jax.ShapeDtypeStruct(dims, dtype)


def plan(per_dev, n_orb, ids_ref, dev_ref, out_ref):
    nproj = ids_ref.shape[0]
    chips = n_orb // 2
    ring = chips // 2
    last = per_dev * n_orb - 1
    dev = dev_ref[0]
    chip = dev // 2
    seen = jnp.int32(0)
    mids = [jnp.int32(0)] * (nproj - 2)
    order = []
    for j in range(nproj):
        block = ids_ref[j]
        middle = jnp.logical_and(block != 0, block != last)
        for k in range(nproj - 2):
            mids[k] = jnp.where(jnp.logical_and(middle, seen == k), block, mids[k])
        order.append(jnp.where(block == 0, 0, jnp.where(block == last, 1, 2 + seen)))
        seen = seen + jnp.where(middle, 1, 0)
    owners = [mid // (2 * per_dev) for mid in mids]
    for k in range(nproj - 2):
        out_ref[MID + k] = mids[k]
        out_ref[CHIP + k] = owners[k]
    out_ref[SAME] = jnp.where(owners[0] == owners[1], 1, 0)
    offer = jnp.where(chip == owners[0], mids[0], mids[1])
    out_ref[SLOT] = offer % per_dev
    out_ref[CORE] = (offer // per_dev) % 2
    out_ref[DEV] = dev
    y, x = chip % ring, chip // ring
    for j in range(nproj):
        for q in range(chips):
            down = (q // 2 + ring - y) % ring
            first = jnp.where(down == 1, 4, jnp.where(down == 3, 8, jnp.where(down == 2, 12, 0)))
            first = first + (order[j] + x) % 2 * 2 + q % 2
            down = (q % ring + ring - y) % ring
            side = (q // ring + x) % 2
            second = jnp.where(down == 1, 4, jnp.where(down == 3, 2, 0)) + side * 6
            second = 14 + jnp.where(down == 2, 12 + side * 2, second) + order[j]
            out_ref[TABLE + j * chips + q] = jnp.where(order[j] < 2, first, second)


def copies(source, target, sem):
    parts = sem.shape[0]
    rows = target.shape[0] // parts
    return [
        pltpu.make_async_copy(source(k * rows, rows), target.at[pl.ds(k * rows, rows)], sem.at[k])
        for k in range(parts)
    ]


def run(started):
    for copy in started:
        copy.start()
    for copy in started:
        copy.wait()


def offer_kernel(per_dev, n_orb, ids_ref, dev_ref, occupied_ref, plan_ref, same_ref, offer_ref, sem):
    plan(per_dev, n_orb, ids_ref, dev_ref, plan_ref)
    same_ref[0] = plan_ref[SAME]
    core = plan_ref[DEV] % 2
    run(copies(lambda at, n: occupied_ref.at[plan_ref[SLOT], pl.ds(at, n), 1 - core], offer_ref, sem))


def fixed_kernel(n_orb, plan_ref, occupied_ref, fixed_ref, sem):
    dev = plan_ref[DEV]
    core = dev % 2
    slot = core * (occupied_ref.shape[0] - 1)

    @pl.when(jnp.logical_or(dev == 0, dev == n_orb - 1))
    def _():
        run(copies(lambda at, n: occupied_ref.at[slot, pl.ds(at, n), 1 - core], fixed_ref, sem))


def pick_kernel(plan_ref, occupied_ref, offer_ref, out_ref, sem):
    core = plan_ref[DEV] % 2

    @pl.when(plan_ref[CORE] == core)
    def _():
        run(copies(lambda at, n: occupied_ref.at[plan_ref[SLOT], pl.ds(at, n), core], out_ref, sem))

    @pl.when(plan_ref[CORE] != core)
    def _():
        step = 16

        @pl.loop(0, out_ref.shape[0] // step)
        def _(k):
            here = pl.ds(k * step, step)
            out_ref[here] = offer_ref[here]


def pieces_kernel(n_orb, plan_ref, occupied_ref, fixed_ref, *refs):
    *piece_refs, sem = refs
    dev = plan_ref[DEV]
    core = dev % 2
    last = occupied_ref.shape[0] - 1
    ring = len(piece_refs)
    rows = piece_refs[0].shape[0]

    def at(s):
        return pl.ds(jnp.where(dev < n_orb // 2, s, (ring - 1 + s) % ring) * rows, rows)

    @pl.when(jnp.logical_or(dev == 0, dev == n_orb - 1))
    def _():
        run([
            pltpu.make_async_copy(occupied_ref.at[core * last, at(s), core], ref, sem.at[s])
            for s, ref in enumerate(piece_refs)
        ])

    @pl.when(jnp.logical_or(dev == 1, dev == n_orb - 2))
    def _():
        for s, ref in enumerate(piece_refs):
            ref[...] = fixed_ref[at(s)]


def share_kernel(plan_ref, *refs):
    *piece_refs, out_ref = refs
    ring = len(piece_refs)
    chip = plan_ref[DEV] // 2
    y, x = chip % ring, chip // ring
    away = (y + x) % ring
    for s, ref in enumerate(piece_refs):

        @pl.when(away == s)
        def _(ref=ref):
            out_ref[...] = ref[...]


def core_mask(low_ref, width):
    return jnp.concatenate([low_ref[...]] * (width // low_ref.shape[1]), axis=1) > 0.5


def split(low_ref, value, mine_ref, other_ref):
    half = value.shape[0] // 2
    low = core_mask(low_ref, value.shape[1])
    first, second = value[:half], value[half:]
    mine_ref[...] = jnp.where(low, first, second)
    other_ref[...] = jnp.where(low, second, first)


def project(scale, low_ref, resid_b, block_refs, mine_ref, other_ref):
    parts = [
        lax.dot_general(resid_b, ref[...], NT, preferred_element_type=jnp.float32) for ref in block_refs
    ]
    split(low_ref, jnp.concatenate(parts, axis=1) * scale, mine_ref, other_ref)


def fields_kernel(low_ref, field_ref, mine_ref, other_ref):
    rows_y, rows_z = field_ref.shape[2:]
    low = low_ref[...] > 0.5
    for y in range(rows_y):
        first, second = field_ref[:, 0, y, :], field_ref[:, 1, y, :]
        here = slice(y * rows_z, (y + 1) * rows_z)
        mine_ref[:, here] = jnp.where(low, first, second)
        other_ref[:, here] = jnp.where(low, second, first)


def pair_kernel(low_ref, mine_ref, other_ref, out_ref, *rounded_refs):
    half = mine_ref.shape[0]
    low = core_mask(low_ref, mine_ref.shape[1])
    mine, other = mine_ref[...], other_ref[...]
    both = jnp.concatenate([jnp.where(low, mine, other), jnp.where(low, other, mine)], axis=0)
    out_ref[...] = both
    for ref in rounded_refs:
        ref[...] = both.astype(jnp.bfloat16)


def take_kernel(plan_ref, offered_ref, second_ref, out_ref):
    rows = offered_ref.shape[1]
    out_ref[:rows] = offered_ref[plan_ref[CHIP]]

    @pl.when(plan_ref[SAME] == 1)
    def _():
        out_ref[rows:] = second_ref[...]

    @pl.when(plan_ref[SAME] != 1)
    def _():
        out_ref[rows:] = offered_ref[plan_ref[CHIP + 1]]


def shares_kernel(scale, places, plan_ref, *refs):
    *field_refs, ends_ref, mids_ref, out_ref = refs
    devices, orbs, lanes = out_ref.shape
    ring = devices // 4
    chip = plan_ref[DEV] // 2
    y, x = chip % ring, chip // ring
    spare = lanes - ends_ref.shape[0] - mids_ref.shape[0]
    for place, field_ref in zip(places, field_refs):
        field = field_ref[...]
        got = [
            lax.dot_general(field, ref[...], NT, preferred_element_type=jnp.float32)
            for ref in (ends_ref, mids_ref)
        ]
        rows = jnp.concatenate(got + [jnp.zeros((field.shape[0], spare), jnp.float32)], axis=1) * scale
        for k, (down, side) in enumerate(place):
            to = 2 * ((x + side) % 2 * ring + (y + down) % ring)
            at = k * 2 * orbs
            out_ref[pl.ds(to, 1)] = rows[at : at + orbs][None]
            out_ref[pl.ds(to + 1, 1)] = rows[at + orbs : at + 2 * orbs][None]


def spread_shares_kernel(parts_ref, out_ref):
    rows = out_ref.shape[2] * 2 // parts_ref.shape[0]
    total = jnp.concatenate(
        [(parts_ref[k] + parts_ref[k + 1])[:, :rows] for k in range(0, parts_ref.shape[0], 2)], axis=1
    )
    for d in range(out_ref.shape[0]):
        out_ref[d] = total


def resid_kernel(
    scale, row, low_ref, x_ref, sib_ref, off_ref, rhs_ref, diag_ref, first_ref, second_ref,
    resid_ref, mine_ref, other_ref, rb_ref,
):
    cells = x_ref.shape[1]
    lane = lax.broadcasted_iota(jnp.int32, (x_ref.shape[0], row), 1)
    for at in range(0, cells, row):
        here = slice(at, at + row)
        x = x_ref[:, here]
        beside = sib_ref[:, here] + off_ref[:, here].astype(jnp.float32)
        if at > 0:
            beside = beside + x_ref[:, at - row : at]
        if at + row < cells:
            beside = beside + x_ref[:, at + row : at + 2 * row]
        beside = beside + jnp.where(lane == 0, 0.0, pltpu.roll(x, 1, 1))
        beside = beside + jnp.where(lane == row - 1, 0.0, pltpu.roll(x, row - 1, 1))
        resid = rhs_ref[:, here] - (diag_ref[:, here] * x - 0.5 * beside)
        resid_ref[:, here] = resid
        rb_ref[:, here] = resid.astype(jnp.bfloat16)
    project(scale, low_ref, rb_ref[...], (first_ref, second_ref), mine_ref, other_ref)


def stacked(value):
    half = value.shape[1] // 2
    return jnp.concatenate([value[:, :half], value[:, half:]], axis=0)


def unstacked(value):
    half = value.shape[0] // 2
    return jnp.concatenate([value[:half], value[half:]], axis=1)


def spread_kernel(mine_ref, other_ref, out_ref):
    total = mine_ref[...] + other_ref[...]
    for d in range(out_ref.shape[0]):
        out_ref[d] = total


def total_kernel(parts_ref, *out_refs):
    total = parts_ref[0]
    for d in range(1, parts_ref.shape[0]):
        total = total + parts_ref[d]
    out_refs[0][...] = stacked(total).astype(jnp.bfloat16)
    if len(out_refs) > 1:
        out_refs[1][...] = total


def pack_kernel(splits, *refs):
    pieces, outs = refs[: sum(splits)], refs[sum(splits) :]
    for count, out_ref in zip(splits, outs):
        at = 0
        for ref in pieces[:count]:
            rows = ref.shape[0]
            out_ref[at : at + rows] = ref[...]
            at += rows
        pieces = pieces[count:]


def update_kernel(scale, tile, has_x, last, root, low_ref, mine_ref, other_ref, resid_ref, diag_ref, *refs):
    refs = list(refs)
    x_ref = refs.pop(0) if has_x else None
    move_ref = None if has_x else refs.pop(0)
    psi_ref = refs.pop(0) if last else None
    first_ref, second_ref, *outs = refs
    low = core_mask(low_ref, 2 * mine_ref.shape[1])
    mine = unstacked(mine_ref[...].astype(jnp.float32))
    other = unstacked(other_ref[...].astype(jnp.float32))
    coeff = jnp.concatenate([jnp.where(low, mine, other), jnp.where(low, other, mine)], axis=0)
    coeff = coeff.astype(jnp.bfloat16)
    if not has_x:
        coeff = jnp.dot(coeff, move_ref[...], preferred_element_type=jnp.float32).astype(jnp.bfloat16)
    cells = resid_ref.shape[1]
    for at in range(0, cells, tile):
        here = slice(at, at + tile)
        corr = 0.0
        start = 0
        for ref in (first_ref, second_ref):
            rows = ref.shape[0]
            some = coeff[:, start : start + rows]
            corr = corr + jnp.dot(some, ref[:, here], preferred_element_type=jnp.float32)
            start += rows
        x = (resid_ref[:, here] - corr * scale) / diag_ref[:, here]
        if has_x:
            x = x + x_ref[:, here]
        if last:
            half = x.shape[0] // 2
            low = core_mask(low_ref, tile)
            outs[0][:, here] = jnp.where(low, x[:half], x[half:])
            outs[1][:, here] = jnp.where(low, x[half:], x[:half])
            raw = jnp.sum(x * psi_ref[:, here].astype(jnp.float32), axis=0, keepdims=True) / root
            rows, wide = outs[2].shape[2:]
            for k in range(tile // wide):
                row = raw[:, k * wide : (k + 1) * wide]
                spot = at // wide + k
                outs[2][spot // rows, :, spot % rows, :] = jnp.broadcast_to(row, (outs[2].shape[1], wide))
        else:
            outs[0][:, here] = x
            outs[1][:, here] = x.astype(jnp.bfloat16)


def table_kernel(plan_ref, coeff_ref, out_ref, rows_ref):
    rows_ref[...] = coeff_ref[...].T
    share = 16
    for j in range(out_ref.shape[0] // share):
        at = pl.multiple_of(plan_ref[TABLE + j] * share, share)
        out_ref[j * share : (j + 1) * share] = rows_ref[pl.ds(at, share)]


def finish_kernel(weights_ref, pick_ref, terms_ref, out_ref):
    def product(one, two, dims):
        return lax.dot_general(
            one, two, (dims, ((), ())),
            precision=lax.Precision.HIGHEST, preferred_element_type=jnp.float32,
        )

    for k in range(terms_ref.shape[1]):
        mine = product(pick_ref[...], terms_ref[:, k, :], ((1,), (1,)))
        out_ref[k] = product(mine, weights_ref[...], ((1,), (1,)))


def call(kernel, out_shape, in_specs=None, out_specs=None, scratch=()):
    specs = {}
    if in_specs is not None:
        specs["in_specs"] = in_specs
    if out_specs is not None:
        specs["out_specs"] = out_specs
    return pl.pallas_call(
        kernel,
        out_shape=out_shape,
        scratch_shapes=scratch,
        compiler_params=pltpu.CompilerParams(vmem_limit_bytes=VMEM_LIMIT),
        **specs,
    )


def per_device(rhs, potential, eigen_table, win_index, occupied, block_ids, psi_win, smoother):
    local_orbs, planes, rows_y, rows_z = rhs.shape
    n_dom = lax.axis_size("dom")
    n_orb = lax.axis_size("orb")
    cells = rows_y * rows_z
    wide = 2 * local_orbs
    width = local_orbs * n_orb
    scale = 1.0 / math.sqrt(planes * n_dom * rows_y * rows_z)
    n_occ = eigen_table.shape[0]
    per_dev, blk_rows = occupied.shape[:2]
    nproj = block_ids.shape[0]
    chips = n_orb // 2
    ring = chips // 2
    share = blk_rows // chips
    n_rows = nproj * blk_rows
    o = lax.axis_index("orb")
    core = o % 2
    low = core == 0
    groups = [[2 * k + c for k in range(chips)] for c in range(2)]

    def chip_perm(target):
        return [(2 * k + c, 2 * target(k) + c) for k in range(chips) for c in range(2)]

    swap_core = [(i, i ^ 1) for i in range(n_orb)]
    swap_x = chip_perm(lambda k: (k + ring) % chips)
    up_y = chip_perm(lambda k: k // ring * ring + (k + 1) % ring)
    down_y = chip_perm(lambda k: k // ring * ring + (k - 1) % ring)

    def permute(value, pairs):
        return lax.ppermute(value, "orb", pairs)

    def pair(own, other):
        return jnp.concatenate([jnp.where(low, own, other), jnp.where(low, other, own)], axis=0)

    low_mask = jnp.broadcast_to(jnp.where(low, 1.0, 0.0), (local_orbs, 128))
    four = (pltpu.SemaphoreType.DMA((4,)),)

    plane_shape = shape((blk_rows, rows_y, rows_z), jnp.bfloat16)
    piece_shape = shape((2 * share, rows_y, rows_z), jnp.bfloat16)
    plan, same, offer = call(
        functools.partial(offer_kernel, per_dev, n_orb),
        (shape((TABLE + nproj * chips,), jnp.int32), shape((1,), jnp.int32), plane_shape),
        [SMEM, SMEM, ANY],
        (SMEM, SMEM, VMEM),
        four,
    )(block_ids, o.astype(jnp.int32).reshape(1), occupied)
    offer = permute(offer, swap_core)

    flat_field = shape((local_orbs, cells))
    field_shape = shape((wide, cells))
    rhs_mine, rhs_other = call(fields_kernel, (flat_field, flat_field))(low_mask, rhs)
    rhs_wide, rhs_b = call(pair_kernel, (field_shape, shape((wide, cells), jnp.bfloat16)))(
        low_mask, rhs_mine, permute(rhs_other, swap_core)
    )
    rhs_up, rhs_down = permute(rhs_b, up_y), permute(rhs_b, down_y)

    fixed = call(functools.partial(fixed_kernel, n_orb), plane_shape, [SMEM, ANY], VMEM, four)(plan, occupied)
    fixed = permute(fixed, [(0, 1), (n_orb - 1, n_orb - 2)])
    pieces = call(
        functools.partial(pieces_kernel, n_orb),
        [piece_shape] * ring,
        [SMEM, ANY, VMEM],
        [VMEM] * ring,
        (pltpu.SemaphoreType.DMA((ring,)),),
    )(plan, occupied, fixed)
    offer, *pieces = lax.optimization_barrier((offer, *pieces))
    offer = call(pick_kernel, plane_shape, [SMEM, ANY, VMEM], VMEM, four)(plan, occupied, offer)

    got = [pieces[0]]
    for s in range(1, ring):
        pairs = [(c, 2 * s + c) for c in range(2)]
        pairs += [(n_orb - 2 + c, 2 * (ring + (ring - 1 + s) % ring) + c) for c in range(2)]
        got.append(permute(pieces[s], pairs))
    rhs_up, rhs_down, got[1] = lax.optimization_barrier((rhs_up, rhs_down, got[1]))
    rhs_line = jnp.concatenate([rhs_b, rhs_up, rhs_down], axis=0)
    rhs_line_x = permute(rhs_line, swap_x)
    rhs_far = jnp.concatenate(
        [permute(rhs_up[:local_orbs], up_y), permute(rhs_down[local_orbs:], down_y)], axis=0
    )
    rhs_far_x = permute(rhs_far, swap_x)
    fixed = call(share_kernel, piece_shape, [SMEM] + [VMEM] * ring, VMEM)(plan, *got)

    def scatter(value):
        value = value.reshape(chips, share, rows_y, rows_z)
        return lax.all_to_all(value, "orb", 0, 0, axis_index_groups=groups, tiled=True)

    def take(value, owner):
        return lax.dynamic_index_in_dim(value, owner, 0, keepdims=False)

    def apart(plan, occupied):
        return jnp.zeros((share, rows_y, rows_z), jnp.bfloat16)

    def together(plan, occupied):
        def plane_of(slot, plane):
            dims = (1, blk_rows, 1, rows_y, rows_z)
            return lax.dynamic_slice(occupied, (slot, 0, plane, 0, 0), dims).reshape(plane_shape.shape)

        mid = plan[MID + 1]
        other = permute(plane_of(mid % per_dev, 1 - core), swap_core)
        here = (mid // per_dev) % 2 == core
        again = scatter(jnp.where(here, plane_of(mid % per_dev, core), other))
        return take(again, plan[CHIP + 1])

    offered = scatter(offer)
    second = lax.cond(same[0] == 1, together, apart, plan, occupied)
    mids = call(
        take_kernel, shape((2 * share, rows_y, rows_z), jnp.bfloat16), [SMEM, VMEM, VMEM], VMEM
    )(plan, offered, second)

    xs = fixed.reshape(2 * share, cells)
    ys = mids.reshape(2 * share, cells)
    xs, ys = lax.optimization_barrier((xs, ys))
    xs_x = permute(xs, swap_x)
    ys_x = permute(ys, swap_x)
    ys_up = permute(ys, up_y)
    ys_down = permute(ys, down_y)
    own_rows = 4 * share
    half_shape = shape((local_orbs, n_rows))
    spread_shape = shape((n_dom, local_orbs, n_rows))
    rhs_places = [[(0, k), (ring - 1, k), (1, k)] for k in range(2)] + [[(2, k)] for k in range(2)]
    parts = call(
        functools.partial(shares_kernel, scale, rhs_places),
        shape((n_orb, local_orbs, 128)),
        [SMEM] + [VMEM] * 6,
    )(plan, rhs_line, rhs_line_x, rhs_far, rhs_far_x, xs, ys)
    parts = lax.all_to_all(parts, "orb", 0, 0, tiled=True)
    xs_x, ys_x, ys_up, ys_down = lax.optimization_barrier((xs_x, ys_x, ys_up, ys_down))
    own, line = call(
        functools.partial(pack_kernel, (2, 2)), (shape((4 * share, cells), jnp.bfloat16),) * 2
    )(xs, xs_x, ys_up, ys_down)
    line_x = permute(line, swap_x)
    above = permute(own, up_y)
    below = permute(own, down_y)
    far_up = permute(ys_up[:share], up_y)
    far_down = permute(ys_down[share:], down_y)
    parts, _ = lax.optimization_barrier((parts, line))
    first_parts = lax.all_to_all(
        call(spread_shares_kernel, spread_shape)(parts), "dom", 0, 0, tiled=True
    )
    line_x, above, below, far_up, far_down = lax.optimization_barrier(
        (line_x, above, below, far_up, far_down)
    )
    far_up_x, far_down_x = permute(far_up, swap_x), permute(far_down, swap_x)
    own_up = permute(above[: 2 * share], up_y)
    own_down = permute(below[2 * share :], down_y)
    block_shape = shape((n_rows // 2, cells), jnp.bfloat16)
    blocks = call(functools.partial(pack_kernel, (3, 5)), [block_shape] * 2)(
        own, below, above, ys, line, ys_x, line_x, jnp.concatenate([far_up, far_down], axis=0)
    )
    blocks = list(blocks)
    late = ((own_up, own_down), (far_up_x, far_down_x))
    for k, pair_of in enumerate(late):
        at = n_rows // 2 - sum(piece.shape[0] for piece in pair_of)
        for piece in pair_of:
            blocks[k] = lax.dynamic_update_slice(blocks[k], piece, (at, 0))
            at += piece.shape[0]

    picks = win_index[:, None] == jnp.arange(n_occ, dtype=jnp.int32)[None, :]
    eps = jnp.sum(jnp.where(picks, eigen_table[None, :], 0.0), axis=1)[:, None]
    eps = pair(eps, permute(eps, swap_core))
    plane_pot = lax.dynamic_index_in_dim(potential, core, 0, keepdims=True).reshape(1, cells)
    diag = 3.0 + plane_pot - eps
    psi_mine, psi_other = call(fields_kernel, (flat_field, flat_field))(
        low_mask, psi_win.astype(jnp.float32)
    )
    psi_wide = call(pair_kernel, field_shape)(
        low_mask, psi_mine, permute(psi_other.astype(jnp.bfloat16), swap_core).astype(jnp.float32)
    )
    flat_shape = (wide, n_rows // 2)

    def total(parts, outs):
        coeff_b, *coeff = call(total_kernel, outs)(parts)
        return coeff, coeff_b, permute(coeff_b, swap_core)

    row = jnp.arange(n_rows)
    within = row % (2 * share)
    down = jnp.array([0, 0, 1, 1, 3, 3, 2, 2, 0, 3, 1, 0, 3, 1, 2, 2])
    side = jnp.array([0, 1, 0, 1, 0, 1, 0, 1, 0, 0, 0, 1, 1, 1, 0, 1])
    chip = o // 2
    chip_from = (chip // ring + side) % 2 * ring + (chip % ring + down) % ring
    at = chip_from * own_rows + jnp.where(jnp.arange(16) < 8, 0, 2 * share)
    at = jnp.repeat(at, 2 * share) + within
    move = (row[:, None] == at[None, :]).astype(jnp.bfloat16)

    across = []
    for d in range(n_dom - 1):
        for k in range(chips):
            left, right = d * n_orb + 2 * k + 1, (d + 1) * n_orb + 2 * k
            across += [(left, right), (right, left)]

    x = None
    for step in range(ITERS):
        final = step == ITERS - 1
        sums = [shape(flat_shape, jnp.bfloat16)] + ([half_shape] if final else [])
        if step == 0:
            resid, parts = rhs_wide, first_parts
        else:
            sib = permute(x, swap_core)
            off = lax.ppermute(x_b, ("dom", "orb"), across)
            resid, mine, other = call(
                functools.partial(resid_kernel, scale, rows_z),
                (field_shape, half_shape, half_shape),
                scratch=(pltpu.VMEM((wide, cells), jnp.bfloat16),),
            )(low_mask, x, sib, off, rhs_wide, diag, *blocks)
            spread = call(spread_kernel, spread_shape)(mine, permute(other, swap_core))
            parts = lax.all_to_all(spread, "dom", 0, 0, tiled=True)
        coeff, coeff_b, coeff_o = total(parts, sums)
        extra = ([x] if step else [move]) + ([psi_wide] if final else [])
        outs = [field_shape, shape((wide, cells), jnp.bfloat16)]
        if final:
            outs = [shape((local_orbs, cells))] * 2 + [shape((n_dom, n_orb, rows_y // n_dom, rows_z))]
        x, x_b, *rest = call(
            functools.partial(update_kernel, scale, 512, step > 0, final, math.sqrt(width)), outs
        )(low_mask, coeff_b, coeff_o, resid, diag, *extra, *blocks)
    other, raw = x_b, rest[0]

    weights = jnp.broadcast_to(
        smoother.reshape(2 * n_dom, n_dom, 1, 2), (2 * n_dom, n_dom, chips, 2)
    ).reshape(2 * n_dom, n_dom * n_orb)
    terms = lax.all_to_all(
        raw.reshape((n_dom * n_orb,) + raw.shape[2:]), ("dom", "orb"), 0, 0, tiled=True
    )
    z_part = rows_z // n_orb
    z_mine = o * z_part + jnp.arange(z_part)[:, None]
    pick = (jnp.arange(rows_z)[None, :] == z_mine).astype(jnp.float32)
    gradient = call(finish_kernel, shape((rows_y // n_dom, z_part, 2 * n_dom)))(weights, pick, terms)
    gradient = jnp.transpose(gradient, (2, 0, 1))

    other = permute(other, swap_core)
    solution = jnp.stack([jnp.where(low, x, other), jnp.where(low, other, x)], axis=1)
    solution = solution.reshape(rhs.shape)

    coeff, raw = lax.optimization_barrier((coeff[0], raw))
    correlations = call(
        table_kernel,
        shape((n_rows, local_orbs)),
        [SMEM, VMEM],
        scratch=(pltpu.VMEM((n_rows, local_orbs), jnp.float32),),
    )(plan, coeff).reshape(nproj, blk_rows, local_orbs)
    return (solution, correlations, gradient)


def solution(mesh):
    return jax.shard_map(
        per_device,
        mesh=mesh,
        in_specs=(
            P("orb", "dom", None, None),
            P("dom", None, None),
            P(),
            P("orb"),
            P("orb", None, "dom", None, None),
            P(),
            P("orb", "dom", None, None),
            P(),
        ),
        out_specs=(P("orb", "dom", None, None), P(None, None, "orb"), P(None, "dom", "orb")),
        check_vma=False,
    )
```

```python
import functools
import math

import jax
import jax.numpy as jnp
from jax import lax
from jax.experimental import pallas as pl
from jax.experimental.pallas import tpu as pltpu
from jax.sharding import PartitionSpec as P

ITERS = 3
VMEM_LIMIT = 16 * 1024 * 1024
NT = (((1,), (1,)), ((), ()))
SMEM = pl.BlockSpec(memory_space=pltpu.SMEM)
ANY = pl.BlockSpec(memory_space=pl.ANY)
VMEM = pl.BlockSpec(memory_space=pltpu.VMEM)
HBM = pl.BlockSpec(memory_space=pltpu.HBM)

MID, CHIP, SAME, SLOT, CORE, DEV, TABLE = 0, 2, 4, 5, 6, 7, 8


def shape(dims, dtype=jnp.float32):
    return jax.ShapeDtypeStruct(dims, dtype)


def plan(per_dev, n_orb, ids_ref, dev_ref, out_ref):
    nproj = ids_ref.shape[0]
    chips = n_orb // 2
    ring = chips // 2
    last = per_dev * n_orb - 1
    dev = dev_ref[0]
    chip = dev // 2
    seen = jnp.int32(0)
    mids = [jnp.int32(0)] * (nproj - 2)
    order = []
    for j in range(nproj):
        block = ids_ref[j]
        middle = jnp.logical_and(block != 0, block != last)
        for k in range(nproj - 2):
            mids[k] = jnp.where(jnp.logical_and(middle, seen == k), block, mids[k])
        order.append(jnp.where(block == 0, 0, jnp.where(block == last, 1, 2 + seen)))
        seen = seen + jnp.where(middle, 1, 0)
    owners = [mid // (2 * per_dev) for mid in mids]
    for k in range(nproj - 2):
        out_ref[MID + k] = mids[k]
        out_ref[CHIP + k] = owners[k]
    out_ref[SAME] = jnp.where(owners[0] == owners[1], 1, 0)
    offer = jnp.where(chip == owners[0], mids[0], mids[1])
    out_ref[SLOT] = offer % per_dev
    out_ref[CORE] = (offer // per_dev) % 2
    out_ref[DEV] = dev
    y, x = chip % ring, chip // ring
    for j in range(nproj):
        for q in range(chips):
            down = (q // 2 + ring - y) % ring
            first = jnp.where(down == 1, 4, jnp.where(down == 3, 8, jnp.where(down == 2, 12, 0)))
            first = first + (order[j] + x) % 2 * 2 + q % 2
            down = (q % ring + ring - y) % ring
            side = (q // ring + x) % 2
            second = jnp.where(down == 1, 4, jnp.where(down == 3, 2, 0)) + side * 6
            second = 14 + jnp.where(down == 2, 12 + side * 2, second) + order[j]
            out_ref[TABLE + j * chips + q] = jnp.where(order[j] < 2, first, second)


def copies(source, target, sem):
    parts = sem.shape[0]
    rows = target.shape[0] // parts
    return [
        pltpu.make_async_copy(source(k * rows, rows), target.at[pl.ds(k * rows, rows)], sem.at[k])
        for k in range(parts)
    ]


def run(started):
    for copy in started:
        copy.start()
    for copy in started:
        copy.wait()


def offer_kernel(per_dev, n_orb, ids_ref, dev_ref, occupied_ref, plan_ref, same_ref, offer_ref, sem):
    plan(per_dev, n_orb, ids_ref, dev_ref, plan_ref)
    same_ref[0] = plan_ref[SAME]
    core = plan_ref[DEV] % 2
    run(copies(lambda at, n: occupied_ref.at[plan_ref[SLOT], pl.ds(at, n), 1 - core], offer_ref, sem))


def fixed_kernel(n_orb, plan_ref, occupied_ref, fixed_ref, sem):
    dev = plan_ref[DEV]
    core = dev % 2
    slot = core * (occupied_ref.shape[0] - 1)

    @pl.when(jnp.logical_or(dev == 0, dev == n_orb - 1))
    def _():
        run(copies(lambda at, n: occupied_ref.at[slot, pl.ds(at, n), 1 - core], fixed_ref, sem))


def pick_kernel(plan_ref, occupied_ref, offer_ref, out_ref, sem):
    core = plan_ref[DEV] % 2

    @pl.when(plan_ref[CORE] == core)
    def _():
        run(copies(lambda at, n: occupied_ref.at[plan_ref[SLOT], pl.ds(at, n), core], out_ref, sem))

    @pl.when(plan_ref[CORE] != core)
    def _():
        step = 16

        @pl.loop(0, out_ref.shape[0] // step)
        def _(k):
            here = pl.ds(k * step, step)
            out_ref[here] = offer_ref[here]


def pieces_kernel(n_orb, plan_ref, occupied_ref, fixed_ref, *refs):
    *piece_refs, sem = refs
    dev = plan_ref[DEV]
    core = dev % 2
    last = occupied_ref.shape[0] - 1
    ring = len(piece_refs)
    rows = piece_refs[0].shape[0]

    def at(s):
        return pl.ds(jnp.where(dev < n_orb // 2, s, (ring - 1 + s) % ring) * rows, rows)

    @pl.when(jnp.logical_or(dev == 0, dev == n_orb - 1))
    def _():
        run([
            pltpu.make_async_copy(occupied_ref.at[core * last, at(s), core], ref, sem.at[s])
            for s, ref in enumerate(piece_refs)
        ])

    @pl.when(jnp.logical_or(dev == 1, dev == n_orb - 2))
    def _():
        for s, ref in enumerate(piece_refs):
            ref[...] = fixed_ref[at(s)]


def share_kernel(plan_ref, *refs):
    *piece_refs, out_ref = refs
    ring = len(piece_refs)
    chip = plan_ref[DEV] // 2
    y, x = chip % ring, chip // ring
    away = (y + x) % ring
    for s, ref in enumerate(piece_refs):

        @pl.when(away == s)
        def _(ref=ref):
            out_ref[...] = ref[...]


def core_mask(low_ref, width):
    return jnp.concatenate([low_ref[...]] * (width // low_ref.shape[1]), axis=1) > 0.5


def split(low_ref, value, mine_ref, other_ref):
    half = value.shape[0] // 2
    low = core_mask(low_ref, value.shape[1])
    first, second = value[:half], value[half:]
    mine_ref[...] = jnp.where(low, first, second)
    other_ref[...] = jnp.where(low, second, first)


def project(scale, low_ref, resid_b, block_refs, mine_ref, other_ref):
    parts = [
        lax.dot_general(resid_b, ref[...], NT, preferred_element_type=jnp.float32) for ref in block_refs
    ]
    split(low_ref, jnp.concatenate(parts, axis=1) * scale, mine_ref, other_ref)


def fields_kernel(low_ref, field_ref, mine_ref, other_ref):
    rows_y, rows_z = field_ref.shape[2:]
    low = low_ref[...] > 0.5
    for y in range(rows_y):
        first, second = field_ref[:, 0, y, :], field_ref[:, 1, y, :]
        here = slice(y * rows_z, (y + 1) * rows_z)
        mine_ref[:, here] = jnp.where(low, first, second)
        other_ref[:, here] = jnp.where(low, second, first)


def pair_kernel(low_ref, mine_ref, other_ref, out_ref, *rounded_refs):
    half = mine_ref.shape[0]
    low = core_mask(low_ref, mine_ref.shape[1])
    mine, other = mine_ref[...], other_ref[...]
    both = jnp.concatenate([jnp.where(low, mine, other), jnp.where(low, other, mine)], axis=0)
    out_ref[...] = both
    for ref in rounded_refs:
        ref[...] = both.astype(jnp.bfloat16)


def take_kernel(plan_ref, offered_ref, second_ref, out_ref):
    rows = offered_ref.shape[1]
    out_ref[:rows] = offered_ref[plan_ref[CHIP]]

    @pl.when(plan_ref[SAME] == 1)
    def _():
        out_ref[rows:] = second_ref[...]

    @pl.when(plan_ref[SAME] != 1)
    def _():
        out_ref[rows:] = offered_ref[plan_ref[CHIP + 1]]


def shares_kernel(scale, places, plan_ref, *refs):
    *field_refs, ends_ref, mids_ref, out_ref = refs
    devices, orbs, lanes = out_ref.shape
    ring = devices // 4
    chip = plan_ref[DEV] // 2
    y, x = chip % ring, chip // ring
    spare = lanes - ends_ref.shape[0] - mids_ref.shape[0]
    for place, field_ref in zip(places, field_refs):
        field = field_ref[...]
        got = [
            lax.dot_general(field, ref[...], NT, preferred_element_type=jnp.float32)
            for ref in (ends_ref, mids_ref)
        ]
        rows = jnp.concatenate(got + [jnp.zeros((field.shape[0], spare), jnp.float32)], axis=1) * scale
        for k, (down, side) in enumerate(place):
            to = 2 * ((x + side) % 2 * ring + (y + down) % ring)
            at = k * 2 * orbs
            out_ref[pl.ds(to, 1)] = rows[at : at + orbs][None]
            out_ref[pl.ds(to + 1, 1)] = rows[at + orbs : at + 2 * orbs][None]


def spread_shares_kernel(parts_ref, out_ref):
    rows = out_ref.shape[2] * 2 // parts_ref.shape[0]
    total = jnp.concatenate(
        [(parts_ref[k] + parts_ref[k + 1])[:, :rows] for k in range(0, parts_ref.shape[0], 2)], axis=1
    )
    for d in range(out_ref.shape[0]):
        out_ref[d] = total


def resid_kernel(
    scale, row, low_ref, x_ref, sib_ref, off_ref, rhs_ref, diag_ref, first_ref, second_ref,
    resid_ref, mine_ref, other_ref, rb_ref,
):
    cells = x_ref.shape[1]
    lane = lax.broadcasted_iota(jnp.int32, (x_ref.shape[0], row), 1)
    for at in range(0, cells, row):
        here = slice(at, at + row)
        x = x_ref[:, here]
        beside = sib_ref[:, here] + off_ref[:, here].astype(jnp.float32)
        if at > 0:
            beside = beside + x_ref[:, at - row : at]
        if at + row < cells:
            beside = beside + x_ref[:, at + row : at + 2 * row]
        beside = beside + jnp.where(lane == 0, 0.0, pltpu.roll(x, 1, 1))
        beside = beside + jnp.where(lane == row - 1, 0.0, pltpu.roll(x, row - 1, 1))
        resid = rhs_ref[:, here] - (diag_ref[:, here] * x - 0.5 * beside)
        resid_ref[:, here] = resid
        rb_ref[:, here] = resid.astype(jnp.bfloat16)
    project(scale, low_ref, rb_ref[...], (first_ref, second_ref), mine_ref, other_ref)


def stacked(value):
    half = value.shape[1] // 2
    return jnp.concatenate([value[:, :half], value[:, half:]], axis=0)


def unstacked(value):
    half = value.shape[0] // 2
    return jnp.concatenate([value[:half], value[half:]], axis=1)


def spread_kernel(mine_ref, other_ref, out_ref):
    total = mine_ref[...] + other_ref[...]
    for d in range(out_ref.shape[0]):
        out_ref[d] = total


def total_kernel(parts_ref, *out_refs):
    total = parts_ref[0]
    for d in range(1, parts_ref.shape[0]):
        total = total + parts_ref[d]
    out_refs[0][...] = stacked(total).astype(jnp.bfloat16)
    if len(out_refs) > 1:
        out_refs[1][...] = total


def pack_kernel(splits, *refs):
    pieces, outs = refs[: sum(splits)], refs[sum(splits) :]
    for count, out_ref in zip(splits, outs):
        at = 0
        for ref in pieces[:count]:
            rows = ref.shape[0]
            out_ref[at : at + rows] = ref[...]
            at += rows
        pieces = pieces[count:]


def update_kernel(scale, tile, has_x, last, root, low_ref, mine_ref, other_ref, resid_ref, diag_ref, *refs):
    refs = list(refs)
    x_ref = refs.pop(0) if has_x else None
    move_ref = None if has_x else refs.pop(0)
    psi_ref = refs.pop(0) if last else None
    first_ref, second_ref, *outs = refs
    low = core_mask(low_ref, 2 * mine_ref.shape[1])
    mine = unstacked(mine_ref[...].astype(jnp.float32))
    other = unstacked(other_ref[...].astype(jnp.float32))
    coeff = jnp.concatenate([jnp.where(low, mine, other), jnp.where(low, other, mine)], axis=0)
    coeff = coeff.astype(jnp.bfloat16)
    if not has_x:
        coeff = jnp.dot(coeff, move_ref[...], preferred_element_type=jnp.float32).astype(jnp.bfloat16)
    cells = resid_ref.shape[1]
    for at in range(0, cells, tile):
        here = slice(at, at + tile)
        corr = 0.0
        start = 0
        for ref in (first_ref, second_ref):
            rows = ref.shape[0]
            some = coeff[:, start : start + rows]
            corr = corr + jnp.dot(some, ref[:, here], preferred_element_type=jnp.float32)
            start += rows
        x = (resid_ref[:, here] - corr * scale) / diag_ref[:, here]
        if has_x:
            x = x + x_ref[:, here]
        if last:
            half = x.shape[0] // 2
            low = core_mask(low_ref, tile)
            outs[0][:, here] = jnp.where(low, x[:half], x[half:])
            outs[1][:, here] = jnp.where(low, x[half:], x[:half])
            raw = jnp.sum(x * psi_ref[:, here].astype(jnp.float32), axis=0, keepdims=True) / root
            rows, wide = outs[2].shape[2:]
            for k in range(tile // wide):
                row = raw[:, k * wide : (k + 1) * wide]
                spot = at // wide + k
                outs[2][spot // rows, :, spot % rows, :] = jnp.broadcast_to(row, (outs[2].shape[1], wide))
        else:
            outs[0][:, here] = x
            outs[1][:, here] = x.astype(jnp.bfloat16)


def table_kernel(plan_ref, coeff_ref, out_ref, rows_ref):
    rows_ref[...] = coeff_ref[...].T
    share = 16
    for j in range(out_ref.shape[0] // share):
        at = pl.multiple_of(plan_ref[TABLE + j] * share, share)
        out_ref[j * share : (j + 1) * share] = rows_ref[pl.ds(at, share)]


def finish_kernel(weights_ref, pick_ref, terms_ref, out_ref):
    def product(one, two, dims):
        return lax.dot_general(
            one, two, (dims, ((), ())),
            precision=lax.Precision.HIGHEST, preferred_element_type=jnp.float32,
        )

    for k in range(terms_ref.shape[1]):
        mine = product(pick_ref[...], terms_ref[:, k, :], ((1,), (1,)))
        out_ref[k] = product(mine, weights_ref[...], ((1,), (1,)))


def call(kernel, out_shape, in_specs=None, out_specs=None, scratch=()):
    specs = {}
    if in_specs is not None:
        specs["in_specs"] = in_specs
    if out_specs is not None:
        specs["out_specs"] = out_specs
    return pl.pallas_call(
        kernel,
        out_shape=out_shape,
        scratch_shapes=scratch,
        compiler_params=pltpu.CompilerParams(vmem_limit_bytes=VMEM_LIMIT),
        **specs,
    )


def per_device(rhs, potential, eigen_table, win_index, occupied, block_ids, psi_win, smoother):
    local_orbs, planes, rows_y, rows_z = rhs.shape
    n_dom = lax.axis_size("dom")
    n_orb = lax.axis_size("orb")
    cells = rows_y * rows_z
    wide = 2 * local_orbs
    width = local_orbs * n_orb
    scale = 1.0 / math.sqrt(planes * n_dom * rows_y * rows_z)
    n_occ = eigen_table.shape[0]
    per_dev, blk_rows = occupied.shape[:2]
    nproj = block_ids.shape[0]
    chips = n_orb // 2
    ring = chips // 2
    share = blk_rows // chips
    n_rows = nproj * blk_rows
    o = lax.axis_index("orb")
    core = o % 2
    low = core == 0
    groups = [[2 * k + c for k in range(chips)] for c in range(2)]

    def chip_perm(target):
        return [(2 * k + c, 2 * target(k) + c) for k in range(chips) for c in range(2)]

    swap_core = [(i, i ^ 1) for i in range(n_orb)]
    swap_x = chip_perm(lambda k: (k + ring) % chips)
    up_y = chip_perm(lambda k: k // ring * ring + (k + 1) % ring)
    down_y = chip_perm(lambda k: k // ring * ring + (k - 1) % ring)

    def permute(value, pairs):
        return lax.ppermute(value, "orb", pairs)

    def pair(own, other):
        return jnp.concatenate([jnp.where(low, own, other), jnp.where(low, other, own)], axis=0)

    low_mask = jnp.broadcast_to(jnp.where(low, 1.0, 0.0), (local_orbs, 128))
    four = (pltpu.SemaphoreType.DMA((4,)),)

    plane_shape = shape((blk_rows, rows_y, rows_z), jnp.bfloat16)
    piece_shape = shape((2 * share, rows_y, rows_z), jnp.bfloat16)
    plan, same, offer = call(
        functools.partial(offer_kernel, per_dev, n_orb),
        (shape((TABLE + nproj * chips,), jnp.int32), shape((1,), jnp.int32), plane_shape),
        [SMEM, SMEM, ANY],
        (SMEM, SMEM, VMEM),
        four,
    )(block_ids, o.astype(jnp.int32).reshape(1), occupied)
    offer = permute(offer, swap_core)

    flat_field = shape((local_orbs, cells))
    field_shape = shape((wide, cells))
    rhs_mine, rhs_other = call(fields_kernel, (flat_field, flat_field))(low_mask, rhs)
    rhs_wide, rhs_b = call(pair_kernel, (field_shape, shape((wide, cells), jnp.bfloat16)))(
        low_mask, rhs_mine, permute(rhs_other, swap_core)
    )
    rhs_up, rhs_down = permute(rhs_b, up_y), permute(rhs_b, down_y)

    fixed = call(functools.partial(fixed_kernel, n_orb), plane_shape, [SMEM, ANY], VMEM, four)(plan, occupied)
    fixed = permute(fixed, [(0, 1), (n_orb - 1, n_orb - 2)])
    pieces = call(
        functools.partial(pieces_kernel, n_orb),
        [piece_shape] * ring,
        [SMEM, ANY, VMEM],
        [VMEM] * ring,
        (pltpu.SemaphoreType.DMA((ring,)),),
    )(plan, occupied, fixed)
    offer, *pieces = lax.optimization_barrier((offer, *pieces))
    offer = call(pick_kernel, plane_shape, [SMEM, ANY, VMEM], VMEM, four)(plan, occupied, offer)

    got = [pieces[0]]
    for s in range(1, ring):
        pairs = [(c, 2 * s + c) for c in range(2)]
        pairs += [(n_orb - 2 + c, 2 * (ring + (ring - 1 + s) % ring) + c) for c in range(2)]
        got.append(permute(pieces[s], pairs))
    rhs_up, rhs_down, *got[1:] = lax.optimization_barrier((rhs_up, rhs_down, *got[1:]))
    rhs_line = jnp.concatenate([rhs_b, rhs_up, rhs_down], axis=0)
    rhs_line_x = permute(rhs_line, swap_x)
    rhs_far = jnp.concatenate(
        [permute(rhs_up[:local_orbs], up_y), permute(rhs_down[local_orbs:], down_y)], axis=0
    )
    rhs_far_x = permute(rhs_far, swap_x)
    fixed = call(share_kernel, piece_shape, [SMEM] + [VMEM] * ring, VMEM)(plan, *got)

    def scatter(value):
        value = value.reshape(chips, share, rows_y, rows_z)
        return lax.all_to_all(value, "orb", 0, 0, axis_index_groups=groups, tiled=True)

    def take(value, owner):
        return lax.dynamic_index_in_dim(value, owner, 0, keepdims=False)

    def apart(plan, occupied):
        return jnp.zeros((share, rows_y, rows_z), jnp.bfloat16)

    def together(plan, occupied):
        def plane_of(slot, plane):
            dims = (1, blk_rows, 1, rows_y, rows_z)
            return lax.dynamic_slice(occupied, (slot, 0, plane, 0, 0), dims).reshape(plane_shape.shape)

        mid = plan[MID + 1]
        other = permute(plane_of(mid % per_dev, 1 - core), swap_core)
        here = (mid // per_dev) % 2 == core
        again = scatter(jnp.where(here, plane_of(mid % per_dev, core), other))
        return take(again, plan[CHIP + 1])

    offered = scatter(offer)
    second = lax.cond(same[0] == 1, together, apart, plan, occupied)
    mids = call(
        take_kernel, shape((2 * share, rows_y, rows_z), jnp.bfloat16), [SMEM, VMEM, VMEM], VMEM
    )(plan, offered, second)

    xs = fixed.reshape(2 * share, cells)
    ys = mids.reshape(2 * share, cells)
    xs, ys = lax.optimization_barrier((xs, ys))
    xs_x = permute(xs, swap_x)
    ys_x = permute(ys, swap_x)
    ys_up = permute(ys, up_y)
    ys_down = permute(ys, down_y)
    own_rows = 4 * share
    half_shape = shape((local_orbs, n_rows))
    spread_shape = shape((n_dom, local_orbs, n_rows))
    rhs_places = [[(0, k), (ring - 1, k), (1, k)] for k in range(2)] + [[(2, k)] for k in range(2)]
    parts = call(
        functools.partial(shares_kernel, scale, rhs_places),
        shape((n_orb, local_orbs, 128)),
        [SMEM] + [VMEM] * 6,
    )(plan, rhs_line, rhs_line_x, rhs_far, rhs_far_x, xs, ys)
    parts = lax.all_to_all(parts, "orb", 0, 0, tiled=True)
    xs_x, ys_x, ys_up, ys_down = lax.optimization_barrier((xs_x, ys_x, ys_up, ys_down))
    own, line = call(
        functools.partial(pack_kernel, (2, 2)), (shape((4 * share, cells), jnp.bfloat16),) * 2
    )(xs, xs_x, ys_up, ys_down)
    line_x = permute(line, swap_x)
    above = permute(own, up_y)
    below = permute(own, down_y)
    far_up = permute(ys_up[:share], up_y)
    far_down = permute(ys_down[share:], down_y)
    parts, _ = lax.optimization_barrier((parts, line))
    first_parts = lax.all_to_all(
        call(spread_shares_kernel, spread_shape)(parts), "dom", 0, 0, tiled=True
    )
    line_x, above, below, far_up, far_down = lax.optimization_barrier(
        (line_x, above, below, far_up, far_down)
    )
    far_up_x, far_down_x = permute(far_up, swap_x), permute(far_down, swap_x)
    own_up = permute(above[: 2 * share], up_y)
    own_down = permute(below[2 * share :], down_y)
    first_parts, own_up, own_down = lax.optimization_barrier((first_parts, own_up, own_down))
    block_shape = shape((n_rows // 2, cells), jnp.bfloat16)
    blocks = call(functools.partial(pack_kernel, (3, 5)), [block_shape] * 2)(
        own, below, above, ys, line, ys_x, line_x, jnp.concatenate([far_up, far_down], axis=0)
    )
    blocks = list(blocks)
    late = ((own_up, own_down), (far_up_x, far_down_x))
    for k, pair_of in enumerate(late):
        at = n_rows // 2 - sum(piece.shape[0] for piece in pair_of)
        for piece in pair_of:
            blocks[k] = lax.dynamic_update_slice(blocks[k], piece, (at, 0))
            at += piece.shape[0]

    picks = win_index[:, None] == jnp.arange(n_occ, dtype=jnp.int32)[None, :]
    eps = jnp.sum(jnp.where(picks, eigen_table[None, :], 0.0), axis=1)[:, None]
    eps = pair(eps, permute(eps, swap_core))
    plane_pot = lax.dynamic_index_in_dim(potential, core, 0, keepdims=True).reshape(1, cells)
    diag = 3.0 + plane_pot - eps
    psi_mine, psi_other = call(fields_kernel, (flat_field, flat_field))(
        low_mask, psi_win.astype(jnp.float32)
    )
    psi_wide = call(pair_kernel, field_shape)(
        low_mask, psi_mine, permute(psi_other.astype(jnp.bfloat16), swap_core).astype(jnp.float32)
    )
    flat_shape = (wide, n_rows // 2)

    def total(parts, outs):
        coeff_b, *coeff = call(total_kernel, outs)(parts)
        return coeff, coeff_b, permute(coeff_b, swap_core)

    row = jnp.arange(n_rows)
    within = row % (2 * share)
    down = jnp.array([0, 0, 1, 1, 3, 3, 2, 2, 0, 3, 1, 0, 3, 1, 2, 2])
    side = jnp.array([0, 1, 0, 1, 0, 1, 0, 1, 0, 0, 0, 1, 1, 1, 0, 1])
    chip = o // 2
    chip_from = (chip // ring + side) % 2 * ring + (chip % ring + down) % ring
    at = chip_from * own_rows + jnp.where(jnp.arange(16) < 8, 0, 2 * share)
    at = jnp.repeat(at, 2 * share) + within
    move = (row[:, None] == at[None, :]).astype(jnp.bfloat16)

    across = []
    for d in range(n_dom - 1):
        for k in range(chips):
            left, right = d * n_orb + 2 * k + 1, (d + 1) * n_orb + 2 * k
            across += [(left, right), (right, left)]

    x = None
    for step in range(ITERS):
        final = step == ITERS - 1
        sums = [shape(flat_shape, jnp.bfloat16)] + ([half_shape] if final else [])
        if step == 0:
            resid, parts = rhs_wide, first_parts
        else:
            sib = permute(x, swap_core)
            off = lax.ppermute(x_b, ("dom", "orb"), across)
            resid, mine, other = call(
                functools.partial(resid_kernel, scale, rows_z),
                (field_shape, half_shape, half_shape),
                scratch=(pltpu.VMEM((wide, cells), jnp.bfloat16),),
            )(low_mask, x, sib, off, rhs_wide, diag, *blocks)
            spread = call(spread_kernel, spread_shape)(mine, permute(other, swap_core))
            parts = lax.all_to_all(spread, "dom", 0, 0, tiled=True)
        coeff, coeff_b, coeff_o = total(parts, sums)
        extra = ([x] if step else [move]) + ([psi_wide] if final else [])
        outs = [field_shape, shape((wide, cells), jnp.bfloat16)]
        if final:
            outs = [shape((local_orbs, cells))] * 2 + [shape((n_dom, n_orb, rows_y // n_dom, rows_z))]
        x, x_b, *rest = call(
            functools.partial(update_kernel, scale, 512, step > 0, final, math.sqrt(width)), outs
        )(low_mask, coeff_b, coeff_o, resid, diag, *extra, *blocks)
    other, raw = x_b, rest[0]

    weights = jnp.broadcast_to(
        smoother.reshape(2 * n_dom, n_dom, 1, 2), (2 * n_dom, n_dom, chips, 2)
    ).reshape(2 * n_dom, n_dom * n_orb)
    terms = lax.all_to_all(
        raw.reshape((n_dom * n_orb,) + raw.shape[2:]), ("dom", "orb"), 0, 0, tiled=True
    )
    z_part = rows_z // n_orb
    z_mine = o * z_part + jnp.arange(z_part)[:, None]
    pick = (jnp.arange(rows_z)[None, :] == z_mine).astype(jnp.float32)
    gradient = call(finish_kernel, shape((rows_y // n_dom, z_part, 2 * n_dom)))(weights, pick, terms)
    gradient = jnp.transpose(gradient, (2, 0, 1))

    other = permute(other, swap_core)
    solution = jnp.stack([jnp.where(low, x, other), jnp.where(low, other, x)], axis=1)
    solution = solution.reshape(rhs.shape)

    coeff, raw = lax.optimization_barrier((coeff[0], raw))
    correlations = call(
        table_kernel,
        shape((n_rows, local_orbs)),
        [SMEM, VMEM],
        scratch=(pltpu.VMEM((n_rows, local_orbs), jnp.float32),),
    )(plan, coeff).reshape(nproj, blk_rows, local_orbs)
    return (solution, correlations, gradient)


def solution(mesh):
    return jax.shard_map(
        per_device,
        mesh=mesh,
        in_specs=(
            P("orb", "dom", None, None),
            P("dom", None, None),
            P(),
            P("orb"),
            P("orb", None, "dom", None, None),
            P(),
            P("orb", "dom", None, None),
            P(),
        ),
        out_specs=(P("orb", "dom", None, None), P(None, None, "orb"), P(None, "dom", "orb")),
        check_vma=False,
    )
```

```python
import functools
import math

import jax
import jax.numpy as jnp
from jax import lax
from jax.experimental import pallas as pl
from jax.experimental.pallas import tpu as pltpu
from jax.sharding import PartitionSpec as P

ITERS = 3
VMEM_LIMIT = 16 * 1024 * 1024
NT = (((1,), (1,)), ((), ()))
SMEM = pl.BlockSpec(memory_space=pltpu.SMEM)
ANY = pl.BlockSpec(memory_space=pl.ANY)
VMEM = pl.BlockSpec(memory_space=pltpu.VMEM)
HBM = pl.BlockSpec(memory_space=pltpu.HBM)

MID, CHIP, SAME, SLOT, CORE, DEV, TABLE = 0, 2, 4, 5, 6, 7, 8


def shape(dims, dtype=jnp.float32):
    return jax.ShapeDtypeStruct(dims, dtype)


def plan(per_dev, n_orb, ids_ref, dev_ref, out_ref):
    nproj = ids_ref.shape[0]
    chips = n_orb // 2
    ring = chips // 2
    last = per_dev * n_orb - 1
    dev = dev_ref[0]
    chip = dev // 2
    seen = jnp.int32(0)
    mids = [jnp.int32(0)] * (nproj - 2)
    order = []
    for j in range(nproj):
        block = ids_ref[j]
        middle = jnp.logical_and(block != 0, block != last)
        for k in range(nproj - 2):
            mids[k] = jnp.where(jnp.logical_and(middle, seen == k), block, mids[k])
        order.append(jnp.where(block == 0, 0, jnp.where(block == last, 1, 2 + seen)))
        seen = seen + jnp.where(middle, 1, 0)
    owners = [mid // (2 * per_dev) for mid in mids]
    for k in range(nproj - 2):
        out_ref[MID + k] = mids[k]
        out_ref[CHIP + k] = owners[k]
    out_ref[SAME] = jnp.where(owners[0] == owners[1], 1, 0)
    offer = jnp.where(chip == owners[0], mids[0], mids[1])
    out_ref[SLOT] = offer % per_dev
    out_ref[CORE] = (offer // per_dev) % 2
    out_ref[DEV] = dev
    y, x = chip % ring, chip // ring
    for j in range(nproj):
        for q in range(chips):
            down = (q // 2 + ring - y) % ring
            first = jnp.where(down == 1, 4, jnp.where(down == 3, 8, jnp.where(down == 2, 12, 0)))
            first = first + (order[j] + x) % 2 * 2 + q % 2
            down = (q % ring + ring - y) % ring
            side = (q // ring + x) % 2
            second = jnp.where(down == 1, 4, jnp.where(down == 3, 2, 0)) + side * 6
            second = 14 + jnp.where(down == 2, 12 + side * 2, second) + order[j]
            out_ref[TABLE + j * chips + q] = jnp.where(order[j] < 2, first, second)


def copies(source, target, sem):
    parts = sem.shape[0]
    rows = target.shape[0] // parts
    return [
        pltpu.make_async_copy(source(k * rows, rows), target.at[pl.ds(k * rows, rows)], sem.at[k])
        for k in range(parts)
    ]


def run(started):
    for copy in started:
        copy.start()
    for copy in started:
        copy.wait()


def offer_kernel(per_dev, n_orb, ids_ref, dev_ref, occupied_ref, plan_ref, same_ref, offer_ref, sem):
    plan(per_dev, n_orb, ids_ref, dev_ref, plan_ref)
    same_ref[0] = plan_ref[SAME]
    core = plan_ref[DEV] % 2
    run(copies(lambda at, n: occupied_ref.at[plan_ref[SLOT], pl.ds(at, n), 1 - core], offer_ref, sem))


def fixed_kernel(n_orb, plan_ref, occupied_ref, fixed_ref, sem):
    dev = plan_ref[DEV]
    core = dev % 2
    slot = core * (occupied_ref.shape[0] - 1)

    @pl.when(jnp.logical_or(dev == 0, dev == n_orb - 1))
    def _():
        run(copies(lambda at, n: occupied_ref.at[slot, pl.ds(at, n), 1 - core], fixed_ref, sem))


def pick_kernel(plan_ref, occupied_ref, offer_ref, out_ref, sem):
    core = plan_ref[DEV] % 2

    @pl.when(plan_ref[CORE] == core)
    def _():
        run(copies(lambda at, n: occupied_ref.at[plan_ref[SLOT], pl.ds(at, n), core], out_ref, sem))

    @pl.when(plan_ref[CORE] != core)
    def _():
        step = 16

        @pl.loop(0, out_ref.shape[0] // step)
        def _(k):
            here = pl.ds(k * step, step)
            out_ref[here] = offer_ref[here]


def pieces_kernel(n_orb, plan_ref, occupied_ref, fixed_ref, *refs):
    *piece_refs, sem = refs
    dev = plan_ref[DEV]
    core = dev % 2
    last = occupied_ref.shape[0] - 1
    ring = len(piece_refs)
    rows = piece_refs[0].shape[0]

    def at(s):
        return pl.ds(jnp.where(dev < n_orb // 2, s, (ring - 1 + s) % ring) * rows, rows)

    @pl.when(jnp.logical_or(dev == 0, dev == n_orb - 1))
    def _():
        run([
            pltpu.make_async_copy(occupied_ref.at[core * last, at(s), core], ref, sem.at[s])
            for s, ref in enumerate(piece_refs)
        ])

    @pl.when(jnp.logical_or(dev == 1, dev == n_orb - 2))
    def _():
        for s, ref in enumerate(piece_refs):
            ref[...] = fixed_ref[at(s)]


def share_kernel(plan_ref, *refs):
    *piece_refs, out_ref = refs
    ring = len(piece_refs)
    chip = plan_ref[DEV] // 2
    y, x = chip % ring, chip // ring
    away = (y + x) % ring
    for s, ref in enumerate(piece_refs):

        @pl.when(away == s)
        def _(ref=ref):
            out_ref[...] = ref[...]


def core_mask(low_ref, width):
    return jnp.concatenate([low_ref[...]] * (width // low_ref.shape[1]), axis=1) > 0.5


def split(low_ref, value, mine_ref, other_ref):
    half = value.shape[0] // 2
    low = core_mask(low_ref, value.shape[1])
    first, second = value[:half], value[half:]
    mine_ref[...] = jnp.where(low, first, second)
    other_ref[...] = jnp.where(low, second, first)


def project(scale, low_ref, resid_b, block_refs, mine_ref, other_ref):
    parts = [
        lax.dot_general(resid_b, ref[...], NT, preferred_element_type=jnp.float32) for ref in block_refs
    ]
    split(low_ref, jnp.concatenate(parts, axis=1) * scale, mine_ref, other_ref)


def fields_kernel(low_ref, field_ref, mine_ref, other_ref):
    rows_y, rows_z = field_ref.shape[2:]
    low = low_ref[...] > 0.5
    for y in range(rows_y):
        first, second = field_ref[:, 0, y, :], field_ref[:, 1, y, :]
        here = slice(y * rows_z, (y + 1) * rows_z)
        mine_ref[:, here] = jnp.where(low, first, second)
        other_ref[:, here] = jnp.where(low, second, first)


def pair_kernel(low_ref, mine_ref, other_ref, out_ref, *rounded_refs):
    half = mine_ref.shape[0]
    low = core_mask(low_ref, mine_ref.shape[1])
    mine, other = mine_ref[...], other_ref[...]
    both = jnp.concatenate([jnp.where(low, mine, other), jnp.where(low, other, mine)], axis=0)
    out_ref[...] = both
    for ref in rounded_refs:
        ref[...] = both.astype(jnp.bfloat16)


def take_kernel(plan_ref, offered_ref, second_ref, out_ref):
    rows = offered_ref.shape[1]
    out_ref[:rows] = offered_ref[plan_ref[CHIP]]

    @pl.when(plan_ref[SAME] == 1)
    def _():
        out_ref[rows:] = second_ref[...]

    @pl.when(plan_ref[SAME] != 1)
    def _():
        out_ref[rows:] = offered_ref[plan_ref[CHIP + 1]]


def shares_kernel(scale, places, plan_ref, *refs):
    *field_refs, ends_ref, mids_ref, out_ref = refs
    devices, orbs, lanes = out_ref.shape
    ring = devices // 4
    chip = plan_ref[DEV] // 2
    y, x = chip % ring, chip // ring
    spare = lanes - ends_ref.shape[0] - mids_ref.shape[0]
    for place, field_ref in zip(places, field_refs):
        field = field_ref[...]
        got = [
            lax.dot_general(field, ref[...], NT, preferred_element_type=jnp.float32)
            for ref in (ends_ref, mids_ref)
        ]
        rows = jnp.concatenate(got + [jnp.zeros((field.shape[0], spare), jnp.float32)], axis=1) * scale
        for k, (down, side) in enumerate(place):
            to = 2 * ((x + side) % 2 * ring + (y + down) % ring)
            at = k * 2 * orbs
            out_ref[pl.ds(to, 1)] = rows[at : at + orbs][None]
            out_ref[pl.ds(to + 1, 1)] = rows[at + orbs : at + 2 * orbs][None]


def spread_shares_kernel(parts_ref, out_ref):
    rows = out_ref.shape[2] * 2 // parts_ref.shape[0]
    total = jnp.concatenate(
        [(parts_ref[k] + parts_ref[k + 1])[:, :rows] for k in range(0, parts_ref.shape[0], 2)], axis=1
    )
    for d in range(out_ref.shape[0]):
        out_ref[d] = total


def resid_kernel(
    scale, row, low_ref, x_ref, sib_ref, off_ref, rhs_ref, diag_ref, first_ref, second_ref,
    resid_ref, mine_ref, other_ref, rb_ref,
):
    cells = x_ref.shape[1]
    lane = lax.broadcasted_iota(jnp.int32, (x_ref.shape[0], row), 1)
    for at in range(0, cells, row):
        here = slice(at, at + row)
        x = x_ref[:, here]
        beside = sib_ref[:, here] + off_ref[:, here].astype(jnp.float32)
        if at > 0:
            beside = beside + x_ref[:, at - row : at]
        if at + row < cells:
            beside = beside + x_ref[:, at + row : at + 2 * row]
        beside = beside + jnp.where(lane == 0, 0.0, pltpu.roll(x, 1, 1))
        beside = beside + jnp.where(lane == row - 1, 0.0, pltpu.roll(x, row - 1, 1))
        resid = rhs_ref[:, here] - (diag_ref[:, here] * x - 0.5 * beside)
        resid_ref[:, here] = resid
        rb_ref[:, here] = resid.astype(jnp.bfloat16)
    project(scale, low_ref, rb_ref[...], (first_ref, second_ref), mine_ref, other_ref)


def stacked(value):
    half = value.shape[1] // 2
    return jnp.concatenate([value[:, :half], value[:, half:]], axis=0)


def unstacked(value):
    half = value.shape[0] // 2
    return jnp.concatenate([value[:half], value[half:]], axis=1)


def spread_kernel(mine_ref, other_ref, out_ref):
    total = mine_ref[...] + other_ref[...]
    for d in range(out_ref.shape[0]):
        out_ref[d] = total


def total_kernel(parts_ref, *out_refs):
    total = parts_ref[0]
    for d in range(1, parts_ref.shape[0]):
        total = total + parts_ref[d]
    out_refs[0][...] = stacked(total).astype(jnp.bfloat16)
    if len(out_refs) > 1:
        out_refs[1][...] = total


def pack_kernel(splits, *refs):
    pieces, outs = refs[: sum(splits)], refs[sum(splits) :]
    for count, out_ref in zip(splits, outs):
        at = 0
        for ref in pieces[:count]:
            rows = ref.shape[0]
            out_ref[at : at + rows] = ref[...]
            at += rows
        pieces = pieces[count:]


def packed(splits, *refs):
    *refs, sem = refs
    pieces, outs = refs[: sum(splits)], refs[sum(splits) :]
    moves = []
    for count, out_ref in zip(splits, outs):
        at = 0
        for ref in pieces[:count]:
            rows = ref.shape[0]
            moves.append(pltpu.make_async_copy(ref, out_ref.at[pl.ds(at, rows)], sem.at[len(moves)]))
            at += rows
        pieces = pieces[count:]
    return moves


def update_kernel(scale, tile, has_x, last, root, splits, low_ref, mine_ref, other_ref, resid_ref, diag_ref, *refs):
    refs = list(refs)
    x_ref = refs.pop(0) if has_x else None
    move_ref = None if has_x else refs.pop(0)
    psi_ref = refs.pop(0) if last else None
    if has_x:
        first_ref, second_ref, *outs = refs
    else:
        *refs, x_out, x_b_out, first_ref, second_ref, sem = refs
        outs = [x_out, x_b_out]
    low = core_mask(low_ref, 2 * mine_ref.shape[1])
    mine = unstacked(mine_ref[...].astype(jnp.float32))
    other = unstacked(other_ref[...].astype(jnp.float32))
    coeff = jnp.concatenate([jnp.where(low, mine, other), jnp.where(low, other, mine)], axis=0)
    coeff = coeff.astype(jnp.bfloat16)
    if not has_x:
        coeff = jnp.dot(coeff, move_ref[...], preferred_element_type=jnp.float32).astype(jnp.bfloat16)
        run(packed(splits, *refs, first_ref, second_ref, sem))
    cells = resid_ref.shape[1]
    for at in range(0, cells, tile):
        here = slice(at, at + tile)
        corr = 0.0
        start = 0
        for ref in (first_ref, second_ref):
            rows = ref.shape[0]
            some = coeff[:, start : start + rows]
            corr = corr + jnp.dot(some, ref[:, here], preferred_element_type=jnp.float32)
            start += rows
        x = (resid_ref[:, here] - corr * scale) / diag_ref[:, here]
        if has_x:
            x = x + x_ref[:, here]
        if last:
            half = x.shape[0] // 2
            low = core_mask(low_ref, tile)
            outs[0][:, here] = jnp.where(low, x[:half], x[half:])
            outs[1][:, here] = jnp.where(low, x[half:], x[:half])
            raw = jnp.sum(x * psi_ref[:, here].astype(jnp.float32), axis=0, keepdims=True) / root
            rows, wide = outs[2].shape[2:]
            for k in range(tile // wide):
                row = raw[:, k * wide : (k + 1) * wide]
                spot = at // wide + k
                outs[2][spot // rows, :, spot % rows, :] = jnp.broadcast_to(row, (outs[2].shape[1], wide))
        else:
            outs[0][:, here] = x
            outs[1][:, here] = x.astype(jnp.bfloat16)


def table_kernel(plan_ref, coeff_ref, out_ref, rows_ref):
    rows_ref[...] = coeff_ref[...].T
    share = 16
    for j in range(out_ref.shape[0] // share):
        at = pl.multiple_of(plan_ref[TABLE + j] * share, share)
        out_ref[j * share : (j + 1) * share] = rows_ref[pl.ds(at, share)]


def finish_kernel(smoother_ref, pick_ref, terms_ref, out_ref):
    def product(one, two, dims):
        return lax.dot_general(
            one, two, (dims, ((), ())),
            precision=lax.Precision.HIGHEST, preferred_element_type=jnp.float32,
        )

    sources, planes = terms_ref.shape[0], smoother_ref.shape[1]
    chips = sources // planes
    row = lax.broadcasted_iota(jnp.int32, (sources, planes), 0)
    plane = lax.broadcasted_iota(jnp.int32, (sources, planes), 1)
    same = jnp.logical_and(row // (2 * chips) == plane // 2, row % 2 == plane % 2)
    gather = jnp.where(same, 1.0, 0.0)
    for k in range(terms_ref.shape[1]):
        mine = product(pick_ref[...], terms_ref[:, k, :], ((1,), (1,)))
        raw = product(mine, gather, ((1,), (0,)))
        out_ref[k] = product(raw, smoother_ref[...], ((1,), (1,)))


def call(kernel, out_shape, in_specs=None, out_specs=None, scratch=()):
    specs = {}
    if in_specs is not None:
        specs["in_specs"] = in_specs
    if out_specs is not None:
        specs["out_specs"] = out_specs
    return pl.pallas_call(
        kernel,
        out_shape=out_shape,
        scratch_shapes=scratch,
        compiler_params=pltpu.CompilerParams(vmem_limit_bytes=VMEM_LIMIT),
        **specs,
    )


def per_device(rhs, potential, eigen_table, win_index, occupied, block_ids, psi_win, smoother):
    local_orbs, planes, rows_y, rows_z = rhs.shape
    n_dom = lax.axis_size("dom")
    n_orb = lax.axis_size("orb")
    cells = rows_y * rows_z
    wide = 2 * local_orbs
    width = local_orbs * n_orb
    scale = 1.0 / math.sqrt(planes * n_dom * rows_y * rows_z)
    n_occ = eigen_table.shape[0]
    per_dev, blk_rows = occupied.shape[:2]
    nproj = block_ids.shape[0]
    chips = n_orb // 2
    ring = chips // 2
    share = blk_rows // chips
    n_rows = nproj * blk_rows
    o = lax.axis_index("orb")
    core = o % 2
    low = core == 0
    groups = [[2 * k + c for k in range(chips)] for c in range(2)]

    def chip_perm(target):
        return [(2 * k + c, 2 * target(k) + c) for k in range(chips) for c in range(2)]

    swap_core = [(i, i ^ 1) for i in range(n_orb)]
    swap_x = chip_perm(lambda k: (k + ring) % chips)
    up_y = chip_perm(lambda k: k // ring * ring + (k + 1) % ring)
    down_y = chip_perm(lambda k: k // ring * ring + (k - 1) % ring)

    over_y = chip_perm(lambda k: k // ring * ring + (k + 2) % ring)

    def permute(value, pairs):
        return lax.ppermute(value, "orb", pairs)

    def pair(own, other):
        return jnp.concatenate([jnp.where(low, own, other), jnp.where(low, other, own)], axis=0)

    low_mask = jnp.broadcast_to(jnp.where(low, 1.0, 0.0), (local_orbs, 128))
    four = (pltpu.SemaphoreType.DMA((4,)),)

    plane_shape = shape((blk_rows, rows_y, rows_z), jnp.bfloat16)
    piece_shape = shape((2 * share, rows_y, rows_z), jnp.bfloat16)
    plan, same, offer = call(
        functools.partial(offer_kernel, per_dev, n_orb),
        (shape((TABLE + nproj * chips,), jnp.int32), shape((1,), jnp.int32), plane_shape),
        [SMEM, SMEM, ANY],
        (SMEM, SMEM, VMEM),
        four,
    )(block_ids, o.astype(jnp.int32).reshape(1), occupied)
    offer = permute(offer, swap_core)

    flat_field = shape((local_orbs, cells))
    field_shape = shape((wide, cells))
    rhs_mine, rhs_other = call(fields_kernel, (flat_field, flat_field))(low_mask, rhs)
    rhs_wide, rhs_b = call(pair_kernel, (field_shape, shape((wide, cells), jnp.bfloat16)))(
        low_mask, rhs_mine, permute(rhs_other, swap_core)
    )
    rhs_up, rhs_down, rhs_far = permute(rhs_b, up_y), permute(rhs_b, down_y), permute(rhs_b, over_y)

    offer = call(pick_kernel, plane_shape, [SMEM, ANY, VMEM], VMEM, four)(plan, occupied, offer)
    fixed = call(functools.partial(fixed_kernel, n_orb), plane_shape, [SMEM, ANY], VMEM, four)(plan, occupied)
    fixed = permute(fixed, [(0, 1), (n_orb - 1, n_orb - 2)])
    offer, fixed = lax.optimization_barrier((offer, fixed))
    pieces = call(
        functools.partial(pieces_kernel, n_orb),
        [piece_shape] * ring,
        [SMEM, ANY, VMEM],
        [VMEM] * ring,
        (pltpu.SemaphoreType.DMA((ring,)),),
    )(plan, occupied, fixed)

    got = [pieces[0]]
    for s in range(1, ring):
        pairs = [(c, 2 * s + c) for c in range(2)]
        pairs += [(n_orb - 2 + c, 2 * (ring + (ring - 1 + s) % ring) + c) for c in range(2)]
        got.append(permute(pieces[s], pairs))
    rhs_up, rhs_down, rhs_far, got[1] = lax.optimization_barrier((rhs_up, rhs_down, rhs_far, got[1]))
    rhs_line = jnp.concatenate([rhs_b, rhs_up, rhs_down, rhs_far], axis=0)
    rhs_line_x = permute(rhs_line, swap_x)
    fixed = call(share_kernel, piece_shape, [SMEM] + [VMEM] * ring, VMEM)(plan, *got)

    def scatter(value):
        value = value.reshape(chips, share, rows_y, rows_z)
        return lax.all_to_all(value, "orb", 0, 0, axis_index_groups=groups, tiled=True)

    def take(value, owner):
        return lax.dynamic_index_in_dim(value, owner, 0, keepdims=False)

    def apart(plan, occupied):
        return jnp.zeros((share, rows_y, rows_z), jnp.bfloat16)

    def together(plan, occupied):
        def plane_of(slot, plane):
            dims = (1, blk_rows, 1, rows_y, rows_z)
            return lax.dynamic_slice(occupied, (slot, 0, plane, 0, 0), dims).reshape(plane_shape.shape)

        mid = plan[MID + 1]
        other = permute(plane_of(mid % per_dev, 1 - core), swap_core)
        here = (mid // per_dev) % 2 == core
        again = scatter(jnp.where(here, plane_of(mid % per_dev, core), other))
        return take(again, plan[CHIP + 1])

    offered = scatter(offer)
    second = lax.cond(same[0] == 1, together, apart, plan, occupied)
    mids = call(
        take_kernel, shape((2 * share, rows_y, rows_z), jnp.bfloat16), [SMEM, VMEM, VMEM], VMEM
    )(plan, offered, second)

    xs = fixed.reshape(2 * share, cells)
    ys = mids.reshape(2 * share, cells)
    xs, ys = lax.optimization_barrier((xs, ys))
    xs_x = permute(xs, swap_x)
    ys_up = permute(ys, up_y)
    ys_down = permute(ys, down_y)
    own_rows = 4 * share
    half_shape = shape((local_orbs, n_rows))
    spread_shape = shape((n_dom, local_orbs, n_rows))
    rhs_places = [[(0, k), (ring - 1, k), (1, k), (2, k)] for k in range(2)]
    parts = call(
        functools.partial(shares_kernel, scale, rhs_places),
        shape((n_orb, local_orbs, 128)),
        [SMEM] + [VMEM] * 4,
    )(plan, rhs_line, rhs_line_x, xs, ys)
    parts = lax.all_to_all(parts, "orb", 0, 0, tiled=True)
    xs_x, ys_up, ys_down = lax.optimization_barrier((xs_x, ys_up, ys_down))
    own, line = call(
        functools.partial(pack_kernel, (2, 3)),
        (shape((4 * share, cells), jnp.bfloat16), shape((6 * share, cells), jnp.bfloat16)),
    )(xs, xs_x, ys, ys_up, ys_down)
    line_x = permute(line, swap_x)
    above = permute(own, up_y)
    below = permute(own, down_y)
    far_up = permute(ys_up[:share], up_y)
    far_down = permute(ys_down[share:], down_y)
    parts, _ = lax.optimization_barrier((parts, line))
    first_parts = lax.all_to_all(
        call(spread_shares_kernel, spread_shape)(parts), "dom", 0, 0, tiled=True
    )
    line_x, above, below, far_up, far_down = lax.optimization_barrier(
        (line_x, above, below, far_up, far_down)
    )
    far_up_x, far_down_x = permute(far_up, swap_x), permute(far_down, swap_x)
    own_up = permute(above[: 2 * share], up_y)
    own_down = permute(below[2 * share :], down_y)
    pieces = [own, below, above, own_up, own_down]
    pieces += [line, line_x, far_up, far_down, far_up_x, far_down_x]
    blocks_shape = [shape((n_rows // 2, cells), jnp.bfloat16)] * 2

    picks = win_index[:, None] == jnp.arange(n_occ, dtype=jnp.int32)[None, :]
    eps = jnp.sum(jnp.where(picks, eigen_table[None, :], 0.0), axis=1)[:, None]
    eps = pair(eps, permute(eps, swap_core))
    plane_pot = lax.dynamic_index_in_dim(potential, core, 0, keepdims=True).reshape(1, cells)
    diag = 3.0 + plane_pot - eps
    psi_mine, psi_other = call(fields_kernel, (flat_field, flat_field))(
        low_mask, psi_win.astype(jnp.float32)
    )
    psi_wide = call(pair_kernel, field_shape)(
        low_mask, psi_mine, permute(psi_other.astype(jnp.bfloat16), swap_core).astype(jnp.float32)
    )
    flat_shape = (wide, n_rows // 2)

    def total(parts, outs):
        coeff_b, *coeff = call(total_kernel, outs)(parts)
        return coeff, coeff_b, permute(coeff_b, swap_core)

    row = jnp.arange(n_rows)
    within = row % (2 * share)
    down = jnp.array([0, 0, 1, 1, 3, 3, 2, 2, 0, 3, 1, 0, 3, 1, 2, 2])
    side = jnp.array([0, 1, 0, 1, 0, 1, 0, 1, 0, 0, 0, 1, 1, 1, 0, 1])
    chip = o // 2
    chip_from = (chip // ring + side) % 2 * ring + (chip % ring + down) % ring
    at = chip_from * own_rows + jnp.where(jnp.arange(16) < 8, 0, 2 * share)
    at = jnp.repeat(at, 2 * share) + within
    move = (row[:, None] == at[None, :]).astype(jnp.bfloat16)

    across = []
    for d in range(n_dom - 1):
        for k in range(chips):
            left, right = d * n_orb + 2 * k + 1, (d + 1) * n_orb + 2 * k
            across += [(left, right), (right, left)]

    x = None
    for step in range(ITERS):
        final = step == ITERS - 1
        sums = [shape(flat_shape, jnp.bfloat16)] + ([half_shape] if final else [])
        if step == 0:
            resid, parts = rhs_wide, first_parts
        else:
            sib = permute(x, swap_core)
            off = lax.ppermute(x_b, ("dom", "orb"), across)
            resid, mine, other = call(
                functools.partial(resid_kernel, scale, rows_z),
                (field_shape, half_shape, half_shape),
                scratch=(pltpu.VMEM((wide, cells), jnp.bfloat16),),
            )(low_mask, x, sib, off, rhs_wide, diag, *blocks)
            spread = call(spread_kernel, spread_shape)(mine, permute(other, swap_core))
            parts = lax.all_to_all(spread, "dom", 0, 0, tiled=True)
        coeff, coeff_b, coeff_o = total(parts, sums)
        extra = ([x] if step else [move]) + ([psi_wide] if final else [])
        outs = [field_shape, shape((wide, cells), jnp.bfloat16)]
        if final:
            outs = [shape((local_orbs, cells))] * 2 + [shape((n_dom, n_orb, rows_y // n_dom, rows_z))]
        if step == 0:
            outs, blocks = outs + blocks_shape, pieces
            specs = [VMEM] * 6 + [HBM] * len(pieces), [VMEM] * 4
            sems = (pltpu.SemaphoreType.DMA((len(pieces),)),)
        else:
            specs, sems = (None, None), ()
        x, x_b, *rest = call(
            functools.partial(update_kernel, scale, 512, step > 0, final, math.sqrt(width), (5, 6)),
            outs,
            *specs,
            sems,
        )(low_mask, coeff_b, coeff_o, resid, diag, *extra, *blocks)
        if step == 0:
            blocks = rest
    other, raw = x_b, rest[0]

    terms = lax.all_to_all(
        raw.reshape((n_dom * n_orb,) + raw.shape[2:]), ("dom", "orb"), 0, 0, tiled=True
    )
    z_part = rows_z // n_orb
    z_mine = o * z_part + jnp.arange(z_part)[:, None]
    pick = (jnp.arange(rows_z)[None, :] == z_mine).astype(jnp.float32)
    gradient = call(finish_kernel, shape((rows_y // n_dom, z_part, 2 * n_dom)))(smoother, pick, terms)
    gradient = jnp.transpose(gradient, (2, 0, 1))

    other = permute(other, swap_core)
    solution = jnp.stack([jnp.where(low, x, other), jnp.where(low, other, x)], axis=1)
    solution = solution.reshape(rhs.shape)

    coeff, raw = lax.optimization_barrier((coeff[0], raw))
    correlations = call(
        table_kernel,
        shape((n_rows, local_orbs)),
        [SMEM, VMEM],
        scratch=(pltpu.VMEM((n_rows, local_orbs), jnp.float32),),
    )(plan, coeff).reshape(nproj, blk_rows, local_orbs)
    return (solution, correlations, gradient)


def solution(mesh):
    return jax.shard_map(
        per_device,
        mesh=mesh,
        in_specs=(
            P("orb", "dom", None, None),
            P("dom", None, None),
            P(),
            P("orb"),
            P("orb", None, "dom", None, None),
            P(),
            P("orb", "dom", None, None),
            P(),
        ),
        out_specs=(P("orb", "dom", None, None), P(None, None, "orb"), P(None, "dom", "orb")),
        check_vma=False,
    )
```

```python
import functools
import math

import jax
import jax.numpy as jnp
from jax import lax
from jax.experimental import pallas as pl
from jax.experimental.pallas import tpu as pltpu
from jax.sharding import PartitionSpec as P

ITERS = 3
VMEM_LIMIT = 16 * 1024 * 1024
NT = (((1,), (1,)), ((), ()))
SMEM = pl.BlockSpec(memory_space=pltpu.SMEM)
ANY = pl.BlockSpec(memory_space=pl.ANY)
VMEM = pl.BlockSpec(memory_space=pltpu.VMEM)
HBM = pl.BlockSpec(memory_space=pltpu.HBM)

MID, CHIP, SAME, SLOT, CORE, DEV, TABLE = 0, 2, 4, 5, 6, 7, 8


def shape(dims, dtype=jnp.float32):
    return jax.ShapeDtypeStruct(dims, dtype)


def plan(per_dev, n_orb, ids_ref, dev_ref, out_ref):
    nproj = ids_ref.shape[0]
    chips = n_orb // 2
    ring = chips // 2
    last = per_dev * n_orb - 1
    dev = dev_ref[0]
    chip = dev // 2
    seen = jnp.int32(0)
    mids = [jnp.int32(0)] * (nproj - 2)
    order = []
    for j in range(nproj):
        block = ids_ref[j]
        middle = jnp.logical_and(block != 0, block != last)
        for k in range(nproj - 2):
            mids[k] = jnp.where(jnp.logical_and(middle, seen == k), block, mids[k])
        order.append(jnp.where(block == 0, 0, jnp.where(block == last, 1, 2 + seen)))
        seen = seen + jnp.where(middle, 1, 0)
    owners = [mid // (2 * per_dev) for mid in mids]
    for k in range(nproj - 2):
        out_ref[MID + k] = mids[k]
        out_ref[CHIP + k] = owners[k]
    out_ref[SAME] = jnp.where(owners[0] == owners[1], 1, 0)
    offer = jnp.where(chip == owners[0], mids[0], mids[1])
    out_ref[SLOT] = offer % per_dev
    out_ref[CORE] = (offer // per_dev) % 2
    out_ref[DEV] = dev
    y, x = chip % ring, chip // ring
    for j in range(nproj):
        for q in range(chips):
            down = (q // 2 + ring - y) % ring
            first = jnp.where(down == 1, 4, jnp.where(down == 3, 8, jnp.where(down == 2, 12, 0)))
            first = first + (order[j] + x) % 2 * 2 + q % 2
            down = (q % ring + ring - y) % ring
            side = (q // ring + x) % 2
            second = jnp.where(down == 1, 4, jnp.where(down == 3, 2, 0)) + side * 6
            second = 14 + jnp.where(down == 2, 12 + side * 2, second) + order[j]
            out_ref[TABLE + j * chips + q] = jnp.where(order[j] < 2, first, second)


def copies(source, target, sem):
    parts = sem.shape[0]
    rows = target.shape[0] // parts
    return [
        pltpu.make_async_copy(source(k * rows, rows), target.at[pl.ds(k * rows, rows)], sem.at[k])
        for k in range(parts)
    ]


def run(started):
    for copy in started:
        copy.start()
    for copy in started:
        copy.wait()


def offer_kernel(per_dev, n_orb, ids_ref, dev_ref, occupied_ref, plan_ref, same_ref, offer_ref, sem):
    plan(per_dev, n_orb, ids_ref, dev_ref, plan_ref)
    same_ref[0] = plan_ref[SAME]
    core = plan_ref[DEV] % 2
    run(copies(lambda at, n: occupied_ref.at[plan_ref[SLOT], pl.ds(at, n), 1 - core], offer_ref, sem))


def fixed_kernel(n_orb, plan_ref, occupied_ref, fixed_ref, sem):
    dev = plan_ref[DEV]
    core = dev % 2
    slot = core * (occupied_ref.shape[0] - 1)

    @pl.when(jnp.logical_or(dev == 0, dev == n_orb - 1))
    def _():
        run(copies(lambda at, n: occupied_ref.at[slot, pl.ds(at, n), 1 - core], fixed_ref, sem))


def pick_kernel(plan_ref, occupied_ref, offer_ref, out_ref, sem):
    core = plan_ref[DEV] % 2

    @pl.when(plan_ref[CORE] == core)
    def _():
        run(copies(lambda at, n: occupied_ref.at[plan_ref[SLOT], pl.ds(at, n), core], out_ref, sem))

    @pl.when(plan_ref[CORE] != core)
    def _():
        step = 16

        @pl.loop(0, out_ref.shape[0] // step)
        def _(k):
            here = pl.ds(k * step, step)
            out_ref[here] = offer_ref[here]


def pieces_kernel(n_orb, plan_ref, occupied_ref, fixed_ref, *refs):
    *piece_refs, sem = refs
    dev = plan_ref[DEV]
    core = dev % 2
    last = occupied_ref.shape[0] - 1
    ring = len(piece_refs)
    rows = piece_refs[0].shape[0]

    def at(s):
        return pl.ds(jnp.where(dev < n_orb // 2, s, (ring - 1 + s) % ring) * rows, rows)

    @pl.when(jnp.logical_or(dev == 0, dev == n_orb - 1))
    def _():
        run([
            pltpu.make_async_copy(occupied_ref.at[core * last, at(s), core], ref, sem.at[s])
            for s, ref in enumerate(piece_refs)
        ])

    @pl.when(jnp.logical_or(dev == 1, dev == n_orb - 2))
    def _():
        for s, ref in enumerate(piece_refs):
            ref[...] = fixed_ref[at(s)]


def share_kernel(plan_ref, *refs):
    *piece_refs, out_ref = refs
    ring = len(piece_refs)
    chip = plan_ref[DEV] // 2
    y, x = chip % ring, chip // ring
    away = (y + x) % ring
    for s, ref in enumerate(piece_refs):

        @pl.when(away == s)
        def _(ref=ref):
            out_ref[...] = ref[...]


def core_mask(low_ref, width):
    return jnp.concatenate([low_ref[...]] * (width // low_ref.shape[1]), axis=1) > 0.5


def split(low_ref, value, mine_ref, other_ref):
    half = value.shape[0] // 2
    low = core_mask(low_ref, value.shape[1])
    first, second = value[:half], value[half:]
    mine_ref[...] = jnp.where(low, first, second)
    other_ref[...] = jnp.where(low, second, first)


def project(scale, low_ref, resid_b, block_refs, mine_ref, other_ref):
    parts = [
        lax.dot_general(resid_b, ref[...], NT, preferred_element_type=jnp.float32) for ref in block_refs
    ]
    split(low_ref, jnp.concatenate(parts, axis=1) * scale, mine_ref, other_ref)


def fields_kernel(low_ref, field_ref, mine_ref, other_ref):
    rows_y, rows_z = field_ref.shape[2:]
    low = low_ref[...] > 0.5
    for y in range(rows_y):
        first, second = field_ref[:, 0, y, :], field_ref[:, 1, y, :]
        here = slice(y * rows_z, (y + 1) * rows_z)
        mine_ref[:, here] = jnp.where(low, first, second)
        other_ref[:, here] = jnp.where(low, second, first)


def pair_kernel(low_ref, mine_ref, other_ref, out_ref, *rounded_refs):
    half = mine_ref.shape[0]
    low = core_mask(low_ref, mine_ref.shape[1])
    mine, other = mine_ref[...], other_ref[...]
    both = jnp.concatenate([jnp.where(low, mine, other), jnp.where(low, other, mine)], axis=0)
    out_ref[...] = both
    for ref in rounded_refs:
        ref[...] = both.astype(jnp.bfloat16)


def take_kernel(plan_ref, offered_ref, second_ref, out_ref):
    rows = offered_ref.shape[1]
    out_ref[:rows] = offered_ref[plan_ref[CHIP]]

    @pl.when(plan_ref[SAME] == 1)
    def _():
        out_ref[rows:] = second_ref[...]

    @pl.when(plan_ref[SAME] != 1)
    def _():
        out_ref[rows:] = offered_ref[plan_ref[CHIP + 1]]


def shares_kernel(scale, places, plan_ref, *refs):
    *field_refs, ends_ref, mids_ref, out_ref = refs
    devices, orbs, lanes = out_ref.shape
    ring = devices // 4
    chip = plan_ref[DEV] // 2
    y, x = chip % ring, chip // ring
    spare = lanes - ends_ref.shape[0] - mids_ref.shape[0]
    for place, field_ref in zip(places, field_refs):
        field = field_ref[...]
        got = [
            lax.dot_general(field, ref[...], NT, preferred_element_type=jnp.float32)
            for ref in (ends_ref, mids_ref)
        ]
        rows = jnp.concatenate(got + [jnp.zeros((field.shape[0], spare), jnp.float32)], axis=1) * scale
        for k, (down, side) in enumerate(place):
            to = 2 * ((x + side) % 2 * ring + (y + down) % ring)
            at = k * 2 * orbs
            out_ref[pl.ds(to, 1)] = rows[at : at + orbs][None]
            out_ref[pl.ds(to + 1, 1)] = rows[at + orbs : at + 2 * orbs][None]


def spread_shares_kernel(parts_ref, out_ref):
    rows = out_ref.shape[2] * 2 // parts_ref.shape[0]
    total = jnp.concatenate(
        [(parts_ref[k] + parts_ref[k + 1])[:, :rows] for k in range(0, parts_ref.shape[0], 2)], axis=1
    )
    for d in range(out_ref.shape[0]):
        out_ref[d] = total


def resid_kernel(
    scale, row, low_ref, x_ref, sib_ref, off_ref, rhs_ref, diag_ref, first_ref, second_ref,
    resid_ref, mine_ref, other_ref, rb_ref,
):
    cells = x_ref.shape[1]
    lane = lax.broadcasted_iota(jnp.int32, (x_ref.shape[0], row), 1)
    for at in range(0, cells, row):
        here = slice(at, at + row)
        x = x_ref[:, here]
        beside = sib_ref[:, here] + off_ref[:, here].astype(jnp.float32)
        if at > 0:
            beside = beside + x_ref[:, at - row : at]
        if at + row < cells:
            beside = beside + x_ref[:, at + row : at + 2 * row]
        beside = beside + jnp.where(lane == 0, 0.0, pltpu.roll(x, 1, 1))
        beside = beside + jnp.where(lane == row - 1, 0.0, pltpu.roll(x, row - 1, 1))
        resid = rhs_ref[:, here] - (diag_ref[:, here] * x - 0.5 * beside)
        resid_ref[:, here] = resid
        rb_ref[:, here] = resid.astype(jnp.bfloat16)
    project(scale, low_ref, rb_ref[...], (first_ref, second_ref), mine_ref, other_ref)


def stacked(value):
    half = value.shape[1] // 2
    return jnp.concatenate([value[:, :half], value[:, half:]], axis=0)


def unstacked(value):
    half = value.shape[0] // 2
    return jnp.concatenate([value[:half], value[half:]], axis=1)


def spread_kernel(mine_ref, other_ref, out_ref):
    total = mine_ref[...] + other_ref[...]
    for d in range(out_ref.shape[0]):
        out_ref[d] = total


def total_kernel(parts_ref, *out_refs):
    total = parts_ref[0]
    for d in range(1, parts_ref.shape[0]):
        total = total + parts_ref[d]
    out_refs[0][...] = stacked(total).astype(jnp.bfloat16)
    if len(out_refs) > 1:
        out_refs[1][...] = total


def pack_kernel(splits, *refs):
    pieces, outs = refs[: sum(splits)], refs[sum(splits) :]
    for count, out_ref in zip(splits, outs):
        at = 0
        for ref in pieces[:count]:
            rows = ref.shape[0]
            out_ref[at : at + rows] = ref[...]
            at += rows
        pieces = pieces[count:]


def packed(splits, *refs):
    *refs, sem = refs
    pieces, outs = refs[: sum(splits)], refs[sum(splits) :]
    moves = []
    for count, out_ref in zip(splits, outs):
        at = 0
        for ref in pieces[:count]:
            rows = ref.shape[0]
            moves.append(pltpu.make_async_copy(ref, out_ref.at[pl.ds(at, rows)], sem.at[len(moves)]))
            at += rows
        pieces = pieces[count:]
    return moves


def update_kernel(scale, tile, has_x, last, root, splits, low_ref, mine_ref, other_ref, resid_ref, diag_ref, *refs):
    refs = list(refs)
    x_ref = refs.pop(0) if has_x else None
    move_ref = None if has_x else refs.pop(0)
    psi_ref = refs.pop(0) if last else None
    if has_x:
        first_ref, second_ref, *outs = refs
    else:
        *refs, x_out, x_b_out, first_ref, second_ref, sem = refs
        outs = [x_out, x_b_out]
    low = core_mask(low_ref, 2 * mine_ref.shape[1])
    mine = unstacked(mine_ref[...].astype(jnp.float32))
    other = unstacked(other_ref[...].astype(jnp.float32))
    coeff = jnp.concatenate([jnp.where(low, mine, other), jnp.where(low, other, mine)], axis=0)
    coeff = coeff.astype(jnp.bfloat16)
    if not has_x:
        coeff = jnp.dot(coeff, move_ref[...], preferred_element_type=jnp.float32).astype(jnp.bfloat16)
        run(packed(splits, *refs, first_ref, second_ref, sem))
    cells = resid_ref.shape[1]
    for at in range(0, cells, tile):
        here = slice(at, at + tile)
        corr = 0.0
        start = 0
        for ref in (first_ref, second_ref):
            rows = ref.shape[0]
            some = coeff[:, start : start + rows]
            corr = corr + jnp.dot(some, ref[:, here], preferred_element_type=jnp.float32)
            start += rows
        x = (resid_ref[:, here] - corr * scale) / diag_ref[:, here]
        if has_x:
            x = x + x_ref[:, here]
        if last:
            half = x.shape[0] // 2
            low = core_mask(low_ref, tile)
            outs[0][:, here] = jnp.where(low, x[:half], x[half:])
            outs[1][:, here] = jnp.where(low, x[half:], x[:half])
            raw = jnp.sum(x * psi_ref[:, here].astype(jnp.float32), axis=0, keepdims=True) / root
            rows, wide = outs[2].shape[2:]
            for k in range(tile // wide):
                row = raw[:, k * wide : (k + 1) * wide]
                spot = at // wide + k
                outs[2][spot // rows, :, spot % rows, :] = jnp.broadcast_to(row, (outs[2].shape[1], wide))
        else:
            outs[0][:, here] = x
            outs[1][:, here] = x.astype(jnp.bfloat16)


def table_kernel(plan_ref, coeff_ref, out_ref, rows_ref):
    rows_ref[...] = coeff_ref[...].T
    share = 16
    for j in range(out_ref.shape[0] // share):
        at = pl.multiple_of(plan_ref[TABLE + j] * share, share)
        out_ref[j * share : (j + 1) * share] = rows_ref[pl.ds(at, share)]


def finish_kernel(smoother_ref, pick_ref, terms_ref, out_ref):
    def product(one, two, dims):
        return lax.dot_general(
            one, two, (dims, ((), ())),
            precision=lax.Precision.HIGHEST, preferred_element_type=jnp.float32,
        )

    sources, planes = terms_ref.shape[0], smoother_ref.shape[1]
    chips = sources // planes
    row = lax.broadcasted_iota(jnp.int32, (sources, planes), 0)
    plane = lax.broadcasted_iota(jnp.int32, (sources, planes), 1)
    same = jnp.logical_and(row // (2 * chips) == plane // 2, row % 2 == plane % 2)
    gather = jnp.where(same, 1.0, 0.0)
    for k in range(terms_ref.shape[1]):
        mine = product(pick_ref[...], terms_ref[:, k, :], ((1,), (1,)))
        raw = product(mine, gather, ((1,), (0,)))
        out_ref[k] = product(raw, smoother_ref[...], ((1,), (1,)))


def call(kernel, out_shape, in_specs=None, out_specs=None, scratch=()):
    specs = {}
    if in_specs is not None:
        specs["in_specs"] = in_specs
    if out_specs is not None:
        specs["out_specs"] = out_specs
    return pl.pallas_call(
        kernel,
        out_shape=out_shape,
        scratch_shapes=scratch,
        compiler_params=pltpu.CompilerParams(vmem_limit_bytes=VMEM_LIMIT),
        **specs,
    )


def per_device(rhs, potential, eigen_table, win_index, occupied, block_ids, psi_win, smoother):
    local_orbs, planes, rows_y, rows_z = rhs.shape
    n_dom = lax.axis_size("dom")
    n_orb = lax.axis_size("orb")
    cells = rows_y * rows_z
    wide = 2 * local_orbs
    width = local_orbs * n_orb
    scale = 1.0 / math.sqrt(planes * n_dom * rows_y * rows_z)
    n_occ = eigen_table.shape[0]
    per_dev, blk_rows = occupied.shape[:2]
    nproj = block_ids.shape[0]
    chips = n_orb // 2
    ring = chips // 2
    share = blk_rows // chips
    n_rows = nproj * blk_rows
    o = lax.axis_index("orb")
    core = o % 2
    low = core == 0
    groups = [[2 * k + c for k in range(chips)] for c in range(2)]

    def chip_perm(target):
        return [(2 * k + c, 2 * target(k) + c) for k in range(chips) for c in range(2)]

    swap_core = [(i, i ^ 1) for i in range(n_orb)]
    swap_x = chip_perm(lambda k: (k + ring) % chips)
    up_y = chip_perm(lambda k: k // ring * ring + (k + 1) % ring)
    down_y = chip_perm(lambda k: k // ring * ring + (k - 1) % ring)

    over_y = chip_perm(lambda k: k // ring * ring + (k + 2) % ring)

    def permute(value, pairs):
        return lax.ppermute(value, "orb", pairs)

    def pair(own, other):
        return jnp.concatenate([jnp.where(low, own, other), jnp.where(low, other, own)], axis=0)

    low_mask = jnp.broadcast_to(jnp.where(low, 1.0, 0.0), (local_orbs, 128))
    four = (pltpu.SemaphoreType.DMA((4,)),)

    plane_shape = shape((blk_rows, rows_y, rows_z), jnp.bfloat16)
    piece_shape = shape((2 * share, rows_y, rows_z), jnp.bfloat16)
    plan, same, offer = call(
        functools.partial(offer_kernel, per_dev, n_orb),
        (shape((TABLE + nproj * chips,), jnp.int32), shape((1,), jnp.int32), plane_shape),
        [SMEM, SMEM, ANY],
        (SMEM, SMEM, VMEM),
        four,
    )(block_ids, o.astype(jnp.int32).reshape(1), occupied)
    offer = permute(offer, swap_core)

    flat_field = shape((local_orbs, cells))
    field_shape = shape((wide, cells))
    rhs_mine, rhs_other = call(fields_kernel, (flat_field, flat_field))(low_mask, rhs)
    rhs_wide, rhs_b = call(pair_kernel, (field_shape, shape((wide, cells), jnp.bfloat16)))(
        low_mask, rhs_mine, permute(rhs_other, swap_core)
    )
    rhs_up, rhs_down, rhs_far = permute(rhs_b, up_y), permute(rhs_b, down_y), permute(rhs_b, over_y)

    offer = call(pick_kernel, plane_shape, [SMEM, ANY, VMEM], VMEM, four)(plan, occupied, offer)
    fixed = call(functools.partial(fixed_kernel, n_orb), plane_shape, [SMEM, ANY], VMEM, four)(plan, occupied)
    fixed = permute(fixed, [(0, 1), (n_orb - 1, n_orb - 2)])
    offer, fixed = lax.optimization_barrier((offer, fixed))
    pieces = call(
        functools.partial(pieces_kernel, n_orb),
        [piece_shape] * ring,
        [SMEM, ANY, VMEM],
        [VMEM] * ring,
        (pltpu.SemaphoreType.DMA((ring,)),),
    )(plan, occupied, fixed)

    got = [pieces[0]]
    for s in range(1, ring):
        pairs = [(c, 2 * s + c) for c in range(2)]
        pairs += [(n_orb - 2 + c, 2 * (ring + (ring - 1 + s) % ring) + c) for c in range(2)]
        got.append(permute(pieces[s], pairs))
    rhs_up, rhs_down, rhs_far, got[2] = lax.optimization_barrier((rhs_up, rhs_down, rhs_far, got[2]))
    rhs_line = jnp.concatenate([rhs_b, rhs_up, rhs_down, rhs_far], axis=0)
    rhs_line_x = permute(rhs_line, swap_x)
    fixed = call(share_kernel, piece_shape, [SMEM] + [VMEM] * ring, VMEM)(plan, *got)

    def scatter(value):
        value = value.reshape(chips, share, rows_y, rows_z)
        return lax.all_to_all(value, "orb", 0, 0, axis_index_groups=groups, tiled=True)

    def take(value, owner):
        return lax.dynamic_index_in_dim(value, owner, 0, keepdims=False)

    def apart(plan, occupied):
        return jnp.zeros((share, rows_y, rows_z), jnp.bfloat16)

    def together(plan, occupied):
        def plane_of(slot, plane):
            dims = (1, blk_rows, 1, rows_y, rows_z)
            return lax.dynamic_slice(occupied, (slot, 0, plane, 0, 0), dims).reshape(plane_shape.shape)

        mid = plan[MID + 1]
        other = permute(plane_of(mid % per_dev, 1 - core), swap_core)
        here = (mid // per_dev) % 2 == core
        again = scatter(jnp.where(here, plane_of(mid % per_dev, core), other))
        return take(again, plan[CHIP + 1])

    offered = scatter(offer)
    second = lax.cond(same[0] == 1, together, apart, plan, occupied)
    mids = call(
        take_kernel, shape((2 * share, rows_y, rows_z), jnp.bfloat16), [SMEM, VMEM, VMEM], VMEM
    )(plan, offered, second)

    xs = fixed.reshape(2 * share, cells)
    ys = mids.reshape(2 * share, cells)
    xs, ys = lax.optimization_barrier((xs, ys))
    xs_x = permute(xs, swap_x)
    ys_up = permute(ys, up_y)
    ys_down = permute(ys, down_y)
    own_rows = 4 * share
    half_shape = shape((local_orbs, n_rows))
    spread_shape = shape((n_dom, local_orbs, n_rows))
    rhs_places = [[(0, k), (ring - 1, k), (1, k), (2, k)] for k in range(2)]
    parts = call(
        functools.partial(shares_kernel, scale, rhs_places),
        shape((n_orb, local_orbs, 128)),
        [SMEM] + [VMEM] * 4,
    )(plan, rhs_line, rhs_line_x, xs, ys)
    parts = lax.all_to_all(parts, "orb", 0, 0, tiled=True)
    xs_x, ys_up, ys_down = lax.optimization_barrier((xs_x, ys_up, ys_down))
    own, line = call(
        functools.partial(pack_kernel, (2, 3)),
        (shape((4 * share, cells), jnp.bfloat16), shape((6 * share, cells), jnp.bfloat16)),
    )(xs, xs_x, ys, ys_up, ys_down)
    line_x = permute(line, swap_x)
    above = permute(own, up_y)
    below = permute(own, down_y)
    far_up = permute(ys_up[:share], up_y)
    far_down = permute(ys_down[share:], down_y)
    parts, _ = lax.optimization_barrier((parts, line))
    first_parts = lax.all_to_all(
        call(spread_shares_kernel, spread_shape)(parts), "dom", 0, 0, tiled=True
    )
    line_x, above, below, far_up, far_down = lax.optimization_barrier(
        (line_x, above, below, far_up, far_down)
    )
    far_up_x, far_down_x = permute(far_up, swap_x), permute(far_down, swap_x)
    own_up = permute(above[: 2 * share], up_y)
    own_down = permute(below[2 * share :], down_y)
    pieces = [own, below, above, own_up, own_down]
    pieces += [line, line_x, far_up, far_down, far_up_x, far_down_x]
    blocks_shape = [shape((n_rows // 2, cells), jnp.bfloat16)] * 2

    picks = win_index[:, None] == jnp.arange(n_occ, dtype=jnp.int32)[None, :]
    eps = jnp.sum(jnp.where(picks, eigen_table[None, :], 0.0), axis=1)[:, None]
    eps = pair(eps, permute(eps, swap_core))
    plane_pot = lax.dynamic_index_in_dim(potential, core, 0, keepdims=True).reshape(1, cells)
    diag = 3.0 + plane_pot - eps
    psi_mine, psi_other = call(fields_kernel, (flat_field, flat_field))(
        low_mask, psi_win.astype(jnp.float32)
    )
    psi_wide = call(pair_kernel, field_shape)(
        low_mask, psi_mine, permute(psi_other.astype(jnp.bfloat16), swap_core).astype(jnp.float32)
    )
    flat_shape = (wide, n_rows // 2)

    def total(parts, outs):
        coeff_b, *coeff = call(total_kernel, outs)(parts)
        return coeff, coeff_b, permute(coeff_b, swap_core)

    row = jnp.arange(n_rows)
    within = row % (2 * share)
    down = jnp.array([0, 0, 1, 1, 3, 3, 2, 2, 0, 3, 1, 0, 3, 1, 2, 2])
    side = jnp.array([0, 1, 0, 1, 0, 1, 0, 1, 0, 0, 0, 1, 1, 1, 0, 1])
    chip = o // 2
    chip_from = (chip // ring + side) % 2 * ring + (chip % ring + down) % ring
    at = chip_from * own_rows + jnp.where(jnp.arange(16) < 8, 0, 2 * share)
    at = jnp.repeat(at, 2 * share) + within
    move = (row[:, None] == at[None, :]).astype(jnp.bfloat16)

    across = []
    for d in range(n_dom - 1):
        for k in range(chips):
            left, right = d * n_orb + 2 * k + 1, (d + 1) * n_orb + 2 * k
            across += [(left, right), (right, left)]

    x = None
    for step in range(ITERS):
        final = step == ITERS - 1
        sums = [shape(flat_shape, jnp.bfloat16)] + ([half_shape] if final else [])
        if step == 0:
            resid, parts = rhs_wide, first_parts
        else:
            sib = permute(x, swap_core)
            off = lax.ppermute(x_b, ("dom", "orb"), across)
            resid, mine, other = call(
                functools.partial(resid_kernel, scale, rows_z),
                (field_shape, half_shape, half_shape),
                scratch=(pltpu.VMEM((wide, cells), jnp.bfloat16),),
            )(low_mask, x, sib, off, rhs_wide, diag, *blocks)
            spread = call(spread_kernel, spread_shape)(mine, permute(other, swap_core))
            parts = lax.all_to_all(spread, "dom", 0, 0, tiled=True)
        coeff, coeff_b, coeff_o = total(parts, sums)
        extra = ([x] if step else [move]) + ([psi_wide] if final else [])
        outs = [field_shape, shape((wide, cells), jnp.bfloat16)]
        if final:
            outs = [shape((local_orbs, cells))] * 2 + [shape((n_dom, n_orb, rows_y // n_dom, rows_z))]
        if step == 0:
            outs, blocks = outs + blocks_shape, pieces
            specs = [VMEM] * 6 + [HBM] * len(pieces), [VMEM] * 4
            sems = (pltpu.SemaphoreType.DMA((len(pieces),)),)
        else:
            specs, sems = (None, None), ()
        x, x_b, *rest = call(
            functools.partial(update_kernel, scale, 512, step > 0, final, math.sqrt(width), (5, 6)),
            outs,
            *specs,
            sems,
        )(low_mask, coeff_b, coeff_o, resid, diag, *extra, *blocks)
        if step == 0:
            blocks = rest
    other, raw = x_b, rest[0]

    terms = lax.all_to_all(
        raw.reshape((n_dom * n_orb,) + raw.shape[2:]), ("dom", "orb"), 0, 0, tiled=True
    )
    z_part = rows_z // n_orb
    z_mine = o * z_part + jnp.arange(z_part)[:, None]
    pick = (jnp.arange(rows_z)[None, :] == z_mine).astype(jnp.float32)
    gradient = call(finish_kernel, shape((rows_y // n_dom, z_part, 2 * n_dom)))(smoother, pick, terms)
    gradient = jnp.transpose(gradient, (2, 0, 1))

    other = permute(other, swap_core)
    solution = jnp.stack([jnp.where(low, x, other), jnp.where(low, other, x)], axis=1)
    solution = solution.reshape(rhs.shape)

    coeff, raw = lax.optimization_barrier((coeff[0], raw))
    correlations = call(
        table_kernel,
        shape((n_rows, local_orbs)),
        [SMEM, VMEM],
        scratch=(pltpu.VMEM((n_rows, local_orbs), jnp.float32),),
    )(plan, coeff).reshape(nproj, blk_rows, local_orbs)
    return (solution, correlations, gradient)


def solution(mesh):
    return jax.shard_map(
        per_device,
        mesh=mesh,
        in_specs=(
            P("orb", "dom", None, None),
            P("dom", None, None),
            P(),
            P("orb"),
            P("orb", None, "dom", None, None),
            P(),
            P("orb", "dom", None, None),
            P(),
        ),
        out_specs=(P("orb", "dom", None, None), P(None, None, "orb"), P(None, "dom", "orb")),
        check_vma=False,
    )
```
